32 devices in a mesh: parts: 2 (over x), blk: 16 (over z, y, core).
Axes of the slice: x: 2, y: 2, z: 4, core: 2. Of those that a mesh axis runs over, the one named last changes fastest.
Arguments:
- features: bfloat16 [8192, 256], P(('parts', 'blk')), parts along dimension 0, may hold values from -5 to 5
- probes: bfloat16 [8192, 32], P(('parts', 'blk')), parts along dimension 0, may hold values from -6 to 6
- noise_level: float32 [8192], P(('parts', 'blk')), parts along dimension 0, may hold values from 0.05 to 1
Outputs:
- kernel_product: float32 [8192, 32], P(('parts', 'blk')), parts along dimension 0
The draws below stay inside these ranges and needn't reach their ends.
There are 2 independent parts, one for each index of `parts`. The reference program is written for one: setup_inputs(seed, part) draws one part's arguments, and reference() takes and returns one part's arrays. A program takes and returns all parts, laid end to end along the dimension named above; each array names one. Nothing has to cross between parts.
All inputs are finite; a program needn't handle non-finite values.
Results may differ from the reference program's by a relative error of at most 0.0024.
Values may be sent and summed in bfloat16 or wider, within the bound.
No kernel may reach another device: no remote copies, remote signals or barrier semaphores. Data moves between devices by JAX's collectives and lax.ppermute only.
A program may use at most 64 MiB of HBM per device.

```python
import math
import jax
import jax.numpy as jnp
from jax import lax

D = 256
P_SIZE = 32
ROWS_DEV = 256
POINTS = 4096


def draw_features(key, part):
    seed_key = jax.random.fold_in(key, 11)
    key_column, key_row, key_base = jax.random.split(seed_key, 3)
    column_scale = jnp.exp(jax.random.uniform(key_column, (D,), jnp.float32, -1.2, -0.6))
    row_scale = jnp.exp(jax.random.uniform(key_row, (POINTS, 1), jnp.float32, math.log(0.6), math.log(1.3)))
    base_values = jax.random.truncated_normal(key_base, -4.0, 4.0, (POINTS, D), jnp.float32)
    factor = 6.26 / math.sqrt(D)
    return (factor * row_scale * column_scale[None, :] * base_values).astype(jnp.bfloat16)


def levels(key, dims, shards, least, top_value):
    def one(dim, shards_of):
        draws = jax.random.uniform(jax.random.fold_in(jax.random.fold_in(key, 6), dim), (shards_of,), jnp.float32, least / len(shards), top_value / len(shards))
        return jnp.repeat(jnp.exp(draws), dims[dim] // shards_of).reshape((-1,) + (1,) * (len(dims) - dim - 1))

    level = one(*shards[0])
    for cut in shards[1:]:
        level = level * one(*cut)
    return level


def bell_draw(key, dims, width, most, cuts=(), kind=jnp.bfloat16):
    array = width * jax.random.normal(key, dims, jnp.float32)
    if cuts:
        array = array * levels(key, dims, cuts, -0.22, 0.18)
    return jnp.clip(array, -most, most).astype(kind)


def setup_inputs(seed: int = 0, part: int = 0) -> dict:
    keys = jax.random.split(jax.random.key(seed), 4)
    part_keys = jax.random.split(jax.random.fold_in(keys[3], part), 4)
    features = draw_features(jax.random.fold_in(jax.random.fold_in(keys[3], part), 71), part)
    probes = bell_draw(part_keys[1], (POINTS, P_SIZE), 1.0, 6.0, ((0, 16),))
    noise_level = jnp.clip(jnp.exp(math.log(1.0) - 2.9957323 * jax.random.uniform(part_keys[2], (POINTS,), jnp.float32) ** levels(part_keys[2], (POINTS,), ((0, 16),), -0.2, 0.2)), 0.05, 1.0)
    return dict(features=features, probes=probes, noise_level=noise_level)


def kernel_tile(left_x, left_sq, right_x, right_sq, right_v):
    cross = lax.dot_general(left_x, right_x, (((1,), (1,)), ((), ())), preferred_element_type=jnp.float32)
    dist2 = jnp.maximum(left_sq[:, None] + right_sq[None, :] - 2.0 * cross, 0.0)
    scaled = jnp.sqrt(5.0 * dist2)
    kernel = ((1.0 + scaled + scaled * scaled / 3.0) * jnp.exp(-scaled)).astype(jnp.bfloat16)
    return jnp.dot(kernel, right_v, preferred_element_type=jnp.float32)

def reference(features, probes, noise_level):
    wide = features.astype(jnp.float32)
    squares = lax.optimization_barrier(jnp.sum(wide * wide, axis=1))
    blocks = POINTS // ROWS_DEV
    row_blocks = features.reshape(blocks, ROWS_DEV, D)
    square_blocks = squares.reshape(blocks, ROWS_DEV)

    def one_block(members):
        return kernel_tile(members[0], members[1], features, squares, probes)
    product = lax.map(one_block, (row_blocks, square_blocks)).reshape(POINTS, P_SIZE)
    return product + noise_level[:, None] * probes.astype(jnp.float32)
```

```python
import functools
import math

import jax
import jax.numpy as jnp
from jax import lax
from jax.experimental import pallas as pl
from jax.experimental.pallas import tpu as pltpu
from jax.sharding import PartitionSpec as P

ROOT5 = math.sqrt(5.0)
DECAY = -ROOT5 * math.log2(math.e)


def partner(index, step, count):
    if count & (count - 1) == 0:
        return index ^ step
    return (index + step) % count


def group_size(count):
    size = 1
    while size * size < count or count % size:
        size += 1
    return size


def matern(dist2):
    dist2 = jnp.maximum(dist2, 1e-30)
    dist = dist2 * lax.rsqrt(dist2)
    poly = (1.0 + ROOT5 * dist) + (5.0 / 3.0) * dist2
    return (poly * jnp.exp2(DECAY * dist)).astype(jnp.bfloat16)


def squares_on_lanes(block):
    wide = block.astype(jnp.float32)
    square = wide * wide
    high = square.astype(jnp.bfloat16)
    low = (square - high.astype(jnp.float32)).astype(jnp.bfloat16)
    ones = jnp.ones((8, block.shape[1]), jnp.bfloat16)
    dims = (((1,), (1,)), ((), ()))
    return lax.dot_general(ones, high, dims, preferred_element_type=jnp.float32) + lax.dot_general(
        ones, low, dims, preferred_element_type=jnp.float32
    )


def tile_kernel(row_count, col_count, *refs):
    row_refs = refs[:row_count]
    col_refs = refs[row_count : row_count + col_count]
    probe_refs = refs[row_count + col_count : row_count + 2 * col_count]
    out_ref, rows, row_squares = refs[row_count + 2 * col_count :]
    shard, width = row_refs[0].shape
    for slot, ref in enumerate(row_refs):
        block = ref[...]
        rows[pl.ds(slot * shard, shard), :] = block * jnp.asarray(-2.0, block.dtype)
        row_squares[:, pl.ds(slot * shard, shard)] = squares_on_lanes(block)
    out_ref[...] = jnp.zeros_like(out_ref)
    for col_ref, probe_ref in zip(col_refs, probe_refs):
        cols = col_ref[...]
        wide = cols.astype(jnp.float32)
        col_squares = jnp.sum(wide * wide, axis=1, keepdims=True)

        @pl.loop(0, row_count)
        def _(slot):
            start = pl.multiple_of(slot * shard, shard)
            cross = lax.dot_general(
                cols, rows[pl.ds(start, shard), :], (((1,), (1,)), ((), ())), preferred_element_type=jnp.float32
            )
            kernel = matern((col_squares + row_squares[0:1, pl.ds(start, shard)]) + cross)
            out_ref[slot] += jnp.dot(probe_ref[...], kernel, preferred_element_type=jnp.float32)


def tile_product(rows, cols, probes):
    shard, width = rows[0].shape
    vectors = probes[0].shape[0]
    body = functools.partial(tile_kernel, len(rows), len(cols))
    elements = len(rows) * len(cols) * shard * shard
    return pl.pallas_call(
        body,
        out_shape=jax.ShapeDtypeStruct((len(rows), vectors, shard), jnp.float32),
        in_specs=[pl.BlockSpec(memory_space=pltpu.VMEM)] * (len(rows) + 2 * len(cols)),
        out_specs=pl.BlockSpec(memory_space=pltpu.VMEM),
        scratch_shapes=[
            pltpu.VMEM((len(rows) * shard, width), jnp.bfloat16),
            pltpu.VMEM((8, len(rows) * shard), jnp.float32),
        ],
        compiler_params=pltpu.CompilerParams(vmem_limit_bytes=32 * 1024 * 1024),
        cost_estimate=pl.CostEstimate(
            flops=2 * elements * (width + vectors),
            bytes_accessed=2 * width * shard * (len(rows) + len(cols)),
            transcendentals=2 * elements,
        ),
    )(*rows, *cols, *probes)


def on_device(features, probes, noise_level):
    count = lax.axis_size("blk")
    inner = group_size(count)
    outer = count // inner
    flat = probes.T

    def from_outer(value, step):
        pairs = [
            (partner(a, step, outer) * inner + b, a * inner + b) for a in range(outer) for b in range(inner)
        ]
        return lax.ppermute(value, "blk", pairs)

    def from_inner(value, step):
        pairs = [
            (a * inner + partner(b, step, inner), a * inner + b) for a in range(outer) for b in range(inner)
        ]
        return lax.ppermute(value, "blk", pairs)

    def to_inner(value, step):
        pairs = [
            (a * inner + b, a * inner + partner(b, step, inner)) for a in range(outer) for b in range(inner)
        ]
        return lax.ppermute(value, "blk", pairs)

    cols = [features] + [from_outer(features, step) for step in range(1, outer)]
    col_probes = [flat] + [from_outer(flat, step) for step in range(1, outer)]
    rows = [features] + [from_inner(features, step) for step in range(1, inner)]
    partial = tile_product(rows, cols, col_probes)
    total = partial[0] + noise_level[None, :] * flat.astype(jnp.float32)
    for step in range(1, inner):
        total = total + to_inner(partial[step], step)
    return total.T


def solution(mesh):
    placed = (P(("parts", "blk"), None), P(("parts", "blk"), None), P(("parts", "blk")))
    return jax.shard_map(
        on_device, mesh=mesh, in_specs=placed, out_specs=P(("parts", "blk"), None), check_vma=False
    )
```

```python
import functools
import math

import jax
import jax.numpy as jnp
from jax import lax
from jax.experimental import pallas as pl
from jax.experimental.pallas import tpu as pltpu
from jax.sharding import PartitionSpec as P

ROOT5 = math.sqrt(5.0)
DECAY = -ROOT5 * math.log2(math.e)
ROWS_BY_ROWS = (((1,), (1,)), ((), ()))


def group_size(count):
    size = 1
    while size * size < count or count % size:
        size += 1
    return size


def inner_partner(index, step, count):
    if count & (count - 1) == 0:
        return index ^ step
    return (index + step) % count


def outer_edges(count):
    maps = [[(a, (a + step) % count) for a in range(count)] for step in range(1, (count + 1) // 2)]
    if count % 2 == 0:
        half = count // 2
        maps.append([(a, a + half) if a % 2 == 0 else (a + half, a) for a in range(half)])
    return maps


def matern(dist2):
    dist2 = jnp.maximum(dist2, 1e-30)
    dist = dist2 * lax.rsqrt(dist2)
    poly = (1.0 + ROOT5 * dist) + (5.0 / 3.0) * dist2
    return (poly * jnp.exp2(DECAY * dist)).astype(jnp.bfloat16)


def lane_squares(block):
    wide = block.astype(jnp.float32)
    square = wide * wide
    high = square.astype(jnp.bfloat16)
    low = (square - high.astype(jnp.float32)).astype(jnp.bfloat16)
    ones = jnp.ones((8, block.shape[1]), jnp.bfloat16)
    total = lax.dot_general(ones, high, ROWS_BY_ROWS, preferred_element_type=jnp.float32)
    total += lax.dot_general(ones, low, ROWS_BY_ROWS, preferred_element_type=jnp.float32)
    return total[0:1, :]


def own_kernel(count, shard, *refs):
    rows, noise_ref = refs[:count], refs[count]
    out_ref, squares_ref = refs[count + 1 :]
    col = rows[0][0:shard, :]
    own_squares = lane_squares(col)
    scaled = col * jnp.asarray(-2.0, col.dtype)
    total = noise_ref[...] * rows[0][shard:, :].astype(jnp.float32)
    for slot, row in enumerate(rows):
        block = row[0:shard, :]
        wide = block.astype(jnp.float32)
        squares = jnp.sum(wide * wide, axis=1, keepdims=True)
        squares_ref[pl.ds(slot * shard, shard), :] = jnp.broadcast_to(squares, (shard, 128))
        cross = lax.dot_general(block, scaled, ROWS_BY_ROWS, preferred_element_type=jnp.float32)
        kernel = matern((squares + own_squares) + cross)
        total += jnp.dot(row[shard:, :], kernel, preferred_element_type=jnp.float32)
    out_ref[...] = total


def pair_kernel(count, shard, follows, *refs):
    rows, col_ref, squares_ref = refs[:count], refs[count], refs[count + 1]
    earlier = refs[count + 2 : count + 2 + count * follows]
    back_ref = refs[count + 2 + count * follows]
    outs = refs[count + 3 + count * follows :]
    col = col_ref[0:shard, :]
    col_squares = lane_squares(col)
    scaled = col * jnp.asarray(-2.0, col.dtype)
    back = jnp.zeros(back_ref.shape, jnp.float32)
    for slot, row in enumerate(rows):
        cross = lax.dot_general(row[0:shard, :], scaled, ROWS_BY_ROWS, preferred_element_type=jnp.float32)
        squares = squares_ref[pl.ds(slot * shard, shard), 0:1]
        kernel = matern((squares + col_squares) + cross)
        back += jnp.dot(row[shard:, :], kernel, preferred_element_type=jnp.float32)
        term = lax.dot_general(col_ref[shard:, :], kernel, ROWS_BY_ROWS, preferred_element_type=jnp.float32)
        outs[slot][...] = earlier[slot][...] + term if follows else term
    back_ref[...] = back


def call(body, outs, args, pairs, shard, width, vectors):
    elements = pairs * shard * shard
    whole = pl.BlockSpec(memory_space=pltpu.VMEM)
    return pl.pallas_call(
        body,
        out_shape=[jax.ShapeDtypeStruct(dims, jnp.float32) for dims in outs],
        in_specs=[whole] * len(args),
        out_specs=[whole] * len(outs),
        compiler_params=pltpu.CompilerParams(vmem_limit_bytes=32 * 1024 * 1024),
        cost_estimate=pl.CostEstimate(
            flops=2 * elements * (width + 2 * vectors),
            bytes_accessed=2 * width * shard * (pairs + 1),
            transcendentals=2 * elements,
        ),
    )(*args)


def on_device(features, probes, noise_level):
    count = lax.axis_size("blk")
    inner = group_size(count)
    outer = count // inner
    shard, width = features.shape
    vectors = probes.shape[1]
    flat = (vectors, shard)
    packed = jnp.concatenate([features, probes.T], axis=0)

    def along_outer(value, edges):
        return lax.ppermute(value, "blk", [(s * inner + b, t * inner + b) for s, t in edges for b in range(inner)])

    def in_plane(value, step, give):
        hops = [(b, inner_partner(b, step, inner)) for b in range(inner)]
        if not give:
            hops = [(t, s) for s, t in hops]
        return lax.ppermute(value, "blk", [(a * inner + s, a * inner + t) for a in range(outer) for s, t in hops])

    maps = outer_edges(outer)
    cols = [along_outer(packed, edges) for edges in maps]
    rows = [packed] + [in_plane(packed, step, False) for step in range(1, inner)]

    total, squares = call(
        functools.partial(own_kernel, inner, shard),
        [flat, (inner * shard, 128)],
        rows + [noise_level[None, :]],
        inner, shard, width, vectors,
    )
    terms, backs = [], []
    for edges, col in zip(maps, cols):
        back, *terms = call(
            functools.partial(pair_kernel, inner, shard, 1 if terms else 0),
            [flat] * (inner + 1),
            rows + [col, squares] + terms,
            inner, shard, width, vectors,
        )
        backs.append(along_outer(back, [(t, s) for s, t in edges]))
    for step, term in enumerate(terms):
        total = total + (in_plane(term, step, True) if step else term)
    for back in backs:
        total = total + back
    return total.T


def solution(mesh):
    placed = (P(("parts", "blk"), None), P(("parts", "blk"), None), P(("parts", "blk")))
    return jax.shard_map(
        on_device, mesh=mesh, in_specs=placed, out_specs=P(("parts", "blk"), None), check_vma=False
    )
```

```python
import functools
import math

import jax
import jax.numpy as jnp
from jax import lax
from jax.experimental import pallas as pl
from jax.experimental.pallas import tpu as pltpu
from jax.sharding import PartitionSpec as P

ROOT5 = math.sqrt(5.0)
DECAY = -ROOT5 * math.log2(math.e)
ROWS_BY_ROWS = (((1,), (1,)), ((), ()))


def group_size(count):
    size = 1
    while size * size < count or count % size:
        size += 1
    return size


def plane_blocks(value, count, send):
    if count & (count - 1):
        maps = {step: [(b, (b - step) % count) for b in range(count)] for step in range(1, count)}
        return [value] + [send(value, maps[step]) for step in range(1, count)]
    blocks = {0: value}
    bit = count // 2
    while bit:
        for known in list(blocks):
            blocks[known | bit] = send(blocks[known], [(b, b ^ bit) for b in range(count)])
        bit //= 2
    return [blocks[distance] for distance in range(count)]


def plane_target(index, step, count):
    return (index + step) % count if count & (count - 1) else index ^ step


def outer_edges(count):
    maps = [([(a, (a + step) % count) for a in range(count)], range(count)) for step in range(1, (count + 1) // 2)]
    if count % 2 == 0:
        half = count // 2
        real = [(a, a + half) if a % 2 == 0 else (a + half, a) for a in range(half)]
        if half % 2 == 0:
            spare = [(a, a - 1) if a % 2 else (a + half, a + half + 1) for a in range(half)]
        else:
            spare = [(t, s) for s, t in real]
        maps.append((real + spare, [t for _, t in real]))
    return maps


def matern(dist2):
    dist2 = jnp.maximum(dist2, 1e-30)
    dist = dist2 * lax.rsqrt(dist2)
    poly = (1.0 + ROOT5 * dist) + (5.0 / 3.0) * dist2
    return (poly * jnp.exp2(DECAY * dist)).astype(jnp.bfloat16)


def lane_squares(block):
    wide = block.astype(jnp.float32)
    square = wide * wide
    high = square.astype(jnp.bfloat16)
    low = (square - high.astype(jnp.float32)).astype(jnp.bfloat16)
    ones = jnp.ones((8, block.shape[1]), jnp.bfloat16)
    total = lax.dot_general(ones, high, ROWS_BY_ROWS, preferred_element_type=jnp.float32)
    total += lax.dot_general(ones, low, ROWS_BY_ROWS, preferred_element_type=jnp.float32)
    return total[0:1, :]


def tile_kernel(rows_in, cols_in, spreads, weights, terms_in, backs_in, noise_in, shard, *refs):
    refs = list(refs)
    take = lambda number: [refs.pop(0) for _ in range(number)]
    rows, cols = take(rows_in), take(cols_in)
    old_terms, old_backs, noise = take(terms_in), take(backs_in), take(noise_in)
    new_backs, new_terms = take(cols_in), refs
    terms = [ref[...] for ref in old_terms] or [None] * rows_in
    row_squares = []
    for row in rows:
        wide = row[0:shard, :].astype(jnp.float32)
        row_squares.append(jnp.sum(wide * wide, axis=1, keepdims=True))
    for place, col_ref in enumerate(cols):
        col = col_ref[0:shard, :]
        col_squares = lane_squares(col)
        scaled = col * jnp.asarray(-2.0, col.dtype)
        weight = None
        if weights[place] is not None:
            outer = lax.axis_index("blk") // weights[place][0]
            weight = functools.reduce(lambda sofar, a: jnp.where(outer == a, 1.0, sofar), weights[place][1], 0.0)
        back = None
        for slot, row in enumerate(rows):
            cross = lax.dot_general(row[0:shard, :], scaled, ROWS_BY_ROWS, preferred_element_type=jnp.float32)
            kernel = matern((row_squares[slot] + col_squares) + cross)
            share = jnp.dot(row[shard:, :], kernel, preferred_element_type=jnp.float32)
            back = share if back is None else back + share
            if spreads[place]:
                term = lax.dot_general(col_ref[shard:, :], kernel, ROWS_BY_ROWS, preferred_element_type=jnp.float32)
                term = term if weight is None else weight * term
                terms[slot] = term if terms[slot] is None else terms[slot] + term
        back = back if weight is None else weight * back
        if noise and not spreads[place]:
            back = back + noise[0][...] * col_ref[shard:, :].astype(jnp.float32)
        new_backs[place][...] = old_backs[place][...] + back if old_backs else back
    for ref, term in zip(new_terms, terms):
        ref[...] = term


def tile(rows, cols, spreads, weights, terms, backs, noise, shard):
    width, vectors = rows[0].shape[1], rows[0].shape[0] - shard
    args = [*rows, *cols, *terms, *backs, *noise]
    elements = len(rows) * len(cols) * shard * shard
    whole = pl.BlockSpec(memory_space=pltpu.VMEM)
    outs = [jax.ShapeDtypeStruct((vectors, shard), jnp.float32)] * (len(cols) + len(rows))
    found = pl.pallas_call(
        functools.partial(tile_kernel, len(rows), len(cols), spreads, weights, len(terms), len(backs), len(noise), shard),
        out_shape=outs,
        in_specs=[whole] * len(args),
        out_specs=[whole] * len(outs),
        compiler_params=pltpu.CompilerParams(vmem_limit_bytes=32 * 1024 * 1024),
        cost_estimate=pl.CostEstimate(
            flops=2 * elements * (width + 2 * vectors),
            bytes_accessed=2 * width * shard * (len(rows) + len(cols)),
            transcendentals=2 * elements,
        ),
    )(*args)
    return found[: len(cols)], found[len(cols) :]


def on_device(features, probes, noise_level):
    count = lax.axis_size("blk")
    inner = group_size(count)
    outer = count // inner
    shard = features.shape[0]
    packed = jnp.concatenate([features, probes.T], axis=0)

    def along_outer(value, edges):
        return lax.ppermute(value, "blk", [(s * inner + b, t * inner + b) for s, t in edges for b in range(inner)])

    def in_plane(value, hops):
        return lax.ppermute(value, "blk", [(a * inner + s, a * inner + t) for a in range(outer) for s, t in hops])

    maps = outer_edges(outer)
    cols = [along_outer(packed, edges) for edges, _ in maps]
    weights = [None if len(targets) == outer else (inner, tuple(targets)) for _, targets in maps]
    blocks = plane_blocks(packed, inner, in_plane)

    direct = [d for d in range(inner) if d & (d - 1) == 0]
    passed = [d for d in range(inner) if d & (d - 1)]
    rows = [blocks[d] for d in direct]
    backs, terms = tile(
        rows,
        [packed] + cols[:-1],
        [False] + [True] * len(cols[:-1]),
        [None] + weights[:-1],
        [],
        [],
        [noise_level[None, :]],
        shard,
    )
    last, terms = tile(rows, cols[-1:], [True], weights[-1:], terms, [], [], shard)
    backs, late = tile(
        [blocks[d] for d in passed],
        [packed] + cols,
        [False] + [True] * len(cols),
        [None] + weights,
        [],
        list(backs) + list(last),
        [],
        shard,
    )
    total = backs[0] + terms[0]
    for step, term in zip(direct[1:] + passed, list(terms[1:]) + list(late)):
        total = total + in_plane(term, [(b, plane_target(b, step, inner)) for b in range(inner)])
    for (edges, _), back in zip(maps, backs[1:]):
        total = total + along_outer(back, [(t, s) for s, t in edges])
    return total.T


def solution(mesh):
    placed = (P(("parts", "blk"), None), P(("parts", "blk"), None), P(("parts", "blk")))
    return jax.shard_map(
        on_device, mesh=mesh, in_specs=placed, out_specs=P(("parts", "blk"), None), check_vma=False
    )
```

```python
import functools
import math

import jax
import jax.numpy as jnp
from jax import lax
from jax.experimental import pallas as pl
from jax.experimental.pallas import tpu as pltpu
from jax.sharding import PartitionSpec as P

ROOT5 = math.sqrt(5.0)
DECAY = -ROOT5 * math.log2(math.e)
ROWS_BY_ROWS = (((1,), (1,)), ((), ()))


def group_size(count):
    size = 1
    while size * size < count or count % size:
        size += 1
    return size


def plane_blocks(value, count, send):
    if count & (count - 1):
        maps = {step: [(b, (b - step) % count) for b in range(count)] for step in range(1, count)}
        return [value] + [send(value, maps[step]) for step in range(1, count)]
    blocks = {0: value}
    bit = count // 2
    while bit:
        for known in list(blocks):
            blocks[known | bit] = send(blocks[known], [(b, b ^ bit) for b in range(count)])
        bit //= 2
    return [blocks[distance] for distance in range(count)]


def plane_target(index, step, count):
    return (index + step) % count if count & (count - 1) else index ^ step


def outer_edges(count):
    maps = [([(a, (a + step) % count) for a in range(count)], range(count)) for step in range(1, (count + 1) // 2)]
    if count % 2 == 0:
        half = count // 2
        real = [(a, a + half) if a % 2 == 0 else (a + half, a) for a in range(half)]
        if half % 2 == 0:
            spare = [(a, a - 1) if a % 2 else (a + half, a + half + 1) for a in range(half)]
        else:
            spare = [(t, s) for s, t in real]
        maps.append((real + spare, [t for _, t in real]))
    return maps


def matern(dist2):
    dist2 = jnp.maximum(dist2, 1e-30)
    dist = dist2 * lax.rsqrt(dist2)
    poly = (1.0 + ROOT5 * dist) + (5.0 / 3.0) * dist2
    return (poly * jnp.exp2(DECAY * dist)).astype(jnp.bfloat16)


def lane_squares(block):
    wide = block.astype(jnp.float32)
    square = wide * wide
    high = square.astype(jnp.bfloat16)
    low = (square - high.astype(jnp.float32)).astype(jnp.bfloat16)
    ones = jnp.ones((8, block.shape[1]), jnp.bfloat16)
    total = lax.dot_general(ones, high, ROWS_BY_ROWS, preferred_element_type=jnp.float32)
    total += lax.dot_general(ones, low, ROWS_BY_ROWS, preferred_element_type=jnp.float32)
    return total[0:1, :]


def tile_kernel(rows_in, cols_in, spreads, weights, terms_in, backs_in, noise_in, extras_in, shard, *refs):
    refs = list(refs)
    take = lambda number: [refs.pop(0) for _ in range(number)]
    rows, cols = take(rows_in), take(cols_in)
    old_terms, old_backs, noise, extras = take(terms_in), take(backs_in), take(noise_in), take(extras_in)
    new_backs, new_terms = take(cols_in), refs
    terms = [ref[...] for ref in old_terms] or [None] * rows_in
    row_squares = []
    for row in rows:
        wide = row[0:shard, :].astype(jnp.float32)
        row_squares.append(jnp.sum(wide * wide, axis=1, keepdims=True))
    for place, col_ref in enumerate(cols):
        col = col_ref[0:shard, :]
        col_squares = lane_squares(col)
        scaled = col * jnp.asarray(-2.0, col.dtype)
        weight = None
        if weights[place] is not None:
            outer = lax.axis_index("blk") // weights[place][0]
            weight = functools.reduce(lambda sofar, a: jnp.where(outer == a, 1.0, sofar), weights[place][1], 0.0)
        back = None
        for slot, row in enumerate(rows):
            cross = lax.dot_general(row[0:shard, :], scaled, ROWS_BY_ROWS, preferred_element_type=jnp.float32)
            kernel = matern((row_squares[slot] + col_squares) + cross)
            share = jnp.dot(row[shard:, :], kernel, preferred_element_type=jnp.float32)
            back = share if back is None else back + share
            if spreads[place]:
                term = lax.dot_general(col_ref[shard:, :], kernel, ROWS_BY_ROWS, preferred_element_type=jnp.float32)
                term = term if weight is None else weight * term
                terms[slot] = term if terms[slot] is None else terms[slot] + term
        back = back if weight is None else weight * back
        if noise and not spreads[place]:
            back = back + noise[0][...] * col_ref[shard:, :].astype(jnp.float32)
        new_backs[place][...] = old_backs[place][...] + back if old_backs else back
    for extra in extras:
        terms[0] = terms[0] + extra[...]
    for ref, term in zip(new_terms, terms):
        ref[...] = term


def tile(rows, cols, spreads, weights, shard, terms=(), backs=(), noise=(), extras=()):
    width, vectors = rows[0].shape[1], rows[0].shape[0] - shard
    args = [*rows, *cols, *terms, *backs, *noise, *extras]
    elements = len(rows) * len(cols) * shard * shard
    whole = pl.BlockSpec(memory_space=pltpu.VMEM)
    outs = [jax.ShapeDtypeStruct((vectors, shard), jnp.float32)] * (len(cols) + len(rows))
    found = pl.pallas_call(
        functools.partial(
            tile_kernel, len(rows), len(cols), spreads, weights, len(terms), len(backs), len(noise), len(extras), shard
        ),
        out_shape=outs,
        in_specs=[whole] * len(args),
        out_specs=[whole] * len(outs),
        compiler_params=pltpu.CompilerParams(vmem_limit_bytes=32 * 1024 * 1024),
        cost_estimate=pl.CostEstimate(
            flops=2 * elements * (width + 2 * vectors),
            bytes_accessed=2 * width * shard * (len(rows) + len(cols)),
            transcendentals=2 * elements,
        ),
    )(*args)
    return found[: len(cols)], found[len(cols) :]


def on_device(features, probes, noise_level):
    count = lax.axis_size("blk")
    inner = group_size(count)
    outer = count // inner
    shard = features.shape[0]
    packed = jnp.concatenate([features, probes.T], axis=0)

    def along_outer(value, edges):
        return lax.ppermute(value, "blk", [(s * inner + b, t * inner + b) for s, t in edges for b in range(inner)])

    def in_plane(value, hops):
        return lax.ppermute(value, "blk", [(a * inner + s, a * inner + t) for a in range(outer) for s, t in hops])

    maps = outer_edges(outer)
    cols = [along_outer(packed, edges) for edges, _ in maps]
    weights = [None if len(targets) == outer else (inner, tuple(targets)) for _, targets in maps]
    blocks = plane_blocks(packed, inner, in_plane)

    backs, terms = tile(
        blocks,
        [packed] + cols[:-1],
        [False] + [True] * len(cols[:-1]),
        [None] + weights[:-1],
        shard,
        noise=[noise_level[None, :]],
    )
    returned = [along_outer(back, [(t, s) for s, t in edges]) for (edges, _), back in zip(maps, backs[1:])]
    half = inner // 2
    last, far = tile(blocks[half:], cols[-1:], [True], weights[-1:], shard, terms=terms[half:])
    last, near = tile(
        blocks[:half], cols[-1:], [True], weights[-1:], shard, terms=terms[:half], backs=last, extras=[backs[0]] + returned
    )
    total = near[0]
    for step, term in enumerate(list(near) + list(far)):
        if step:
            total = total + in_plane(term, [(b, plane_target(b, step, inner)) for b in range(inner)])
    total = total + along_outer(last[0], [(t, s) for s, t in maps[-1][0]])
    return total.T


def solution(mesh):
    placed = (P(("parts", "blk"), None), P(("parts", "blk"), None), P(("parts", "blk")))
    return jax.shard_map(
        on_device, mesh=mesh, in_specs=placed, out_specs=P(("parts", "blk"), None), check_vma=False
    )
```

```python
import functools
import math

import jax
import jax.numpy as jnp
from jax import lax
from jax.experimental import pallas as pl
from jax.experimental.pallas import tpu as pltpu
from jax.sharding import PartitionSpec as P

ROOT5 = math.sqrt(5.0)
DECAY = -ROOT5 * math.log2(math.e)
ROWS_BY_ROWS = (((1,), (1,)), ((), ()))


def group_size(count):
    size = 1
    while size * size < count or count % size:
        size += 1
    return size


def plane_blocks(value, count, send):
    if count & (count - 1):
        maps = {step: [(b, (b - step) % count) for b in range(count)] for step in range(1, count)}
        return [value] + [send(value, maps[step]) for step in range(1, count)]
    blocks = {0: value}
    bit = count // 2
    while bit:
        for known in list(blocks):
            blocks[known | bit] = send(blocks[known], [(b, b ^ bit) for b in range(count)])
        bit //= 2
    return [blocks[distance] for distance in range(count)]


def plane_target(index, step, count):
    return (index + step) % count if count & (count - 1) else index ^ step


def outer_edges(count):
    maps = [([(a, (a + step) % count) for a in range(count)], range(count)) for step in range(1, (count + 1) // 2)]
    if count % 2 == 0:
        half = count // 2
        real = [(a, a + half) if a % 2 == 0 else (a + half, a) for a in range(half)]
        if half % 2 == 0:
            spare = [(a, a - 1) if a % 2 else (a + half, a + half + 1) for a in range(half)]
        else:
            spare = [(t, s) for s, t in real]
        maps.append((real + spare, [t for _, t in real]))
    return maps


def matern(dist2):
    dist2 = jnp.maximum(dist2, 1e-30)
    dist = dist2 * lax.rsqrt(dist2)
    poly = (1.0 + ROOT5 * dist) + (5.0 / 3.0) * dist2
    return (poly * jnp.exp2(DECAY * dist)).astype(jnp.bfloat16)


def lane_squares(block):
    wide = block.astype(jnp.float32)
    square = wide * wide
    high = square.astype(jnp.bfloat16)
    low = (square - high.astype(jnp.float32)).astype(jnp.bfloat16)
    ones = jnp.ones((8, block.shape[1]), jnp.bfloat16)
    total = lax.dot_general(ones, high, ROWS_BY_ROWS, preferred_element_type=jnp.float32)
    total += lax.dot_general(ones, low, ROWS_BY_ROWS, preferred_element_type=jnp.float32)
    return total[0:1, :]


def tile_kernel(rows_in, cols_in, spreads, weights, terms_in, backs_in, noise_in, extras_in, owned, shard, *refs):
    refs = list(refs)
    take = lambda number: [refs.pop(0) for _ in range(number)]
    rows, cols = take(rows_in), take(cols_in)
    old_terms, old_backs, noise, extras = take(terms_in), take(backs_in), take(noise_in), take(extras_in)
    new_backs, new_terms = take(cols_in), refs
    terms = [ref[...] for ref in old_terms] or [None] * rows_in
    row_squares = []
    for row in rows:
        wide = row[0:shard, :].astype(jnp.float32)
        row_squares.append(jnp.sum(wide * wide, axis=1, keepdims=True))
    for place, col_ref in enumerate(cols):
        col = col_ref[0:shard, :]
        col_squares = lane_squares(col)
        scaled = col * jnp.asarray(-2.0, col.dtype)
        weight = None
        if weights[place] is not None:
            outer = lax.axis_index("blk") // weights[place][0]
            weight = functools.reduce(lambda sofar, a: jnp.where(outer == a, 1.0, sofar), weights[place][1], 0.0)
        back = None
        for slot, row in enumerate(rows):
            cross = lax.dot_general(row[0:shard, :], scaled, ROWS_BY_ROWS, preferred_element_type=jnp.float32)
            kernel = matern((row_squares[slot] + col_squares) + cross)
            share = jnp.dot(row[shard:, :], kernel, preferred_element_type=jnp.float32)
            back = share if back is None else back + share
            if spreads[place]:
                term = lax.dot_general(col_ref[shard:, :], kernel, ROWS_BY_ROWS, preferred_element_type=jnp.float32)
                term = term if weight is None else weight * term
                terms[slot] = term if terms[slot] is None else terms[slot] + term
        back = back if weight is None else weight * back
        if noise and not spreads[place]:
            back = back + noise[0][...] * col_ref[shard:, :].astype(jnp.float32)
        new_backs[place][...] = old_backs[place][...] + back if old_backs else back
    for extra in extras:
        terms[0] = terms[0] + extra[...]
    if owned:
        place = lax.rem(lax.axis_index("blk"), owned)
        for slot, term in enumerate(terms):
            new_terms[0][plane_target(place, slot, owned)] = term
    else:
        for ref, term in zip(new_terms, terms):
            ref[...] = term


def tile(rows, cols, spreads, weights, shard, terms=(), backs=(), noise=(), extras=(), owned=0):
    width, vectors = rows[0].shape[1], rows[0].shape[0] - shard
    args = [*rows, *cols, *terms, *backs, *noise, *extras]
    elements = len(rows) * len(cols) * shard * shard
    whole = pl.BlockSpec(memory_space=pltpu.VMEM)
    flat = jax.ShapeDtypeStruct((vectors, shard), jnp.float32)
    outs = [flat] * len(cols) + ([jax.ShapeDtypeStruct((owned, vectors, shard), jnp.float32)] if owned else [flat] * len(rows))
    found = pl.pallas_call(
        functools.partial(
            tile_kernel, len(rows), len(cols), spreads, weights, len(terms), len(backs), len(noise), len(extras), owned, shard
        ),
        out_shape=outs,
        in_specs=[whole] * len(args),
        out_specs=[whole] * len(outs),
        compiler_params=pltpu.CompilerParams(vmem_limit_bytes=32 * 1024 * 1024),
        cost_estimate=pl.CostEstimate(
            flops=2 * elements * (width + 2 * vectors),
            bytes_accessed=2 * width * shard * (len(rows) + len(cols)),
            transcendentals=2 * elements,
        ),
    )(*args)
    return found[: len(cols)], found[len(cols) :]


def on_device(features, probes, noise_level):
    count = lax.axis_size("blk")
    inner = group_size(count)
    outer = count // inner
    shard = features.shape[0]
    packed = jnp.concatenate([features, probes.T], axis=0)

    def along_outer(value, edges):
        return lax.ppermute(value, "blk", [(s * inner + b, t * inner + b) for s, t in edges for b in range(inner)])

    def in_plane(value, hops):
        return lax.ppermute(value, "blk", [(a * inner + s, a * inner + t) for a in range(outer) for s, t in hops])

    maps = outer_edges(outer)
    cols = [along_outer(packed, edges) for edges, _ in maps]
    weights = [None if len(targets) == outer else (inner, tuple(targets)) for _, targets in maps]
    blocks = plane_blocks(packed, inner, in_plane)

    backs, terms = tile(
        blocks,
        [packed] + cols[:-1],
        [False] + [True] * len(cols[:-1]),
        [None] + weights[:-1],
        shard,
        noise=[noise_level[None, :]],
    )
    returned = [along_outer(back, [(t, s) for s, t in edges]) for (edges, _), back in zip(maps, backs[1:])]
    last, owned = tile(blocks, cols[-1:], [True], weights[-1:], shard, terms=terms, owned=inner)
    groups = [[a * inner + b for b in range(inner)] for a in range(outer)]
    gathered = lax.all_to_all(owned[0], "blk", 0, 0, axis_index_groups=groups)
    total = backs[0] + along_outer(last[0], [(t, s) for s, t in maps[-1][0]])
    for back in returned:
        total = total + back
    total = total + jnp.sum(gathered, axis=0)
    return total.T


def solution(mesh):
    placed = (P(("parts", "blk"), None), P(("parts", "blk"), None), P(("parts", "blk")))
    return jax.shard_map(
        on_device, mesh=mesh, in_specs=placed, out_specs=P(("parts", "blk"), None), check_vma=False
    )
```

```python
import functools
import math

import jax
import jax.numpy as jnp
from jax import lax
from jax.experimental import pallas as pl
from jax.experimental.pallas import tpu as pltpu
from jax.sharding import PartitionSpec as P

ROOT5 = math.sqrt(5.0)
DECAY = -ROOT5 * math.log2(math.e)
ROWS_BY_ROWS = (((1,), (1,)), ((), ()))


def group_size(count):
    size = 1
    while size * size < count or count % size:
        size += 1
    return size


def plane_blocks(value, count, send):
    if count & (count - 1):
        maps = {step: [(b, (b - step) % count) for b in range(count)] for step in range(1, count)}
        return [value] + [send(value, maps[step]) for step in range(1, count)]
    blocks = {0: value}
    bit = count // 2
    while bit:
        for known in list(blocks):
            blocks[known | bit] = send(blocks[known], [(b, b ^ bit) for b in range(count)])
        bit //= 2
    return [blocks[distance] for distance in range(count)]


def plane_target(index, step, count):
    return (index + step) % count if count & (count - 1) else index ^ step


def outer_maps(count):
    bits = count.bit_length() - 1
    order = list(range(count))
    if count == 1 << bits:
        order = [int(f"{a:0{bits}b}"[::-1], 2) if bits else a for a in order]
    shifts = [[(order[p], order[(p + step) % count]) for p in range(count)] for step in range(1, count // 2 + 1)]
    if count % 2:
        return shifts, []
    return shifts[:-1], shifts[-1:]


def matern(dist2):
    dist2 = jnp.maximum(dist2, 1e-30)
    dist = dist2 * lax.rsqrt(dist2)
    poly = (1.0 + ROOT5 * dist) + (5.0 / 3.0) * dist2
    return (poly * jnp.exp2(DECAY * dist)).astype(jnp.bfloat16)


def lane_squares(block):
    wide = block.astype(jnp.float32)
    square = wide * wide
    high = square.astype(jnp.bfloat16)
    low = (square - high.astype(jnp.float32)).astype(jnp.bfloat16)
    ones = jnp.ones((8, block.shape[1]), jnp.bfloat16)
    total = lax.dot_general(ones, high, ROWS_BY_ROWS, preferred_element_type=jnp.float32)
    total += lax.dot_general(ones, low, ROWS_BY_ROWS, preferred_element_type=jnp.float32)
    return total[0:1, :]


def tile_kernel(shape, kinds, sums, shard, *refs):
    refs = list(refs)
    rows_in, cols_in = shape
    terms_in, backs_in, noise_in = sums
    rows, cols = refs[:rows_in], refs[rows_in : rows_in + cols_in]
    del refs[: rows_in + cols_in]
    old_terms, old_backs, noise = refs[:terms_in], refs[terms_in : terms_in + backs_in], refs[terms_in + backs_in :][:noise_in]
    del refs[: terms_in + backs_in + noise_in]
    returning = sum("back" in kind for kind in kinds)
    new_backs, new_terms = refs[:returning], refs[returning:]
    terms = [ref[...] for ref in old_terms] or [None] * rows_in
    row_squares = []
    for row in rows:
        wide = row[0:shard, :].astype(jnp.float32)
        row_squares.append(jnp.sum(wide * wide, axis=1, keepdims=True))
    filled = 0
    for kind, col_ref in zip(kinds, cols):
        col = col_ref[0:shard, :]
        col_squares = lane_squares(col)
        scaled = col * jnp.asarray(-2.0, col.dtype)
        back = old_backs[filled][...] if old_backs and "back" in kind else None
        if noise and "back" in kind:
            back = noise[0][...] * col_ref[shard:, :].astype(jnp.float32)
        for slot, row in enumerate(rows):
            cross = lax.dot_general(row[0:shard, :], scaled, ROWS_BY_ROWS, preferred_element_type=jnp.float32)
            kernel = matern((row_squares[slot] + col_squares) + cross)
            if "back" in kind:
                share = jnp.dot(row[shard:, :], kernel, preferred_element_type=jnp.float32)
                back = share if back is None else back + share
            if "rows" in kind:
                term = lax.dot_general(col_ref[shard:, :], kernel, ROWS_BY_ROWS, preferred_element_type=jnp.float32)
                terms[slot] = term if terms[slot] is None else terms[slot] + term
        if "back" in kind:
            new_backs[filled][...] = back
            filled += 1
    for ref, term in zip(new_terms, terms):
        ref[...] = term


def tile(rows, cols, kinds, shard, terms=(), backs=(), noise=()):
    width, vectors = rows[0].shape[1], rows[0].shape[0] - shard
    args = [*rows, *cols, *terms, *backs, *noise]
    elements = len(rows) * len(cols) * shard * shard
    whole = pl.BlockSpec(memory_space=pltpu.VMEM)
    returning = sum("back" in kind for kind in kinds)
    spread = len(rows) if any("rows" in kind for kind in kinds) else 0
    outs = [jax.ShapeDtypeStruct((vectors, shard), jnp.float32)] * (returning + spread)
    found = pl.pallas_call(
        functools.partial(
            tile_kernel, (len(rows), len(cols)), tuple(kinds), (len(terms), len(backs), len(noise)), shard
        ),
        out_shape=outs,
        in_specs=[whole] * len(args),
        out_specs=[whole] * len(outs),
        compiler_params=pltpu.CompilerParams(vmem_limit_bytes=32 * 1024 * 1024),
        cost_estimate=pl.CostEstimate(
            flops=2 * elements * (width + 2 * vectors),
            bytes_accessed=2 * width * shard * (len(rows) + len(cols)),
            transcendentals=2 * elements,
        ),
    )(*args)
    return found[:returning], found[returning:]


def on_device(features, probes, noise_level):
    count = lax.axis_size("blk")
    inner = group_size(count)
    outer = count // inner
    shard = features.shape[0]
    packed = jnp.concatenate([features, probes.T], axis=0)

    def along_outer(value, edges):
        return lax.ppermute(value, "blk", [(s * inner + b, t * inner + b) for s, t in edges for b in range(inner)])

    def in_plane(value, hops):
        return lax.ppermute(value, "blk", [(a * inner + s, a * inner + t) for a in range(outer) for s, t in hops])

    one_way, exchanges = outer_maps(outer)
    cols = [along_outer(packed, edges) for edges in one_way + exchanges]
    kinds = [("rows", "back")] * len(one_way) + [("rows",)] * len(exchanges)
    blocks = plane_blocks(packed, inner, in_plane)

    direct = [d for d in range(inner) if d & (d - 1) == 0]
    passed = [d for d in range(inner) if d & (d - 1)]
    backs, terms = tile([blocks[d] for d in direct], cols, kinds, shard)
    backs, late = tile([blocks[d] for d in passed], cols, kinds, shard, backs=backs)
    (total,), _ = tile(blocks, [packed], [("back",)], shard, noise=[noise_level[None, :]])
    for back, edges in zip(backs, one_way):
        total = total + along_outer(back, [(t, s) for s, t in edges])
    for step, term in zip(direct + passed, list(terms) + list(late)):
        total = total + (in_plane(term, [(b, plane_target(b, step, inner)) for b in range(inner)]) if step else term)
    return total.T


def solution(mesh):
    placed = (P(("parts", "blk"), None), P(("parts", "blk"), None), P(("parts", "blk")))
    return jax.shard_map(
        on_device, mesh=mesh, in_specs=placed, out_specs=P(("parts", "blk"), None), check_vma=False
    )
```

```python
import functools
import math

import jax
import jax.numpy as jnp
from jax import lax
from jax.experimental import pallas as pl
from jax.experimental.pallas import tpu as pltpu
from jax.sharding import PartitionSpec as P

ROOT5 = math.sqrt(5.0)
DECAY = -ROOT5 * math.log2(math.e)
ROWS_BY_ROWS = (((1,), (1,)), ((), ()))


def group_size(count):
    size = 1
    while size * size < count or count % size:
        size += 1
    return size


def plane_target(index, step, count):
    return (index + step) % count if count & (count - 1) else index ^ step


def outer_maps(count):
    bits = count.bit_length() - 1
    order = list(range(count))
    if count == 1 << bits:
        order = [int(f"{a:0{bits}b}"[::-1], 2) if bits else a for a in order]
    shifts = [[(order[p], order[(p + step) % count]) for p in range(count)] for step in range(1, count // 2 + 1)]
    if count % 2:
        return shifts, []
    return shifts[:-1], shifts[-1:]


def matern(dist2):
    dist2 = jnp.maximum(dist2, 1e-30)
    dist = dist2 * lax.rsqrt(dist2)
    poly = (1.0 + ROOT5 * dist) + (5.0 / 3.0) * dist2
    return (poly * jnp.exp2(DECAY * dist)).astype(jnp.bfloat16)


def lane_squares(block):
    wide = block.astype(jnp.float32)
    square = wide * wide
    high = square.astype(jnp.bfloat16)
    low = (square - high.astype(jnp.float32)).astype(jnp.bfloat16)
    ones = jnp.ones((8, block.shape[1]), jnp.bfloat16)
    total = lax.dot_general(ones, high, ROWS_BY_ROWS, preferred_element_type=jnp.float32)
    total += lax.dot_general(ones, low, ROWS_BY_ROWS, preferred_element_type=jnp.float32)
    return total[0:1, :]


def tile_kernel(shape, order, kinds, sums, shard, *refs):
    refs = list(refs)
    rows_in, cols_in = shape
    terms_in, backs_in, noise_in = sums
    blocks = [refs.pop(0) for _ in range(rows_in + cols_in)]
    rows, cols = [blocks[place] for place in order[:rows_in]], [blocks[place] for place in order[rows_in:]]
    old_terms, old_backs, noise = refs[:terms_in], refs[terms_in : terms_in + backs_in], refs[terms_in + backs_in :][:noise_in]
    del refs[: terms_in + backs_in + noise_in]
    returning = sum("back" in kind for kind in kinds)
    new_backs, new_terms = refs[:returning], refs[returning:]
    terms = [ref[...] for ref in old_terms] or [None] * rows_in
    row_squares = []
    for row in rows:
        wide = row[0:shard, :].astype(jnp.float32)
        row_squares.append(jnp.sum(wide * wide, axis=1, keepdims=True))
    filled = 0
    for kind, col_ref in zip(kinds, cols):
        col = col_ref[0:shard, :]
        col_squares = lane_squares(col)
        scaled = col * jnp.asarray(-2.0, col.dtype)
        back = old_backs[filled][...] if old_backs and "back" in kind else None
        if noise and "back" in kind:
            back = noise[0][...] * col_ref[shard:, :].astype(jnp.float32)
        for slot, row in enumerate(rows):
            cross = lax.dot_general(row[0:shard, :], scaled, ROWS_BY_ROWS, preferred_element_type=jnp.float32)
            kernel = matern((row_squares[slot] + col_squares) + cross)
            if "back" in kind:
                share = jnp.dot(row[shard:, :], kernel, preferred_element_type=jnp.float32)
                back = share if back is None else back + share
            if "rows" in kind:
                term = lax.dot_general(col_ref[shard:, :], kernel, ROWS_BY_ROWS, preferred_element_type=jnp.float32)
                terms[slot] = term if terms[slot] is None else terms[slot] + term
        if "back" in kind:
            new_backs[filled][...] = back
            filled += 1
    for ref, term in zip(new_terms, terms):
        ref[...] = term


def tile(rows, cols, order, kinds, shard, terms=(), backs=(), noise=()):
    width, vectors = rows[0].shape[1], rows[0].shape[0] - shard
    blocks = [*rows, *cols]
    args = [*[blocks[place] for place in order], *terms, *backs, *noise]
    elements = len(rows) * len(cols) * shard * shard
    whole = pl.BlockSpec(memory_space=pltpu.VMEM)
    returning = sum("back" in kind for kind in kinds)
    spread = len(rows) if any("rows" in kind for kind in kinds) else 0
    outs = [jax.ShapeDtypeStruct((vectors, shard), jnp.float32)] * (returning + spread)
    found = pl.pallas_call(
        functools.partial(
            tile_kernel,
            (len(rows), len(cols)),
            [list(order).index(place) for place in range(len(blocks))],
            tuple(kinds),
            (len(terms), len(backs), len(noise)),
            shard,
        ),
        out_shape=outs,
        in_specs=[whole] * len(args),
        out_specs=[whole] * len(outs),
        compiler_params=pltpu.CompilerParams(vmem_limit_bytes=32 * 1024 * 1024),
        cost_estimate=pl.CostEstimate(
            flops=2 * elements * (width + 2 * vectors),
            bytes_accessed=2 * width * shard * (len(rows) + len(cols)),
            transcendentals=2 * elements,
        ),
    )(*args)
    return found[:returning], found[returning:]


def on_device(features, probes, noise_level):
    count = lax.axis_size("blk")
    inner = group_size(count)
    outer = count // inner
    shard = features.shape[0]
    packed = jnp.concatenate([features, probes.T], axis=0)

    def along_outer(value, edges):
        return lax.ppermute(value, "blk", [(s * inner + b, t * inner + b) for s, t in edges for b in range(inner)])

    def in_plane(value, hops):
        return lax.ppermute(value, "blk", [(a * inner + s, a * inner + t) for a in range(outer) for s, t in hops])

    def near(step):
        return [(plane_target(b, step, inner), b) for b in range(inner)]

    one_way, exchanges = outer_maps(outer)
    cols = [along_outer(packed, edges) for edges in one_way + exchanges]
    kinds = [("rows", "back")] * len(one_way) + [("rows",)] * len(exchanges)
    blocks = [packed] + [in_plane(packed, near(step)) for step in range(1, inner)]

    first = [inner + place for place in range(len(one_way))]
    last = [inner + place for place in range(len(one_way), len(cols))]
    order = [0, 1] + last + list(range(inner - 1, 1, -1)) + first if inner > 1 else [0] + last + first
    backs, terms = tile(blocks, cols, order, kinds, shard)
    sums = [along_outer(back, [(t, s) for s, t in edges]) for back, edges in zip(backs, one_way)]
    sums += [in_plane(terms[step], [(t, s) for s, t in near(step)]) for step in range(inner - 1, 0, -1)]
    (own,), _ = tile(blocks, [packed], range(inner + 1), [("back",)], shard, noise=[noise_level[None, :]])
    return functools.reduce(lambda total, term: total + term, sums + list(terms[:1]) + [own]).T


def solution(mesh):
    placed = (P(("parts", "blk"), None), P(("parts", "blk"), None), P(("parts", "blk")))
    return jax.shard_map(
        on_device, mesh=mesh, in_specs=placed, out_specs=P(("parts", "blk"), None), check_vma=False
    )
```

```python
import functools
import math

import jax
import jax.numpy as jnp
from jax import lax
from jax.experimental import pallas as pl
from jax.experimental.pallas import tpu as pltpu
from jax.sharding import PartitionSpec as P

ROOT5 = math.sqrt(5.0)
DECAY = -ROOT5 * math.log2(math.e)
ROWS_BY_ROWS = (((1,), (1,)), ((), ()))


def group_size(count):
    size = 1
    while size * size < count or count % size:
        size += 1
    return size


def plane_blocks(value, count, send):
    if count & (count - 1):
        maps = {step: [(b, (b - step) % count) for b in range(count)] for step in range(1, count)}
        return [value] + [send(value, maps[step]) for step in range(1, count)]
    blocks = {0: value}
    bit = count // 2
    while bit:
        for known in list(blocks):
            blocks[known | bit] = send(blocks[known], [(b, b ^ bit) for b in range(count)])
        bit //= 2
    return [blocks[distance] for distance in range(count)]


def plane_target(index, step, count):
    return (index + step) % count if count & (count - 1) else index ^ step


def outer_maps(count):
    bits = count.bit_length() - 1
    order = list(range(count))
    if count == 1 << bits:
        order = [int(f"{a:0{bits}b}"[::-1], 2) if bits else a for a in order]
    shifts = [[(order[p], order[(p + step) % count]) for p in range(count)] for step in range(1, count // 2 + 1)]
    if count % 2:
        return shifts, []
    return shifts[:-1], shifts[-1:]


def matern(dist2):
    dist2 = jnp.maximum(dist2, 1e-30)
    dist = dist2 * lax.rsqrt(dist2)
    poly = (1.0 + ROOT5 * dist) + (5.0 / 3.0) * dist2
    return (poly * jnp.exp2(DECAY * dist)).astype(jnp.bfloat16)


def lane_squares(block):
    wide = block.astype(jnp.float32)
    square = wide * wide
    high = square.astype(jnp.bfloat16)
    low = (square - high.astype(jnp.float32)).astype(jnp.bfloat16)
    ones = jnp.ones((8, block.shape[1]), jnp.bfloat16)
    total = lax.dot_general(ones, high, ROWS_BY_ROWS, preferred_element_type=jnp.float32)
    total += lax.dot_general(ones, low, ROWS_BY_ROWS, preferred_element_type=jnp.float32)
    return total[0:1, :]


def tile_kernel(shape, order, kinds, sums, shard, *refs):
    refs = list(refs)
    rows_in, cols_in = shape
    terms_in, backs_in, noise_in = sums
    blocks = [refs.pop(0) for _ in range(rows_in + cols_in)]
    rows, cols = [blocks[place] for place in order[:rows_in]], [blocks[place] for place in order[rows_in:]]
    old_terms, old_backs, noise = refs[:terms_in], refs[terms_in : terms_in + backs_in], refs[terms_in + backs_in :][:noise_in]
    del refs[: terms_in + backs_in + noise_in]
    returning = sum("back" in kind for kind in kinds)
    new_backs, new_terms = refs[:returning], refs[returning:]
    terms = [ref[...] for ref in old_terms] or [None] * rows_in
    row_squares = []
    for row in rows:
        wide = row[0:shard, :].astype(jnp.float32)
        row_squares.append(jnp.sum(wide * wide, axis=1, keepdims=True))
    filled = 0
    for kind, col_ref in zip(kinds, cols):
        col = col_ref[0:shard, :]
        col_squares = lane_squares(col)
        scaled = col * jnp.asarray(-2.0, col.dtype)
        back = old_backs[filled][...] if old_backs and "back" in kind else None
        if noise and "back" in kind:
            back = noise[0][...] * col_ref[shard:, :].astype(jnp.float32)
        for slot, row in enumerate(rows):
            cross = lax.dot_general(row[0:shard, :], scaled, ROWS_BY_ROWS, preferred_element_type=jnp.float32)
            kernel = matern((row_squares[slot] + col_squares) + cross)
            if "back" in kind:
                share = jnp.dot(row[shard:, :], kernel, preferred_element_type=jnp.float32)
                back = share if back is None else back + share
            if "rows" in kind:
                term = lax.dot_general(col_ref[shard:, :], kernel, ROWS_BY_ROWS, preferred_element_type=jnp.float32)
                terms[slot] = term if terms[slot] is None else terms[slot] + term
        if "back" in kind:
            new_backs[filled][...] = back
            filled += 1
    for ref, term in zip(new_terms, terms):
        ref[...] = term


def tile(rows, cols, order, kinds, shard, terms=(), backs=(), noise=()):
    width, vectors = rows[0].shape[1], rows[0].shape[0] - shard
    blocks = [*rows, *cols]
    args = [*[blocks[place] for place in order], *terms, *backs, *noise]
    elements = len(rows) * len(cols) * shard * shard
    whole = pl.BlockSpec(memory_space=pltpu.VMEM)
    returning = sum("back" in kind for kind in kinds)
    spread = len(rows) if any("rows" in kind for kind in kinds) else 0
    outs = [jax.ShapeDtypeStruct((vectors, shard), jnp.float32)] * (returning + spread)
    found = pl.pallas_call(
        functools.partial(
            tile_kernel,
            (len(rows), len(cols)),
            [list(order).index(place) for place in range(len(blocks))],
            tuple(kinds),
            (len(terms), len(backs), len(noise)),
            shard,
        ),
        out_shape=outs,
        in_specs=[whole] * len(args),
        out_specs=[whole] * len(outs),
        compiler_params=pltpu.CompilerParams(vmem_limit_bytes=32 * 1024 * 1024),
        cost_estimate=pl.CostEstimate(
            flops=2 * elements * (width + 2 * vectors),
            bytes_accessed=2 * width * shard * (len(rows) + len(cols)),
            transcendentals=2 * elements,
        ),
    )(*args)
    return found[:returning], found[returning:]


def on_device(features, probes, noise_level):
    count = lax.axis_size("blk")
    inner = group_size(count)
    outer = count // inner
    shard = features.shape[0]
    packed = jnp.concatenate([features, probes.T], axis=0)

    def along_outer(value, edges):
        return lax.ppermute(value, "blk", [(s * inner + b, t * inner + b) for s, t in edges for b in range(inner)])

    def in_plane(value, hops):
        return lax.ppermute(value, "blk", [(a * inner + s, a * inner + t) for a in range(outer) for s, t in hops])

    def near(step):
        return [(plane_target(b, step, inner), b) for b in range(inner)]

    one_way, exchanges = outer_maps(outer)
    cols = [along_outer(packed, edges) for edges in one_way + exchanges]
    kinds = [("rows", "back")] * len(one_way) + [("rows",)] * len(exchanges)
    blocks = plane_blocks(packed, inner, in_plane)

    direct = [step for step in range(1, inner) if step & (step - 1) == 0]
    passed = [step for step in range(1, inner) if step & (step - 1)]
    first = [inner + place for place in range(len(one_way))]
    last = [inner + place for place in range(len(one_way), len(cols))]
    order = [0] + passed + last + direct[:1] + first + direct[1:]
    backs, terms = tile(blocks, cols, order, kinds, shard)
    sums = [along_outer(back, [(t, s) for s, t in edges]) for back, edges in zip(backs, one_way)]
    sums += [in_plane(terms[step], [(t, s) for s, t in near(step)]) for step in range(inner - 1, 0, -1)]
    (own,), _ = tile(blocks, [packed], range(inner + 1), [("back",)], shard, noise=[noise_level[None, :]])
    return functools.reduce(lambda total, term: total + term, sums + list(terms[:1]) + [own]).T


def solution(mesh):
    placed = (P(("parts", "blk"), None), P(("parts", "blk"), None), P(("parts", "blk")))
    return jax.shard_map(
        on_device, mesh=mesh, in_specs=placed, out_specs=P(("parts", "blk"), None), check_vma=False
    )
```

```python
import functools
import math

import jax
import jax.numpy as jnp
from jax import lax
from jax.experimental import pallas as pl
from jax.experimental.pallas import tpu as pltpu
from jax.sharding import PartitionSpec as P

ROOT5 = math.sqrt(5.0)
DECAY = -ROOT5 * math.log2(math.e)
ROWS_BY_ROWS = (((1,), (1,)), ((), ()))


def group_size(count):
    size = 1
    while size * size < count or count % size:
        size += 1
    return size


def plane_blocks(value, count, send):
    if count & (count - 1):
        maps = {step: [(b, (b - step) % count) for b in range(count)] for step in range(1, count)}
        return [value] + [send(value, maps[step]) for step in range(1, count)]
    blocks = {0: value}
    bit = count // 2
    while bit:
        for known in list(blocks):
            blocks[known | bit] = send(blocks[known], [(b, b ^ bit) for b in range(count)])
        bit //= 2
    return [blocks[distance] for distance in range(count)]


def plane_target(index, step, count):
    return (index + step) % count if count & (count - 1) else index ^ step


def outer_maps(count):
    bits = count.bit_length() - 1
    order = list(range(count))
    if count == 1 << bits:
        order = [int(f"{a:0{bits}b}"[::-1], 2) if bits else a for a in order]
    shifts = [[(order[p], order[(p + step) % count]) for p in range(count)] for step in range(1, count // 2 + 1)]
    if count % 2:
        return shifts, []
    return shifts[:-1], shifts[-1:]


def matern(dist2):
    dist2 = jnp.maximum(dist2, 1e-30)
    dist = dist2 * lax.rsqrt(dist2)
    poly = (1.0 + ROOT5 * dist) + (5.0 / 3.0) * dist2
    return (poly * jnp.exp2(DECAY * dist)).astype(jnp.bfloat16)


def lane_squares(block):
    wide = block.astype(jnp.float32)
    square = wide * wide
    high = square.astype(jnp.bfloat16)
    low = (square - high.astype(jnp.float32)).astype(jnp.bfloat16)
    ones = jnp.ones((8, block.shape[1]), jnp.bfloat16)
    total = lax.dot_general(ones, high, ROWS_BY_ROWS, preferred_element_type=jnp.float32)
    total += lax.dot_general(ones, low, ROWS_BY_ROWS, preferred_element_type=jnp.float32)
    return total[0:1, :]


def tile_kernel(order, pairs, known, counts, shard, vectors, *refs):
    rows_in, cols_in, noise_in = counts
    blocks = [refs[order.index(place)] for place in range(rows_in + cols_in)]
    rows, cols = blocks[:rows_in], blocks[rows_in:]
    rest = list(refs[rows_in + cols_in :])
    noise = [rest.pop(0) for _ in range(noise_in)]
    sums = {name: rest.pop(0)[...] for name in known}
    ready_rows, ready_cols = {}, {}
    for row, col, kind in pairs:
        if row not in ready_rows:
            wide = rows[row][0:shard, :].astype(jnp.float32)
            ready_rows[row] = jnp.sum(wide * wide, axis=1, keepdims=True)
        if col not in ready_cols:
            block = cols[col][0:shard, :]
            ready_cols[col] = block * jnp.asarray(-2.0, block.dtype), lane_squares(block)
        scaled, col_squares = ready_cols[col]
        row_block, row_probes = rows[row][0:shard, :], rows[row][pl.ds(shard, vectors), :]
        cross = lax.dot_general(row_block, scaled, ROWS_BY_ROWS, preferred_element_type=jnp.float32)
        kernel = matern((ready_rows[row] + col_squares) + cross)
        found = {}
        if "back" in kind:
            found["back", col] = jnp.dot(row_probes, kernel, preferred_element_type=jnp.float32)
        if "rows" in kind:
            col_probes = cols[col][pl.ds(shard, vectors), :]
            found["rows", row] = lax.dot_general(col_probes, kernel, ROWS_BY_ROWS, preferred_element_type=jnp.float32)
        for name, value in found.items():
            sums[name] = sums[name] + value if name in sums else value
    for place in range(noise_in):
        probes = cols[place][pl.ds(shard, vectors), :].astype(jnp.float32)
        sums["back", place] = sums["back", place] + noise[place][...] * probes
    for ref, name in zip(rest, sorted(sums)):
        ref[...] = sums[name]


def tile(rows, cols, order, pairs, sums, shard, vectors, noise=(), waits=1):
    blocks = [*rows, *cols]
    args = [*[blocks[place] for place in order], *noise, *sums.values()]
    elements = len(pairs) * shard * shard
    width = rows[0].shape[1]
    names = sorted({(part, col if part == "back" else row) for row, col, kind in pairs for part in kind} | set(sums))
    whole = pl.BlockSpec(memory_space=pltpu.VMEM)
    found = pl.pallas_call(
        functools.partial(
            tile_kernel, list(order), tuple(pairs), tuple(sums), (len(rows), len(cols), len(noise)), shard, vectors
        ),
        out_shape=[jax.ShapeDtypeStruct((vectors, shard), jnp.float32)] * len(names),
        in_specs=[whole] * len(args),
        out_specs=[whole] * len(names),
        compiler_params=pltpu.CompilerParams(vmem_limit_bytes=32 * 1024 * 1024),
        cost_estimate=pl.CostEstimate(
            flops=2 * elements * (width + 2 * vectors) * waits,
            bytes_accessed=2 * width * shard * len(blocks),
            transcendentals=2 * elements,
        ),
    )(*args)
    return dict(zip(names, found))


def copy_kernel(from_ref, to_ref):
    to_ref[...] = from_ref[0 : to_ref.shape[0], :]


def copy_rows(value, rows):
    whole = pl.BlockSpec(memory_space=pltpu.VMEM)
    return pl.pallas_call(
        copy_kernel,
        out_shape=jax.ShapeDtypeStruct((rows, value.shape[1]), value.dtype),
        in_specs=[whole],
        out_specs=whole,
    )(value)


def on_device(features, probes, noise_level):
    count = lax.axis_size("blk")
    inner = group_size(count)
    outer = count // inner
    shard, width = features.shape
    vectors = probes.shape[1]
    spare = jnp.zeros((16, width), features.dtype)
    longer = jnp.concatenate([features, probes.T, spare], axis=0)
    packed = copy_rows(longer, shard + vectors)

    def along_outer(value, edges):
        return lax.ppermute(value, "blk", [(s * inner + b, t * inner + b) for s, t in edges for b in range(inner)])

    def in_plane(value, hops):
        return lax.ppermute(value, "blk", [(a * inner + s, a * inner + t) for a in range(outer) for s, t in hops])

    def near(step):
        return [(plane_target(b, step, inner), b) for b in range(inner)]

    one_way, exchanges = outer_maps(outer)
    cols = [along_outer(longer, edges) for edges in one_way] + [along_outer(packed, edges) for edges in exchanges]
    kinds = [("rows", "back")] * len(one_way) + [("rows",)] * len(exchanges)
    blocks = plane_blocks(packed, inner, in_plane)
    direct = [step for step in range(inner) if step & (step - 1) == 0]
    passed = [step for step in range(inner) if step & (step - 1)]

    early = [(row, col, kinds[col]) for col in range(len(one_way)) for row in range(len(direct))]
    order = [0, 1] + list(range(len(direct), len(direct) + len(one_way))) + list(range(2, len(direct)))
    sums = tile([blocks[step] for step in direct], cols[: len(one_way)], order, early, {}, shard, vectors, waits=1000)
    sums = {(part, direct[place] if part == "rows" else place): value for (part, place), value in sums.items()}
    late = [(row, col, kinds[col]) for col in range(len(cols)) for row in range(inner) if col >= len(one_way) or row in passed]
    sums = tile(blocks, cols, range(inner + len(cols)), late, sums, shard, vectors)

    total = [along_outer(sums["back", place], [(t, s) for s, t in edges]) for place, edges in enumerate(one_way)]
    total += [in_plane(sums["rows", step], [(t, s) for s, t in near(step)]) for step in range(inner - 1, 0, -1)]
    own = [(row, 0, ("back",)) for row in range(inner)]
    own = tile(blocks, [packed], range(inner + 1), own, {}, shard, vectors, noise=[noise_level[None, :]])
    return functools.reduce(lambda total, term: total + term, total + [sums["rows", 0], own["back", 0]]).T


def solution(mesh):
    placed = (P(("parts", "blk"), None), P(("parts", "blk"), None), P(("parts", "blk")))
    return jax.shard_map(
        on_device, mesh=mesh, in_specs=placed, out_specs=P(("parts", "blk"), None), check_vma=False
    )
```

```python
import functools
import math

import jax
import jax.numpy as jnp
from jax import lax
from jax.experimental import pallas as pl
from jax.experimental.pallas import tpu as pltpu
from jax.sharding import PartitionSpec as P

ROOT5 = math.sqrt(5.0)
DECAY = -ROOT5 * math.log2(math.e)
ROWS_BY_ROWS = (((1,), (1,)), ((), ()))


def group_size(count):
    size = 1
    while size * size < count or count % size:
        size += 1
    return size


def plane_blocks(value, count, send):
    if count & (count - 1):
        maps = {step: [(b, (b - step) % count) for b in range(count)] for step in range(1, count)}
        return [value] + [send(value, maps[step]) for step in range(1, count)]
    blocks = {0: value}
    bit = count // 2
    while bit:
        for known in list(blocks):
            blocks[known | bit] = send(blocks[known], [(b, b ^ bit) for b in range(count)])
        bit //= 2
    return [blocks[distance] for distance in range(count)]


def plane_target(index, step, count):
    return (index + step) % count if count & (count - 1) else index ^ step


def outer_maps(count):
    bits = count.bit_length() - 1
    order = list(range(count))
    if count == 1 << bits:
        order = [int(f"{a:0{bits}b}"[::-1], 2) if bits else a for a in order]
    shifts = [[(order[p], order[(p + step) % count]) for p in range(count)] for step in range(1, count // 2 + 1)]
    if count % 2:
        return shifts, []
    return shifts[:-1], shifts[-1:]


def matern(dist2):
    dist2 = jnp.maximum(dist2, 1e-30)
    dist = dist2 * lax.rsqrt(dist2)
    poly = (1.0 + ROOT5 * dist) + (5.0 / 3.0) * dist2
    return (poly * jnp.exp2(DECAY * dist)).astype(jnp.bfloat16)


def lane_squares(block):
    wide = block.astype(jnp.float32)
    square = wide * wide
    high = square.astype(jnp.bfloat16)
    low = (square - high.astype(jnp.float32)).astype(jnp.bfloat16)
    ones = jnp.ones((8, block.shape[1]), jnp.bfloat16)
    total = lax.dot_general(ones, high, ROWS_BY_ROWS, preferred_element_type=jnp.float32)
    total += lax.dot_general(ones, low, ROWS_BY_ROWS, preferred_element_type=jnp.float32)
    return total[0:1, :]


def tile_kernel(order, pairs, known, counts, shard, vectors, *refs):
    rows_in, cols_in, noise_in = counts
    blocks = [refs[order.index(place)] for place in range(rows_in + cols_in)]
    rows, cols = blocks[:rows_in], blocks[rows_in:]
    rest = list(refs[rows_in + cols_in :])
    noise = [rest.pop(0) for _ in range(noise_in)]
    sums = {name: rest.pop(0)[...] for name in known}
    ready_rows, ready_cols = {}, {}
    for row, col, kind in pairs:
        if row not in ready_rows:
            wide = rows[row][0:shard, :].astype(jnp.float32)
            ready_rows[row] = jnp.sum(wide * wide, axis=1, keepdims=True)
        if col not in ready_cols:
            block = cols[col][0:shard, :]
            ready_cols[col] = block * jnp.asarray(-2.0, block.dtype), lane_squares(block)
        scaled, col_squares = ready_cols[col]
        row_block, row_probes = rows[row][0:shard, :], rows[row][pl.ds(shard, vectors), :]
        cross = lax.dot_general(row_block, scaled, ROWS_BY_ROWS, preferred_element_type=jnp.float32)
        kernel = matern((ready_rows[row] + col_squares) + cross)
        found = {}
        if "back" in kind:
            found["back", col] = jnp.dot(row_probes, kernel, preferred_element_type=jnp.float32)
        if "rows" in kind:
            col_probes = cols[col][pl.ds(shard, vectors), :]
            found["rows", row] = lax.dot_general(col_probes, kernel, ROWS_BY_ROWS, preferred_element_type=jnp.float32)
        for name, value in found.items():
            sums[name] = sums[name] + value if name in sums else value
    for place in range(noise_in):
        probes = cols[place][pl.ds(shard, vectors), :].astype(jnp.float32)
        sums["back", place] = sums["back", place] + noise[place][...] * probes
    for ref, name in zip(rest, sorted(sums)):
        ref[...] = sums[name]


def tile(rows, cols, order, pairs, sums, shard, vectors, noise=(), waits=1):
    blocks = [*rows, *cols]
    args = [*[blocks[place] for place in order], *noise, *sums.values()]
    elements = len(pairs) * shard * shard
    width = rows[0].shape[1]
    names = sorted({(part, col if part == "back" else row) for row, col, kind in pairs for part in kind} | set(sums))
    whole = pl.BlockSpec(memory_space=pltpu.VMEM)
    found = pl.pallas_call(
        functools.partial(
            tile_kernel, list(order), tuple(pairs), tuple(sums), (len(rows), len(cols), len(noise)), shard, vectors
        ),
        out_shape=[jax.ShapeDtypeStruct((vectors, shard), jnp.float32)] * len(names),
        in_specs=[whole] * len(args),
        out_specs=[whole] * len(names),
        compiler_params=pltpu.CompilerParams(vmem_limit_bytes=32 * 1024 * 1024),
        cost_estimate=pl.CostEstimate(
            flops=2 * elements * (width + 2 * vectors) * waits,
            bytes_accessed=2 * width * shard * len(blocks),
            transcendentals=2 * elements,
        ),
    )(*args)
    return dict(zip(names, found))


def copy_kernel(from_ref, to_ref):
    to_ref[...] = from_ref[0 : to_ref.shape[0], :]


def copy_rows(value, rows):
    whole = pl.BlockSpec(memory_space=pltpu.VMEM)
    return pl.pallas_call(
        copy_kernel,
        out_shape=jax.ShapeDtypeStruct((rows, value.shape[1]), value.dtype),
        in_specs=[whole],
        out_specs=whole,
        compiler_params=pltpu.CompilerParams(vmem_limit_bytes=32 * 1024 * 1024),
    )(value)


def on_device(features, probes, noise_level):
    count = lax.axis_size("blk")
    inner = group_size(count)
    outer = count // inner
    shard, width = features.shape
    vectors = probes.shape[1]
    spare = jnp.zeros((16, width), features.dtype)
    longer = jnp.concatenate([features, probes.T, spare], axis=0)
    packed = copy_rows(longer, shard + vectors)

    def along_outer(value, edges):
        return lax.ppermute(value, "blk", [(s * inner + b, t * inner + b) for s, t in edges for b in range(inner)])

    def in_plane(value, hops):
        return lax.ppermute(value, "blk", [(a * inner + s, a * inner + t) for a in range(outer) for s, t in hops])

    def near(step):
        return [(plane_target(b, step, inner), b) for b in range(inner)]

    one_way, exchanges = outer_maps(outer)
    cols = [along_outer(longer, edges) for edges in one_way] + [along_outer(packed, edges) for edges in exchanges]
    kinds = [("rows", "back")] * len(one_way) + [("rows",)] * len(exchanges)
    blocks = plane_blocks(packed, inner, in_plane)
    direct = [step for step in range(inner) if step & (step - 1) == 0]
    passed = [step for step in range(inner) if step & (step - 1)]

    early = [(row, col, kinds[col]) for col in range(len(one_way)) for row in range(len(direct))]
    order = [0, 1] + list(range(len(direct), len(direct) + len(one_way))) + list(range(2, len(direct)))
    sums = tile([blocks[step] for step in direct], cols[: len(one_way)], order, early, {}, shard, vectors, waits=1000)
    sums = {(part, direct[place] if part == "rows" else place): value for (part, place), value in sums.items()}
    late = [(row, col, kinds[col]) for col in range(len(cols)) for row in range(inner) if col >= len(one_way) or row in passed]
    sums = tile(blocks, cols, range(inner + len(cols)), late, sums, shard, vectors)

    total = [along_outer(sums["back", place], [(t, s) for s, t in edges]) for place, edges in enumerate(one_way)]
    total += [in_plane(sums["rows", step], [(t, s) for s, t in near(step)]) for step in range(inner - 1, 0, -1)]
    own = [(row, 0, ("back",)) for row in range(inner)]
    own = tile(blocks, [packed], range(inner + 1), own, {}, shard, vectors, noise=[noise_level[None, :]])
    return functools.reduce(lambda total, term: total + term, total + [sums["rows", 0], own["back", 0]]).T


def solution(mesh):
    placed = (P(("parts", "blk"), None), P(("parts", "blk"), None), P(("parts", "blk")))
    return jax.shard_map(
        on_device, mesh=mesh, in_specs=placed, out_specs=P(("parts", "blk"), None), check_vma=False
    )
```

```python
import functools
import math

import jax
import jax.numpy as jnp
from jax import lax
from jax.experimental import pallas as pl
from jax.experimental.pallas import tpu as pltpu
from jax.sharding import PartitionSpec as P

ROOT5 = math.sqrt(5.0)
DECAY = -ROOT5 * math.log2(math.e)
ROWS_BY_ROWS = (((1,), (1,)), ((), ()))


def group_size(count):
    size = 1
    while size * size < count or count % size:
        size += 1
    return size


def plane_blocks(value, count, send):
    if count & (count - 1):
        maps = {step: [(b, (b - step) % count) for b in range(count)] for step in range(1, count)}
        return [value] + [send(value, maps[step]) for step in range(1, count)]
    blocks = {0: value}
    bit = count // 2
    while bit:
        for known in list(blocks):
            blocks[known | bit] = send(blocks[known], [(b, b ^ bit) for b in range(count)])
        bit //= 2
    return [blocks[distance] for distance in range(count)]


def plane_target(index, step, count):
    return (index + step) % count if count & (count - 1) else index ^ step


def outer_maps(count):
    bits = count.bit_length() - 1
    order = list(range(count))
    if count == 1 << bits:
        order = [int(f"{a:0{bits}b}"[::-1], 2) if bits else a for a in order]
    shifts = [[(order[p], order[(p + step) % count]) for p in range(count)] for step in range(1, count // 2 + 1)]
    if count % 2:
        return shifts, []
    return shifts[:-1], shifts[-1:]


def matern(dist2):
    dist2 = jnp.maximum(dist2, 1e-30)
    dist = dist2 * lax.rsqrt(dist2)
    poly = (1.0 + ROOT5 * dist) + (5.0 / 3.0) * dist2
    return (poly * jnp.exp2(DECAY * dist)).astype(jnp.bfloat16)


def lane_squares(block):
    wide = block.astype(jnp.float32)
    square = wide * wide
    high = square.astype(jnp.bfloat16)
    low = (square - high.astype(jnp.float32)).astype(jnp.bfloat16)
    ones = jnp.ones((8, block.shape[1]), jnp.bfloat16)
    total = lax.dot_general(ones, high, ROWS_BY_ROWS, preferred_element_type=jnp.float32)
    total += lax.dot_general(ones, low, ROWS_BY_ROWS, preferred_element_type=jnp.float32)
    return total[0:1, :]


def tile_kernel(order, pairs, known, counts, shard, vectors, *refs):
    rows_in, cols_in, noise_in = counts
    blocks = [refs[order.index(place)] for place in range(rows_in + cols_in)]
    rows, cols = blocks[:rows_in], blocks[rows_in:]
    rest = list(refs[rows_in + cols_in :])
    noise = [rest.pop(0) for _ in range(noise_in)]
    sums = {name: rest.pop(0)[...] for name in known}
    ready_rows, ready_cols = {}, {}
    for row, col, kind in pairs:
        if row not in ready_rows:
            wide = rows[row][0:shard, :].astype(jnp.float32)
            ready_rows[row] = jnp.sum(wide * wide, axis=1, keepdims=True)
        if col not in ready_cols:
            block = cols[col][0:shard, :]
            ready_cols[col] = block * jnp.asarray(-2.0, block.dtype), lane_squares(block)
        scaled, col_squares = ready_cols[col]
        row_block, row_probes = rows[row][0:shard, :], rows[row][pl.ds(shard, vectors), :]
        cross = lax.dot_general(row_block, scaled, ROWS_BY_ROWS, preferred_element_type=jnp.float32)
        kernel = matern((ready_rows[row] + col_squares) + cross)
        found = {}
        if "back" in kind:
            found["back", col] = jnp.dot(row_probes, kernel, preferred_element_type=jnp.float32)
        if "rows" in kind:
            col_probes = cols[col][pl.ds(shard, vectors), :]
            found["rows", row] = lax.dot_general(col_probes, kernel, ROWS_BY_ROWS, preferred_element_type=jnp.float32)
        for name, value in found.items():
            sums[name] = sums[name] + value if name in sums else value
    for place in range(noise_in):
        probes = cols[place][pl.ds(shard, vectors), :].astype(jnp.float32)
        sums["back", place] = sums["back", place] + noise[place][...] * probes
    for ref, name in zip(rest, sorted(sums)):
        ref[...] = sums[name]


def tile(rows, cols, order, pairs, sums, shard, vectors, noise=()):
    blocks = [*rows, *cols]
    args = [*[blocks[place] for place in order], *noise, *sums.values()]
    elements = len(pairs) * shard * shard
    width = rows[0].shape[1]
    names = sorted({(part, col if part == "back" else row) for row, col, kind in pairs for part in kind} | set(sums))
    whole = pl.BlockSpec(memory_space=pltpu.VMEM)
    found = pl.pallas_call(
        functools.partial(
            tile_kernel, list(order), tuple(pairs), tuple(sums), (len(rows), len(cols), len(noise)), shard, vectors
        ),
        out_shape=[jax.ShapeDtypeStruct((vectors, shard), jnp.float32)] * len(names),
        in_specs=[whole] * len(args),
        out_specs=[whole] * len(names),
        compiler_params=pltpu.CompilerParams(vmem_limit_bytes=32 * 1024 * 1024),
        cost_estimate=pl.CostEstimate(
            flops=2 * elements * (width + 2 * vectors),
            bytes_accessed=2 * width * shard * len(blocks),
            transcendentals=2 * elements,
        ),
    )(*args)
    return dict(zip(names, found))


def on_device(features, probes, noise_level):
    count = lax.axis_size("blk")
    inner = group_size(count)
    outer = count // inner
    shard = features.shape[0]
    vectors = probes.shape[1]
    packed = jnp.concatenate([features, probes.T], axis=0)

    def along_outer(value, edges):
        return lax.ppermute(value, "blk", [(s * inner + b, t * inner + b) for s, t in edges for b in range(inner)])

    def in_plane(value, hops):
        return lax.ppermute(value, "blk", [(a * inner + s, a * inner + t) for a in range(outer) for s, t in hops])

    def near(step):
        return [(plane_target(b, step, inner), b) for b in range(inner)]

    one_way, exchanges = outer_maps(outer)
    cols = [along_outer(packed, edges) for edges in one_way]
    others = [along_outer(packed, edges) for edges in exchanges]
    blocks = plane_blocks(packed, inner, in_plane)
    direct = [step for step in range(1, inner) if step & (step - 1) == 0]
    passed = [step for step in range(1, inner) if step & (step - 1)]

    order = [0] + passed + [inner + place for place in range(len(cols))] + direct
    pairs = [(row, col, ("rows", "back")) for col in range(len(cols)) for row in range(inner)]
    sums = tile(blocks, cols, order, pairs, {}, shard, vectors)
    backs = [sums.pop(("back", place)) for place in range(len(cols))]
    pairs = [(row, col, ("rows",)) for col in range(len(others)) for row in range(inner)]
    sums = tile(blocks, others, range(inner + len(others)), pairs, sums, shard, vectors)
    pairs = [(row, 0, ("back",)) for row in range(inner)]
    own = tile(blocks, [packed], range(inner + 1), pairs, {}, shard, vectors, noise=[noise_level[None, :]])

    total = [own["back", 0]]
    total += [in_plane(sums["rows", step], [(t, s) for s, t in near(step)]) for step in range(1, inner)]
    total += [sums["rows", 0]]
    total += [along_outer(back, [(t, s) for s, t in edges]) for back, edges in zip(backs, one_way)]
    return functools.reduce(lambda sofar, term: sofar + term, total).T


def solution(mesh):
    placed = (P(("parts", "blk"), None), P(("parts", "blk"), None), P(("parts", "blk")))
    return jax.shard_map(
        on_device, mesh=mesh, in_specs=placed, out_specs=P(("parts", "blk"), None), check_vma=False
    )
```

```python
import functools
import math

import jax
import jax.numpy as jnp
from jax import lax
from jax.experimental import pallas as pl
from jax.experimental.pallas import tpu as pltpu
from jax.sharding import PartitionSpec as P

ROOT5 = math.sqrt(5.0)
DECAY = -ROOT5 * math.log2(math.e)
ROWS_BY_ROWS = (((1,), (1,)), ((), ()))


def group_size(count):
    size = 1
    while size * size < count or count % size:
        size += 1
    return size


def plane_blocks(value, count, send):
    if count & (count - 1):
        maps = {step: [(b, (b - step) % count) for b in range(count)] for step in range(1, count)}
        return [value] + [send(value, maps[step]) for step in range(1, count)]
    blocks = {0: value}
    bit = count // 2
    while bit:
        for known in list(blocks):
            blocks[known | bit] = send(blocks[known], [(b, b ^ bit) for b in range(count)])
        bit //= 2
    return [blocks[distance] for distance in range(count)]


def plane_target(index, step, count):
    return (index + step) % count if count & (count - 1) else index ^ step


def outer_maps(count):
    bits = count.bit_length() - 1
    order = list(range(count))
    if count == 1 << bits:
        order = [int(f"{a:0{bits}b}"[::-1], 2) if bits else a for a in reversed(order)]
    shifts = [[(order[p], order[(p + step) % count]) for p in range(count)] for step in range(1, count // 2 + 1)]
    if count % 2:
        return shifts, []
    return shifts[:-1], shifts[-1:]


def matern(dist2):
    dist2 = jnp.maximum(dist2, 1e-30)
    dist = dist2 * lax.rsqrt(dist2)
    poly = (1.0 + ROOT5 * dist) + (5.0 / 3.0) * dist2
    return (poly * jnp.exp2(DECAY * dist)).astype(jnp.bfloat16)


def lane_squares(block):
    wide = block.astype(jnp.float32)
    square = wide * wide
    high = square.astype(jnp.bfloat16)
    low = (square - high.astype(jnp.float32)).astype(jnp.bfloat16)
    ones = jnp.ones((8, block.shape[1]), jnp.bfloat16)
    total = lax.dot_general(ones, high, ROWS_BY_ROWS, preferred_element_type=jnp.float32)
    total += lax.dot_general(ones, low, ROWS_BY_ROWS, preferred_element_type=jnp.float32)
    return total[0:1, :]


def tile_kernel(shape, order, kinds, sums, shard, *refs):
    refs = list(refs)
    rows_in, cols_in = shape
    terms_in, backs_in, noise_in = sums
    blocks = [refs.pop(0) for _ in range(rows_in + cols_in)]
    rows, cols = [blocks[place] for place in order[:rows_in]], [blocks[place] for place in order[rows_in:]]
    old_terms, old_backs, noise = refs[:terms_in], refs[terms_in : terms_in + backs_in], refs[terms_in + backs_in :][:noise_in]
    del refs[: terms_in + backs_in + noise_in]
    returning = sum("back" in kind for kind in kinds)
    new_backs, new_terms = refs[:returning], refs[returning:]
    terms = [ref[...] for ref in old_terms] or [None] * rows_in
    row_squares = []
    for row in rows:
        wide = row[0:shard, :].astype(jnp.float32)
        row_squares.append(jnp.sum(wide * wide, axis=1, keepdims=True))
    filled = 0
    for kind, col_ref in zip(kinds, cols):
        col = col_ref[0:shard, :]
        col_squares = lane_squares(col)
        scaled = col * jnp.asarray(-2.0, col.dtype)
        back = old_backs[filled][...] if old_backs and "back" in kind else None
        if noise and "back" in kind:
            back = noise[0][...] * col_ref[shard:, :].astype(jnp.float32)
        for slot, row in enumerate(rows):
            cross = lax.dot_general(row[0:shard, :], scaled, ROWS_BY_ROWS, preferred_element_type=jnp.float32)
            kernel = matern((row_squares[slot] + col_squares) + cross)
            if "back" in kind:
                share = jnp.dot(row[shard:, :], kernel, preferred_element_type=jnp.float32)
                back = share if back is None else back + share
            if "rows" in kind:
                term = lax.dot_general(col_ref[shard:, :], kernel, ROWS_BY_ROWS, preferred_element_type=jnp.float32)
                terms[slot] = term if terms[slot] is None else terms[slot] + term
        if "back" in kind:
            new_backs[filled][...] = back
            filled += 1
    for ref, term in zip(new_terms, terms):
        ref[...] = term


def tile(rows, cols, order, kinds, shard, terms=(), backs=(), noise=()):
    width, vectors = rows[0].shape[1], rows[0].shape[0] - shard
    blocks = [*rows, *cols]
    args = [*[blocks[place] for place in order], *terms, *backs, *noise]
    elements = len(rows) * len(cols) * shard * shard
    whole = pl.BlockSpec(memory_space=pltpu.VMEM)
    returning = sum("back" in kind for kind in kinds)
    spread = len(rows) if any("rows" in kind for kind in kinds) else 0
    outs = [jax.ShapeDtypeStruct((vectors, shard), jnp.float32)] * (returning + spread)
    found = pl.pallas_call(
        functools.partial(
            tile_kernel,
            (len(rows), len(cols)),
            [list(order).index(place) for place in range(len(blocks))],
            tuple(kinds),
            (len(terms), len(backs), len(noise)),
            shard,
        ),
        out_shape=outs,
        in_specs=[whole] * len(args),
        out_specs=[whole] * len(outs),
        compiler_params=pltpu.CompilerParams(vmem_limit_bytes=32 * 1024 * 1024),
        cost_estimate=pl.CostEstimate(
            flops=2 * elements * (width + 2 * vectors),
            bytes_accessed=2 * width * shard * (len(rows) + len(cols)),
            transcendentals=2 * elements,
        ),
    )(*args)
    return found[:returning], found[returning:]


def on_device(features, probes, noise_level):
    count = lax.axis_size("blk")
    inner = group_size(count)
    outer = count // inner
    shard = features.shape[0]
    packed = jnp.concatenate([features, probes.T], axis=0)

    def along_outer(value, edges):
        return lax.ppermute(value, "blk", [(s * inner + b, t * inner + b) for s, t in edges for b in range(inner)])

    def in_plane(value, hops):
        return lax.ppermute(value, "blk", [(a * inner + s, a * inner + t) for a in range(outer) for s, t in hops])

    def near(step):
        return [(plane_target(b, step, inner), b) for b in range(inner)]

    one_way, exchanges = outer_maps(outer)
    cols = [along_outer(packed, edges) for edges in one_way + exchanges]
    kinds = [("rows", "back")] * len(one_way) + [("rows",)] * len(exchanges)
    blocks = plane_blocks(packed, inner, in_plane)

    direct = [step for step in range(1, inner) if step & (step - 1) == 0]
    passed = [step for step in range(1, inner) if step & (step - 1)]
    first = [inner + place for place in range(len(one_way))]
    last = [inner + place for place in range(len(one_way), len(cols))]
    order = [0] + passed + last + direct[:1] + first + direct[1:]
    backs, terms = tile(blocks, cols, order, kinds, shard)
    sums = [along_outer(back, [(t, s) for s, t in edges]) for back, edges in zip(backs, one_way)]
    sums += [in_plane(terms[step], [(t, s) for s, t in near(step)]) for step in range(inner - 1, 0, -1)]
    (own,), _ = tile(blocks, [packed], range(inner + 1), [("back",)], shard, noise=[noise_level[None, :]])
    return functools.reduce(lambda total, term: total + term, sums + list(terms[:1]) + [own]).T


def solution(mesh):
    placed = (P(("parts", "blk"), None), P(("parts", "blk"), None), P(("parts", "blk")))
    return jax.shard_map(
        on_device, mesh=mesh, in_specs=placed, out_specs=P(("parts", "blk"), None), check_vma=False
    )
```

```python
import functools
import math

import jax
import jax.numpy as jnp
from jax import lax
from jax.experimental import pallas as pl
from jax.experimental.pallas import tpu as pltpu
from jax.sharding import PartitionSpec as P

ROOT5 = math.sqrt(5.0)
DECAY = -ROOT5 * math.log2(math.e)
ROWS_BY_ROWS = (((1,), (1,)), ((), ()))


def group_size(count):
    size = 1
    while size * size < count or count % size:
        size += 1
    return size


def plane_blocks(value, count, send):
    if count & (count - 1):
        maps = {step: [(b, (b - step) % count) for b in range(count)] for step in range(1, count)}
        return [value] + [send(value, maps[step]) for step in range(1, count)]
    blocks = {0: value}
    bit = count // 2
    while bit:
        for known in list(blocks):
            blocks[known | bit] = send(blocks[known], [(b, b ^ bit) for b in range(count)])
        bit //= 2
    return [blocks[distance] for distance in range(count)]


def plane_target(index, step, count):
    return (index + step) % count if count & (count - 1) else index ^ step


def outer_maps(count):
    bits = count.bit_length() - 1
    order = list(range(count))
    if count == 1 << bits:
        order = [int(f"{a:0{bits}b}"[::-1], 2) if bits else a for a in order]
    shifts = [[(order[p], order[(p + step) % count]) for p in range(count)] for step in range(1, count // 2 + 1)]
    if count % 2:
        return shifts, []
    return shifts[:-1], shifts[-1:]


def matern(dist2):
    dist2 = jnp.maximum(dist2, 1e-30)
    dist = dist2 * lax.rsqrt(dist2)
    poly = (1.0 + ROOT5 * dist) + (5.0 / 3.0) * dist2
    return (poly * jnp.exp2(DECAY * dist)).astype(jnp.bfloat16)


def lane_squares(block):
    wide = block.astype(jnp.float32)
    square = wide * wide
    high = square.astype(jnp.bfloat16)
    low = (square - high.astype(jnp.float32)).astype(jnp.bfloat16)
    ones = jnp.ones((8, block.shape[1]), jnp.bfloat16)
    total = lax.dot_general(ones, high, ROWS_BY_ROWS, preferred_element_type=jnp.float32)
    total += lax.dot_general(ones, low, ROWS_BY_ROWS, preferred_element_type=jnp.float32)
    return total[0:1, :]


def tile_kernel(order, pairs, known, counts, shard, vectors, *refs):
    rows_in, cols_in, noise_in = counts
    blocks = [refs[order.index(place)] for place in range(rows_in + cols_in)]
    rows, cols = blocks[:rows_in], blocks[rows_in:]
    rest = list(refs[rows_in + cols_in :])
    noise = [rest.pop(0) for _ in range(noise_in)]
    sums = {name: rest.pop(0)[...] for name in known}
    ready_rows, ready_cols = {}, {}
    for row, col, kind in pairs:
        if row not in ready_rows:
            wide = rows[row][0:shard, :].astype(jnp.float32)
            ready_rows[row] = jnp.sum(wide * wide, axis=1, keepdims=True)
        if col not in ready_cols:
            block = cols[col][0:shard, :]
            ready_cols[col] = block * jnp.asarray(-2.0, block.dtype), lane_squares(block)
        scaled, col_squares = ready_cols[col]
        row_block, row_probes = rows[row][0:shard, :], rows[row][pl.ds(shard, vectors), :]
        cross = lax.dot_general(row_block, scaled, ROWS_BY_ROWS, preferred_element_type=jnp.float32)
        kernel = matern((ready_rows[row] + col_squares) + cross)
        found = {}
        if "back" in kind:
            found["back", col] = jnp.dot(row_probes, kernel, preferred_element_type=jnp.float32)
        if "rows" in kind:
            col_probes = cols[col][pl.ds(shard, vectors), :]
            found["rows", row] = lax.dot_general(col_probes, kernel, ROWS_BY_ROWS, preferred_element_type=jnp.float32)
        for name, value in found.items():
            sums[name] = sums[name] + value if name in sums else value
    for place in range(noise_in):
        probes = cols[place][pl.ds(shard, vectors), :].astype(jnp.float32)
        sums["back", place] = sums["back", place] + noise[place][...] * probes
    for ref, name in zip(rest, sorted(sums)):
        ref[...] = sums[name]


def tile(rows, cols, order, pairs, sums, shard, vectors, noise=()):
    blocks = [*rows, *cols]
    args = [*[blocks[place] for place in order], *noise, *sums.values()]
    elements = len(pairs) * shard * shard
    width = rows[0].shape[1]
    names = sorted({(part, col if part == "back" else row) for row, col, kind in pairs for part in kind} | set(sums))
    whole = pl.BlockSpec(memory_space=pltpu.VMEM)
    found = pl.pallas_call(
        functools.partial(
            tile_kernel, list(order), tuple(pairs), tuple(sums), (len(rows), len(cols), len(noise)), shard, vectors
        ),
        out_shape=[jax.ShapeDtypeStruct((vectors, shard), jnp.float32)] * len(names),
        in_specs=[whole] * len(args),
        out_specs=[whole] * len(names),
        compiler_params=pltpu.CompilerParams(vmem_limit_bytes=32 * 1024 * 1024),
        cost_estimate=pl.CostEstimate(
            flops=2 * elements * (width + 2 * vectors),
            bytes_accessed=2 * width * shard * len(blocks),
            transcendentals=2 * elements,
        ),
    )(*args)
    return dict(zip(names, found))


def on_device(features, probes, noise_level):
    count = lax.axis_size("blk")
    inner = group_size(count)
    outer = count // inner
    shard = features.shape[0]
    vectors = probes.shape[1]
    packed = jnp.concatenate([features, probes.T], axis=0)

    def along_outer(value, edges):
        return lax.ppermute(value, "blk", [(s * inner + b, t * inner + b) for s, t in edges for b in range(inner)])

    def in_plane(value, hops):
        return lax.ppermute(value, "blk", [(a * inner + s, a * inner + t) for a in range(outer) for s, t in hops])

    def near(step):
        return [(plane_target(b, step, inner), b) for b in range(inner)]

    one_way, exchanges = outer_maps(outer)
    cols = [along_outer(packed, edges) for edges in one_way + exchanges]
    kinds = [("rows", "back")] * len(one_way) + [("rows",)] * len(exchanges)
    blocks = plane_blocks(packed, inner, in_plane)
    direct = [step for step in range(inner) if step & (step - 1) == 0]
    passed = [step for step in range(inner) if step & (step - 1)]

    early = [(row, col, kinds[col]) for col in range(len(one_way)) for row in range(len(direct))]
    order = [0, 1] + list(range(len(direct), len(direct) + len(one_way))) + list(range(2, len(direct)))
    sums = tile([blocks[step] for step in direct], cols[: len(one_way)], order, early, {}, shard, vectors)
    sums = {(part, direct[place] if part == "rows" else place): value for (part, place), value in sums.items()}
    late = [(row, col, kinds[col]) for col in range(len(cols)) for row in range(inner) if col >= len(one_way) or row in passed]
    sums = tile(blocks, cols, range(inner + len(cols)), late, sums, shard, vectors)

    total = [along_outer(sums["back", place], [(t, s) for s, t in edges]) for place, edges in enumerate(one_way)]
    total += [in_plane(sums["rows", step], [(t, s) for s, t in near(step)]) for step in range(inner - 1, 0, -1)]
    own = [(row, 0, ("back",)) for row in range(inner)]
    own = tile(blocks, [packed], range(inner + 1), own, {}, shard, vectors, noise=[noise_level[None, :]])
    return functools.reduce(lambda total, term: total + term, total + [sums["rows", 0], own["back", 0]]).T


def solution(mesh):
    placed = (P(("parts", "blk"), None), P(("parts", "blk"), None), P(("parts", "blk")))
    return jax.shard_map(
        on_device, mesh=mesh, in_specs=placed, out_specs=P(("parts", "blk"), None), check_vma=False
    )
```

```python
import functools
import math

import jax
import jax.numpy as jnp
from jax import lax
from jax.experimental import pallas as pl
from jax.experimental.pallas import tpu as pltpu
from jax.sharding import PartitionSpec as P

ROOT5 = math.sqrt(5.0)
DECAY = -ROOT5 * math.log2(math.e)
ROWS_BY_ROWS = (((1,), (1,)), ((), ()))


def group_size(count):
    size = 1
    while size * size < count or count % size:
        size += 1
    return size


def plane_blocks(value, count, send):
    if count & (count - 1):
        maps = {step: [(b, (b - step) % count) for b in range(count)] for step in range(1, count)}
        return [value] + [send(value, maps[step]) for step in range(1, count)]
    blocks = {0: value}
    bit = count // 2
    while bit:
        for known in list(blocks):
            blocks[known | bit] = send(blocks[known], [(b, b ^ bit) for b in range(count)])
        bit //= 2
    return [blocks[distance] for distance in range(count)]


def plane_target(index, step, count):
    return (index + step) % count if count & (count - 1) else index ^ step


def outer_maps(count):
    bits = count.bit_length() - 1
    order = list(range(count))
    if count == 1 << bits:
        order = [int(f"{a:0{bits}b}"[::-1], 2) if bits else a for a in order]
    shifts = [[(order[p], order[(p + step) % count]) for p in range(count)] for step in range(1, count // 2 + 1)]
    if count % 2:
        return shifts, []
    return shifts[:-1], shifts[-1:]


def matern(dist2):
    dist2 = jnp.maximum(dist2, 1e-30)
    dist = dist2 * lax.rsqrt(dist2)
    poly = (1.0 + ROOT5 * dist) + (5.0 / 3.0) * dist2
    return (poly * jnp.exp2(DECAY * dist)).astype(jnp.bfloat16)


def lane_squares(block):
    wide = block.astype(jnp.float32)
    square = wide * wide
    high = square.astype(jnp.bfloat16)
    low = (square - high.astype(jnp.float32)).astype(jnp.bfloat16)
    ones = jnp.ones((8, block.shape[1]), jnp.bfloat16)
    total = lax.dot_general(ones, high, ROWS_BY_ROWS, preferred_element_type=jnp.float32)
    total += lax.dot_general(ones, low, ROWS_BY_ROWS, preferred_element_type=jnp.float32)
    return total[0:1, :]


def tile_kernel(shape, order, kinds, sums, shard, *refs):
    refs = list(refs)
    rows_in, cols_in = shape
    terms_in, backs_in, noise_in = sums
    blocks = [refs.pop(0) for _ in range(rows_in + cols_in)]
    rows, cols = [blocks[place] for place in order[:rows_in]], [blocks[place] for place in order[rows_in:]]
    old_terms, old_backs, noise = refs[:terms_in], refs[terms_in : terms_in + backs_in], refs[terms_in + backs_in :][:noise_in]
    del refs[: terms_in + backs_in + noise_in]
    returning = sum("back" in kind for kind in kinds)
    new_backs, new_terms = refs[:returning], refs[returning:]
    terms = [ref[...] for ref in old_terms] or [None] * rows_in
    row_squares = []
    for row in rows:
        wide = row[0:shard, :].astype(jnp.float32)
        row_squares.append(jnp.sum(wide * wide, axis=1, keepdims=True))
    filled = 0
    for kind, col_ref in zip(kinds, cols):
        col = col_ref[0:shard, :]
        col_squares = lane_squares(col)
        scaled = col * jnp.asarray(-2.0, col.dtype)
        back = old_backs[filled][...] if old_backs and "back" in kind else None
        if noise and "back" in kind:
            back = noise[0][...] * col_ref[shard:, :].astype(jnp.float32)
        for slot, row in enumerate(rows):
            cross = lax.dot_general(row[0:shard, :], scaled, ROWS_BY_ROWS, preferred_element_type=jnp.float32)
            kernel = matern((row_squares[slot] + col_squares) + cross)
            if "back" in kind:
                share = jnp.dot(row[shard:, :], kernel, preferred_element_type=jnp.float32)
                back = share if back is None else back + share
            if "rows" in kind:
                term = lax.dot_general(col_ref[shard:, :], kernel, ROWS_BY_ROWS, preferred_element_type=jnp.float32)
                terms[slot] = term if terms[slot] is None else terms[slot] + term
        if "back" in kind:
            new_backs[filled][...] = back
            filled += 1
    for ref, term in zip(new_terms, terms):
        ref[...] = term


def tile(rows, cols, order, kinds, shard, terms=(), backs=(), noise=()):
    width, vectors = rows[0].shape[1], rows[0].shape[0] - shard
    blocks = [*rows, *cols]
    args = [*[blocks[place] for place in order], *terms, *backs, *noise]
    elements = len(rows) * len(cols) * shard * shard
    whole = pl.BlockSpec(memory_space=pltpu.VMEM)
    returning = sum("back" in kind for kind in kinds)
    spread = len(rows) if any("rows" in kind for kind in kinds) else 0
    outs = [jax.ShapeDtypeStruct((vectors, shard), jnp.float32)] * (returning + spread)
    found = pl.pallas_call(
        functools.partial(
            tile_kernel,
            (len(rows), len(cols)),
            [list(order).index(place) for place in range(len(blocks))],
            tuple(kinds),
            (len(terms), len(backs), len(noise)),
            shard,
        ),
        out_shape=outs,
        in_specs=[whole] * len(args),
        out_specs=[whole] * len(outs),
        compiler_params=pltpu.CompilerParams(vmem_limit_bytes=32 * 1024 * 1024),
        cost_estimate=pl.CostEstimate(
            flops=2 * elements * (width + 2 * vectors),
            bytes_accessed=2 * width * shard * (len(rows) + len(cols)),
            transcendentals=2 * elements,
        ),
    )(*args)
    return found[:returning], found[returning:]


def on_device(features, probes, noise_level):
    count = lax.axis_size("blk")
    inner = group_size(count)
    outer = count // inner
    shard = features.shape[0]
    packed = jnp.concatenate([features, probes.T], axis=0)

    def along_outer(value, edges):
        return lax.ppermute(value, "blk", [(s * inner + b, t * inner + b) for s, t in edges for b in range(inner)])

    def in_plane(value, hops):
        return lax.ppermute(value, "blk", [(a * inner + s, a * inner + t) for a in range(outer) for s, t in hops])

    def near(step):
        return [(plane_target(b, step, inner), b) for b in range(inner)]

    one_way, exchanges = outer_maps(outer)
    cols = [along_outer(packed, edges) for edges in one_way + exchanges]
    kinds = [("rows", "back")] * len(one_way) + [("rows",)] * len(exchanges)
    blocks = plane_blocks(packed, inner, in_plane)

    direct = [step for step in range(1, inner) if step & (step - 1) == 0]
    passed = [step for step in range(1, inner) if step & (step - 1)]
    first = [inner + place for place in range(len(one_way))]
    last = [inner + place for place in range(len(one_way), len(cols))]
    order = [0] + passed + last + direct[:1] + first + direct[1:]
    backs, terms = tile(blocks, cols, order, kinds, shard)
    (own,), _ = tile(blocks, [packed], range(inner + 1), [("back",)], shard, noise=[noise_level[None, :]])
    sums = [in_plane(terms[step], [(t, s) for s, t in near(step)]) for step in range(inner - 1, 0, -1)]
    sums += [along_outer(back, [(t, s) for s, t in edges]) for back, edges in zip(backs, one_way)]
    return functools.reduce(lambda total, term: total + term, sums + list(terms[:1]) + [own]).T


def solution(mesh):
    placed = (P(("parts", "blk"), None), P(("parts", "blk"), None), P(("parts", "blk")))
    return jax.shard_map(
        on_device, mesh=mesh, in_specs=placed, out_specs=P(("parts", "blk"), None), check_vma=False
    )
```

```python
import functools
import math

import jax
import jax.numpy as jnp
from jax import lax
from jax.experimental import pallas as pl
from jax.experimental.pallas import tpu as pltpu
from jax.sharding import PartitionSpec as P

ROOT5 = math.sqrt(5.0)
DECAY = -ROOT5 * math.log2(math.e)
ROWS_BY_ROWS = (((1,), (1,)), ((), ()))


def group_size(count):
    size = 1
    while size * size < count or count % size:
        size += 1
    return size


def plane_blocks(value, count, send):
    if count & (count - 1):
        maps = {step: [(b, (b - step) % count) for b in range(count)] for step in range(1, count)}
        return [value] + [send(value, maps[step]) for step in range(1, count)]
    blocks = {0: value}
    bit = count // 2
    while bit:
        for known in list(blocks):
            blocks[known | bit] = send(blocks[known], [(b, b ^ bit) for b in range(count)])
        bit //= 2
    return [blocks[distance] for distance in range(count)]


def plane_target(index, step, count):
    return (index + step) % count if count & (count - 1) else index ^ step


def outer_maps(count):
    bits = count.bit_length() - 1
    order = list(range(count))
    if count == 1 << bits:
        order = [int(f"{a:0{bits}b}"[::-1], 2) if bits else a for a in reversed(order)]
    shifts = [[(order[p], order[(p + step) % count]) for p in range(count)] for step in range(1, count // 2 + 1)]
    if count % 2:
        return shifts, []
    return shifts[:-1], shifts[-1:]


def matern(dist2):
    dist2 = jnp.maximum(dist2, 1e-30)
    dist = dist2 * lax.rsqrt(dist2)
    poly = (1.0 + ROOT5 * dist) + (5.0 / 3.0) * dist2
    return (poly * jnp.exp2(DECAY * dist)).astype(jnp.bfloat16)


def lane_squares(block):
    wide = block.astype(jnp.float32)
    square = wide * wide
    high = square.astype(jnp.bfloat16)
    low = (square - high.astype(jnp.float32)).astype(jnp.bfloat16)
    ones = jnp.ones((8, block.shape[1]), jnp.bfloat16)
    total = lax.dot_general(ones, high, ROWS_BY_ROWS, preferred_element_type=jnp.float32)
    total += lax.dot_general(ones, low, ROWS_BY_ROWS, preferred_element_type=jnp.float32)
    return total[0:1, :]


def tile_kernel(order, pairs, known, counts, shard, vectors, *refs):
    rows_in, cols_in, noise_in = counts
    blocks = [refs[order.index(place)] for place in range(rows_in + cols_in)]
    rows, cols = blocks[:rows_in], blocks[rows_in:]
    rest = list(refs[rows_in + cols_in :])
    noise = [rest.pop(0) for _ in range(noise_in)]
    sums = {name: rest.pop(0)[...] for name in known}
    ready_rows, ready_cols = {}, {}
    for row, col, kind in pairs:
        if row not in ready_rows:
            wide = rows[row][0:shard, :].astype(jnp.float32)
            ready_rows[row] = jnp.sum(wide * wide, axis=1, keepdims=True)
        if col not in ready_cols:
            block = cols[col][0:shard, :]
            ready_cols[col] = block * jnp.asarray(-2.0, block.dtype), lane_squares(block)
        scaled, col_squares = ready_cols[col]
        row_block, row_probes = rows[row][0:shard, :], rows[row][pl.ds(shard, vectors), :]
        cross = lax.dot_general(row_block, scaled, ROWS_BY_ROWS, preferred_element_type=jnp.float32)
        kernel = matern((ready_rows[row] + col_squares) + cross)
        found = {}
        if "back" in kind:
            found["back", col] = jnp.dot(row_probes, kernel, preferred_element_type=jnp.float32)
        if "rows" in kind:
            col_probes = cols[col][pl.ds(shard, vectors), :]
            found["rows", row] = lax.dot_general(col_probes, kernel, ROWS_BY_ROWS, preferred_element_type=jnp.float32)
        for name, value in found.items():
            sums[name] = sums[name] + value if name in sums else value
    for place in range(noise_in):
        probes = cols[place][pl.ds(shard, vectors), :].astype(jnp.float32)
        sums["back", place] = sums["back", place] + noise[place][...] * probes
    for ref, name in zip(rest, sorted(sums)):
        ref[...] = sums[name]


def tile(rows, cols, order, pairs, sums, shard, vectors, noise=(), work=1.0):
    blocks = [*rows, *cols]
    args = [*[blocks[place] for place in order], *noise, *sums.values()]
    elements = len(pairs) * shard * shard
    width = rows[0].shape[1]
    names = sorted({(part, col if part == "back" else row) for row, col, kind in pairs for part in kind} | set(sums))
    whole = pl.BlockSpec(memory_space=pltpu.VMEM)
    found = pl.pallas_call(
        functools.partial(
            tile_kernel, list(order), tuple(pairs), tuple(sums), (len(rows), len(cols), len(noise)), shard, vectors
        ),
        out_shape=[jax.ShapeDtypeStruct((vectors, shard), jnp.float32)] * len(names),
        in_specs=[whole] * len(args),
        out_specs=[whole] * len(names),
        compiler_params=pltpu.CompilerParams(vmem_limit_bytes=32 * 1024 * 1024),
        cost_estimate=pl.CostEstimate(
            flops=int(work * 2 * elements * (width + 2 * vectors)),
            bytes_accessed=int(work * 2 * width * shard * len(blocks)),
            transcendentals=int(work * 2 * elements),
        ),
    )(*args)
    return dict(zip(names, found))


def copy_kernel(from_ref, to_ref):
    to_ref[0 : from_ref.shape[0], :] = from_ref[...]
    to_ref[from_ref.shape[0] :, :] = jnp.zeros((to_ref.shape[0] - from_ref.shape[0], to_ref.shape[1]), to_ref.dtype)


def copy_rows(value, rows):
    whole = pl.BlockSpec(memory_space=pltpu.VMEM)
    return pl.pallas_call(
        copy_kernel,
        out_shape=jax.ShapeDtypeStruct((rows, value.shape[1]), value.dtype),
        in_specs=[whole],
        out_specs=whole,
        compiler_params=pltpu.CompilerParams(vmem_limit_bytes=32 * 1024 * 1024),
    )(value)


def on_device(features, probes, noise_level):
    count = lax.axis_size("blk")
    inner = group_size(count)
    outer = count // inner
    shard = features.shape[0]
    vectors = probes.shape[1]
    packed = jnp.concatenate([features, probes.T], axis=0)

    def along_outer(value, edges):
        return lax.ppermute(value, "blk", [(s * inner + b, t * inner + b) for s, t in edges for b in range(inner)])

    def in_plane(value, hops):
        return lax.ppermute(value, "blk", [(a * inner + s, a * inner + t) for a in range(outer) for s, t in hops])

    def near(step):
        return [(plane_target(b, step, inner), b) for b in range(inner)]

    one_way, exchanges = outer_maps(outer)
    longer = copy_rows(packed, shard + vectors + 16)
    cols = [along_outer(longer, edges) for edges in one_way]
    others = [along_outer(longer, edges) for edges in exchanges]
    blocks = plane_blocks(packed, inner, in_plane)
    direct = [step for step in range(1, inner) if step & (step - 1) == 0]
    passed = [step for step in range(1, inner) if step & (step - 1)]

    order = [0] + passed + [inner + place for place in range(len(cols))] + direct
    pairs = [(row, col, ("rows", "back")) for col in range(len(cols)) for row in range(inner)]
    sums = tile(blocks, cols, order, pairs, {}, shard, vectors, work=0.0)
    backs = [sums.pop(("back", place)) for place in range(len(cols))]
    pairs = [(row, col, ("rows",)) for col in range(len(others)) for row in range(inner)]
    sums = tile(blocks, others, range(inner + len(others)), pairs, sums, shard, vectors)
    pairs = [(row, 0, ("back",)) for row in range(inner)]
    own = tile(blocks, [packed], range(inner + 1), pairs, {}, shard, vectors, noise=[noise_level[None, :]])

    total = [own["back", 0]]
    total += [in_plane(sums["rows", step], [(t, s) for s, t in near(step)]) for step in range(1, inner)]
    total += [along_outer(back, [(t, s) for s, t in edges]) for back, edges in zip(backs, one_way)]
    return functools.reduce(lambda sofar, term: sofar + term, total + [sums["rows", 0]]).T


def solution(mesh):
    placed = (P(("parts", "blk"), None), P(("parts", "blk"), None), P(("parts", "blk")))
    return jax.shard_map(
        on_device, mesh=mesh, in_specs=placed, out_specs=P(("parts", "blk"), None), check_vma=False
    )
```

```python
import functools
import math

import jax
import jax.numpy as jnp
from jax import lax
from jax.experimental import pallas as pl
from jax.experimental.pallas import tpu as pltpu
from jax.sharding import PartitionSpec as P

ROOT5 = math.sqrt(5.0)
DECAY = -ROOT5 * math.log2(math.e)
ROWS_BY_ROWS = (((1,), (1,)), ((), ()))


def group_size(count):
    size = 1
    while size * size < count or count % size:
        size += 1
    return size


def plane_blocks(value, count, send):
    if count & (count - 1):
        maps = {step: [(b, (b - step) % count) for b in range(count)] for step in range(1, count)}
        return [value] + [send(value, maps[step]) for step in range(1, count)]
    blocks = {0: value}
    bit = count // 2
    while bit:
        for known in list(blocks):
            blocks[known | bit] = send(blocks[known], [(b, b ^ bit) for b in range(count)])
        bit //= 2
    return [blocks[distance] for distance in range(count)]


def plane_target(index, step, count):
    return (index + step) % count if count & (count - 1) else index ^ step


def outer_maps(count):
    bits = count.bit_length() - 1
    order = list(range(count))
    if count == 1 << bits:
        order = [int(f"{a:0{bits}b}"[::-1], 2) if bits else a for a in reversed(order)]
    shifts = [[(order[p], order[(p + step) % count]) for p in range(count)] for step in range(1, count // 2 + 1)]
    if count % 2:
        return shifts, []
    return shifts[:-1], shifts[-1:]


def matern(dist2):
    dist2 = jnp.maximum(dist2, 1e-30)
    dist = dist2 * lax.rsqrt(dist2)
    poly = (1.0 + ROOT5 * dist) + (5.0 / 3.0) * dist2
    return (poly * jnp.exp2(DECAY * dist)).astype(jnp.bfloat16)


def lane_squares(block):
    wide = block.astype(jnp.float32)
    square = wide * wide
    high = square.astype(jnp.bfloat16)
    low = (square - high.astype(jnp.float32)).astype(jnp.bfloat16)
    ones = jnp.ones((8, block.shape[1]), jnp.bfloat16)
    total = lax.dot_general(ones, high, ROWS_BY_ROWS, preferred_element_type=jnp.float32)
    total += lax.dot_general(ones, low, ROWS_BY_ROWS, preferred_element_type=jnp.float32)
    return total[0:1, :]


def tile_kernel(order, pairs, known, counts, shard, vectors, *refs):
    rows_in, cols_in, noise_in = counts
    blocks = [refs[order.index(place)] for place in range(rows_in + cols_in)]
    rows, cols = blocks[:rows_in], blocks[rows_in:]
    rest = list(refs[rows_in + cols_in :])
    noise = [rest.pop(0) for _ in range(noise_in)]
    sums = {name: rest.pop(0)[...] for name in known}
    ready_rows, ready_cols = {}, {}
    for row, col, kind in pairs:
        if row not in ready_rows:
            wide = rows[row][0:shard, :].astype(jnp.float32)
            ready_rows[row] = jnp.sum(wide * wide, axis=1, keepdims=True)
        if col not in ready_cols:
            block = cols[col][0:shard, :]
            ready_cols[col] = block * jnp.asarray(-2.0, block.dtype), lane_squares(block)
        scaled, col_squares = ready_cols[col]
        row_block, row_probes = rows[row][0:shard, :], rows[row][pl.ds(shard, vectors), :]
        cross = lax.dot_general(row_block, scaled, ROWS_BY_ROWS, preferred_element_type=jnp.float32)
        kernel = matern((ready_rows[row] + col_squares) + cross)
        found = {}
        if "back" in kind:
            found["back", col] = jnp.dot(row_probes, kernel, preferred_element_type=jnp.float32)
        if "rows" in kind:
            col_probes = cols[col][pl.ds(shard, vectors), :]
            found["rows", row] = lax.dot_general(col_probes, kernel, ROWS_BY_ROWS, preferred_element_type=jnp.float32)
        for name, value in found.items():
            sums[name] = sums[name] + value if name in sums else value
    for place in range(noise_in):
        probes = cols[place][pl.ds(shard, vectors), :].astype(jnp.float32)
        sums["back", place] = sums["back", place] + noise[place][...] * probes
    for ref, name in zip(rest, sorted(sums)):
        ref[...] = sums[name].astype(ref.dtype)


def tile(rows, cols, order, pairs, sums, shard, vectors, noise=(), work=1.0, sent=()):
    blocks = [*rows, *cols]
    args = [*[blocks[place] for place in order], *noise, *sums.values()]
    elements = len(pairs) * shard * shard
    width = rows[0].shape[1]
    names = sorted({(part, col if part == "back" else row) for row, col, kind in pairs for part in kind} | set(sums))
    whole = pl.BlockSpec(memory_space=pltpu.VMEM)
    found = pl.pallas_call(
        functools.partial(
            tile_kernel, list(order), tuple(pairs), tuple(sums), (len(rows), len(cols), len(noise)), shard, vectors
        ),
        out_shape=[
            jax.ShapeDtypeStruct((vectors, shard), jnp.bfloat16 if name in sent else jnp.float32) for name in names
        ],
        in_specs=[whole] * len(args),
        out_specs=[whole] * len(names),
        compiler_params=pltpu.CompilerParams(vmem_limit_bytes=32 * 1024 * 1024),
        cost_estimate=pl.CostEstimate(
            flops=int(work * 2 * elements * (width + 2 * vectors)),
            bytes_accessed=int(work * 2 * width * shard * len(blocks)),
            transcendentals=int(work * 2 * elements),
        ),
    )(*args)
    return dict(zip(names, found))


def copy_kernel(from_ref, to_ref):
    to_ref[0 : from_ref.shape[0], :] = from_ref[...]
    to_ref[from_ref.shape[0] :, :] = jnp.zeros((to_ref.shape[0] - from_ref.shape[0], to_ref.shape[1]), to_ref.dtype)


def copy_rows(value, rows):
    whole = pl.BlockSpec(memory_space=pltpu.VMEM)
    return pl.pallas_call(
        copy_kernel,
        out_shape=jax.ShapeDtypeStruct((rows, value.shape[1]), value.dtype),
        in_specs=[whole],
        out_specs=whole,
        compiler_params=pltpu.CompilerParams(vmem_limit_bytes=32 * 1024 * 1024),
    )(value)


def on_device(features, probes, noise_level):
    count = lax.axis_size("blk")
    inner = group_size(count)
    outer = count // inner
    shard = features.shape[0]
    vectors = probes.shape[1]
    packed = jnp.concatenate([features, probes.T], axis=0)

    def along_outer(value, edges):
        return lax.ppermute(value, "blk", [(s * inner + b, t * inner + b) for s, t in edges for b in range(inner)])

    def in_plane(value, hops):
        return lax.ppermute(value, "blk", [(a * inner + s, a * inner + t) for a in range(outer) for s, t in hops])

    def near(step):
        return [(plane_target(b, step, inner), b) for b in range(inner)]

    one_way, exchanges = outer_maps(outer)
    longer = copy_rows(packed, shard + vectors + 16)
    cols = [along_outer(longer, edges) for edges in one_way]
    others = [along_outer(longer, edges) for edges in exchanges]
    blocks = plane_blocks(packed, inner, in_plane)
    direct = [step for step in range(1, inner) if step & (step - 1) == 0]
    passed = [step for step in range(1, inner) if step & (step - 1)]

    order = [0] + passed + [inner + place for place in range(len(cols))] + direct
    pairs = [(row, col, ("rows", "back")) for col in range(len(cols)) for row in range(inner)]
    returns = [("back", place) for place in range(len(cols))]
    sums = tile(blocks, cols, order, pairs, {}, shard, vectors, work=0.0, sent=returns)
    backs = [sums.pop(name) for name in returns]
    pairs = [(row, col, ("rows",)) for col in range(len(others)) for row in range(inner)]
    shares = [("rows", step) for step in range(1, inner)]
    sums = tile(blocks, others, range(inner + len(others)), pairs, sums, shard, vectors, sent=shares)
    pairs = [(row, 0, ("back",)) for row in range(inner)]
    own = tile(blocks, [packed], range(inner + 1), pairs, {}, shard, vectors, noise=[noise_level[None, :]])

    total = [own["back", 0]]
    total += [in_plane(sums["rows", step], [(t, s) for s, t in near(step)]) for step in range(1, inner)]
    total += [along_outer(back, [(t, s) for s, t in edges]) for back, edges in zip(backs, one_way)]
    return functools.reduce(lambda sofar, term: sofar + term, total + [sums["rows", 0]]).T


def solution(mesh):
    placed = (P(("parts", "blk"), None), P(("parts", "blk"), None), P(("parts", "blk")))
    return jax.shard_map(
        on_device, mesh=mesh, in_specs=placed, out_specs=P(("parts", "blk"), None), check_vma=False
    )
```

```python
import functools
import math

import jax
import jax.numpy as jnp
from jax import lax
from jax.experimental import pallas as pl
from jax.experimental.pallas import tpu as pltpu
from jax.sharding import PartitionSpec as P

ROOT5 = math.sqrt(5.0)
DECAY = -ROOT5 * math.log2(math.e)
ROWS_BY_ROWS = (((1,), (1,)), ((), ()))


def group_size(count):
    size = 1
    while size * size < count or count % size:
        size += 1
    return size


def plane_blocks(value, count, send):
    if count & (count - 1):
        maps = {step: [(b, (b - step) % count) for b in range(count)] for step in range(1, count)}
        return [value] + [send(value, maps[step]) for step in range(1, count)]
    blocks = {0: value}
    bit = count // 2
    while bit:
        for known in list(blocks):
            blocks[known | bit] = send(blocks[known], [(b, b ^ bit) for b in range(count)])
        bit //= 2
    return [blocks[distance] for distance in range(count)]


def plane_target(index, step, count):
    return (index + step) % count if count & (count - 1) else index ^ step


def outer_maps(count):
    bits = count.bit_length() - 1
    order = list(range(count))
    if count == 1 << bits:
        order = [int(f"{a:0{bits}b}"[::-1], 2) if bits else a for a in reversed(order)]
    shifts = [[(order[p], order[(p + step) % count]) for p in range(count)] for step in range(1, count // 2 + 1)]
    if count % 2:
        return shifts, []
    return shifts[:-1], shifts[-1:]


def matern(dist2):
    dist2 = jnp.maximum(dist2, 1e-30)
    dist = dist2 * lax.rsqrt(dist2)
    poly = (1.0 + ROOT5 * dist) + (5.0 / 3.0) * dist2
    return (poly * jnp.exp2(DECAY * dist)).astype(jnp.bfloat16)


def lane_squares(block):
    wide = block.astype(jnp.float32)
    square = wide * wide
    high = square.astype(jnp.bfloat16)
    low = (square - high.astype(jnp.float32)).astype(jnp.bfloat16)
    ones = jnp.ones((8, block.shape[1]), jnp.bfloat16)
    total = lax.dot_general(ones, high, ROWS_BY_ROWS, preferred_element_type=jnp.float32)
    total += lax.dot_general(ones, low, ROWS_BY_ROWS, preferred_element_type=jnp.float32)
    return total[0:1, :]


def tile_kernel(order, pairs, known, counts, shard, vectors, *refs):
    rows_in, cols_in, noise_in = counts
    blocks = [refs[order.index(place)] for place in range(rows_in + cols_in)]
    rows, cols = blocks[:rows_in], blocks[rows_in:]
    rest = list(refs[rows_in + cols_in :])
    noise = [rest.pop(0) for _ in range(noise_in)]
    sums = {name: rest.pop(0)[...] for name in known}
    ready_rows, ready_cols = {}, {}
    for row, col, kind in pairs:
        if row not in ready_rows:
            wide = rows[row][0:shard, :].astype(jnp.float32)
            ready_rows[row] = jnp.sum(wide * wide, axis=1, keepdims=True)
        if col not in ready_cols:
            block = cols[col][0:shard, :]
            ready_cols[col] = block * jnp.asarray(-2.0, block.dtype), lane_squares(block)
        scaled, col_squares = ready_cols[col]
        row_block, row_probes = rows[row][0:shard, :], rows[row][pl.ds(shard, vectors), :]
        cross = lax.dot_general(row_block, scaled, ROWS_BY_ROWS, preferred_element_type=jnp.float32)
        kernel = matern((ready_rows[row] + col_squares) + cross)
        found = {}
        if "back" in kind:
            found["back", col] = jnp.dot(row_probes, kernel, preferred_element_type=jnp.float32)
        if "rows" in kind:
            col_probes = cols[col][pl.ds(shard, vectors), :]
            found["rows", row] = lax.dot_general(col_probes, kernel, ROWS_BY_ROWS, preferred_element_type=jnp.float32)
        for name, value in found.items():
            sums[name] = sums[name] + value if name in sums else value
    for place in range(noise_in):
        probes = cols[place][pl.ds(shard, vectors), :].astype(jnp.float32)
        sums["back", place] = sums["back", place] + noise[place][...] * probes
    for ref, name in zip(rest, sorted(sums)):
        ref[...] = sums[name].astype(ref.dtype)


def tile(rows, cols, order, pairs, sums, shard, vectors, noise=(), work=1.0, sent=()):
    blocks = [*rows, *cols]
    args = [*[blocks[place] for place in order], *noise, *sums.values()]
    elements = len(pairs) * shard * shard
    width = rows[0].shape[1]
    names = sorted({(part, col if part == "back" else row) for row, col, kind in pairs for part in kind} | set(sums))
    whole = pl.BlockSpec(memory_space=pltpu.VMEM)
    found = pl.pallas_call(
        functools.partial(
            tile_kernel, list(order), tuple(pairs), tuple(sums), (len(rows), len(cols), len(noise)), shard, vectors
        ),
        out_shape=[
            jax.ShapeDtypeStruct((vectors, shard), jnp.bfloat16 if name in sent else jnp.float32) for name in names
        ],
        in_specs=[whole] * len(args),
        out_specs=[whole] * len(names),
        compiler_params=pltpu.CompilerParams(vmem_limit_bytes=32 * 1024 * 1024),
        cost_estimate=pl.CostEstimate(
            flops=int(work * 2 * elements * (width + 2 * vectors)),
            bytes_accessed=int(work * 2 * width * shard * len(blocks)),
            transcendentals=int(work * 2 * elements),
        ),
    )(*args)
    return dict(zip(names, found))


def copy_kernel(from_ref, to_ref):
    to_ref[0 : from_ref.shape[0], :] = from_ref[...]
    to_ref[from_ref.shape[0] :, :] = jnp.zeros((to_ref.shape[0] - from_ref.shape[0], to_ref.shape[1]), to_ref.dtype)


def copy_rows(value, rows):
    whole = pl.BlockSpec(memory_space=pltpu.VMEM)
    return pl.pallas_call(
        copy_kernel,
        out_shape=jax.ShapeDtypeStruct((rows, value.shape[1]), value.dtype),
        in_specs=[whole],
        out_specs=whole,
        compiler_params=pltpu.CompilerParams(vmem_limit_bytes=32 * 1024 * 1024),
    )(value)


def on_device(features, probes, noise_level):
    count = lax.axis_size("blk")
    inner = group_size(count)
    outer = count // inner
    shard = features.shape[0]
    vectors = probes.shape[1]
    packed = jnp.concatenate([features, probes.T], axis=0)

    def along_outer(value, edges):
        return lax.ppermute(value, "blk", [(s * inner + b, t * inner + b) for s, t in edges for b in range(inner)])

    def in_plane(value, hops):
        return lax.ppermute(value, "blk", [(a * inner + s, a * inner + t) for a in range(outer) for s, t in hops])

    def near(step):
        return [(plane_target(b, step, inner), b) for b in range(inner)]

    one_way, exchanges = outer_maps(outer)
    longer = copy_rows(packed, shard + vectors + 16)
    cols = [along_outer(longer, edges) for edges in one_way]
    others = [along_outer(longer, edges) for edges in exchanges]
    blocks = plane_blocks(packed, inner, in_plane)
    direct = [step for step in range(1, inner) if step & (step - 1) == 0]
    passed = [step for step in range(1, inner) if step & (step - 1)]

    order = [0] + passed + [inner + place for place in range(len(cols))] + direct
    pairs = [(row, col, ("rows", "back")) for col in range(len(cols)) for row in range(inner)]
    returns = [("back", place) for place in range(len(cols))]
    sums = tile(blocks, cols, order, pairs, {}, shard, vectors, work=0.0)
    backs = [sums.pop(name) for name in returns]
    pairs = [(row, col, ("rows",)) for col in range(len(others)) for row in range(inner)]
    shares = [("rows", step) for step in range(1, inner)]
    sums = tile(blocks, others, range(inner + len(others)), pairs, sums, shard, vectors, sent=shares)
    pairs = [(row, 0, ("back",)) for row in range(inner)]
    own = tile(blocks, [packed], range(inner + 1), pairs, {}, shard, vectors, noise=[noise_level[None, :]])

    total = [own["back", 0]]
    total += [in_plane(sums["rows", step], [(t, s) for s, t in near(step)]) for step in range(1, inner)]
    total += [along_outer(back, [(t, s) for s, t in edges]) for back, edges in zip(backs, one_way)]
    return functools.reduce(lambda sofar, term: sofar + term, total + [sums["rows", 0]]).T


def solution(mesh):
    placed = (P(("parts", "blk"), None), P(("parts", "blk"), None), P(("parts", "blk")))
    return jax.shard_map(
        on_device, mesh=mesh, in_specs=placed, out_specs=P(("parts", "blk"), None), check_vma=False
    )
```

```python
import functools
import math

import jax
import jax.numpy as jnp
from jax import lax
from jax.experimental import pallas as pl
from jax.experimental.pallas import tpu as pltpu
from jax.sharding import PartitionSpec as P

ROOT5 = math.sqrt(5.0)
DECAY = -ROOT5 * math.log2(math.e)
ROWS_BY_ROWS = (((1,), (1,)), ((), ()))


def group_size(count):
    size = 1
    while size * size < count or count % size:
        size += 1
    return size


def plane_blocks(value, halves, count, send):
    if count & (count - 1):
        maps = {step: [(b, (b - step) % count) for b in range(count)] for step in range(1, count)}
        return [(value,)] + [(send(value, maps[step]),) for step in range(1, count)]
    blocks = {0: (value,)}
    bit = count // 2
    while bit:
        hops = [(b, b ^ bit) for b in range(count)]
        for known in list(blocks):
            parts = halves if known == 0 and bit == count // 2 and bit > 1 else blocks[known]
            blocks[known | bit] = tuple(send(part, hops) for part in parts)
        bit //= 2
    return [blocks[distance] for distance in range(count)]


def plane_target(index, step, count):
    return (index + step) % count if count & (count - 1) else index ^ step


def outer_maps(count):
    bits = count.bit_length() - 1
    order = list(range(count))
    if count == 1 << bits:
        order = [int(f"{a:0{bits}b}"[::-1], 2) if bits else a for a in reversed(order)]
    shifts = [[(order[p], order[(p + step) % count]) for p in range(count)] for step in range(1, count // 2 + 1)]
    if count % 2:
        return shifts, []
    return shifts[:-1], shifts[-1:]


def matern(dist2):
    dist2 = jnp.maximum(dist2, 1e-30)
    dist = dist2 * lax.rsqrt(dist2)
    poly = (1.0 + ROOT5 * dist) + (5.0 / 3.0) * dist2
    return (poly * jnp.exp2(DECAY * dist)).astype(jnp.bfloat16)


def lane_squares(block):
    wide = block.astype(jnp.float32)
    square = wide * wide
    high = square.astype(jnp.bfloat16)
    low = (square - high.astype(jnp.float32)).astype(jnp.bfloat16)
    ones = jnp.ones((8, block.shape[1]), jnp.bfloat16)
    total = lax.dot_general(ones, high, ROWS_BY_ROWS, preferred_element_type=jnp.float32)
    total += lax.dot_general(ones, low, ROWS_BY_ROWS, preferred_element_type=jnp.float32)
    return total[0:1, :]


def joined(refs, shard, vectors):
    points, some = shard // len(refs), vectors // len(refs)
    features = [ref[0:points, :] for ref in refs]
    probes = [ref[pl.ds(points, some), :] for ref in refs]
    return (jnp.concatenate(features), jnp.concatenate(probes)) if len(refs) > 1 else (features[0], probes[0])


def tile_kernel(order, pairs, known, counts, shard, vectors, *refs):
    parts, cols_in, noise_in = counts
    rest = list(refs)
    blocks = {place: [rest.pop(0) for _ in range((*parts, *[1] * cols_in)[place])] for place in order}
    rows = [joined(blocks[place], shard, vectors) for place in range(len(parts))]
    cols = [blocks[len(parts) + place][0] for place in range(cols_in)]
    noise = [rest.pop(0) for _ in range(noise_in)]
    sums = {name: rest.pop(0)[...] for name in known}
    ready_rows, ready_cols = {}, {}
    for row, col, kind in pairs:
        if row not in ready_rows:
            wide = rows[row][0].astype(jnp.float32)
            ready_rows[row] = jnp.sum(wide * wide, axis=1, keepdims=True)
        if col not in ready_cols:
            block = cols[col][0:shard, :]
            ready_cols[col] = block * jnp.asarray(-2.0, block.dtype), lane_squares(block)
        scaled, col_squares = ready_cols[col]
        row_block, row_probes = rows[row]
        cross = lax.dot_general(row_block, scaled, ROWS_BY_ROWS, preferred_element_type=jnp.float32)
        kernel = matern((ready_rows[row] + col_squares) + cross)
        found = {}
        if "back" in kind:
            found["back", col] = jnp.dot(row_probes, kernel, preferred_element_type=jnp.float32)
        if "rows" in kind:
            col_probes = cols[col][pl.ds(shard, vectors), :]
            found["rows", row] = lax.dot_general(col_probes, kernel, ROWS_BY_ROWS, preferred_element_type=jnp.float32)
        for name, value in found.items():
            sums[name] = sums[name] + value if name in sums else value
    for place in range(noise_in):
        probes = cols[place][pl.ds(shard, vectors), :].astype(jnp.float32)
        sums["back", place] = sums["back", place] + noise[place][...] * probes
    for ref, name in zip(rest, sorted(sums)):
        ref[...] = sums[name]


def tile(rows, cols, order, pairs, sums, shard, vectors, noise=(), work=1.0):
    blocks = [*rows, *[(col,) for col in cols]]
    args = [*[part for place in order for part in blocks[place]], *noise, *sums.values()]
    elements = len(pairs) * shard * shard
    width = cols[0].shape[1]
    names = sorted({(part, col if part == "back" else row) for row, col, kind in pairs for part in kind} | set(sums))
    whole = pl.BlockSpec(memory_space=pltpu.VMEM)
    found = pl.pallas_call(
        functools.partial(
            tile_kernel, list(order), tuple(pairs), tuple(sums), (tuple(map(len, rows)), len(cols), len(noise)), shard, vectors
        ),
        out_shape=[jax.ShapeDtypeStruct((vectors, shard), jnp.float32)] * len(names),
        in_specs=[whole] * len(args),
        out_specs=[whole] * len(names),
        compiler_params=pltpu.CompilerParams(vmem_limit_bytes=32 * 1024 * 1024),
        cost_estimate=pl.CostEstimate(
            flops=int(work * 2 * elements * (width + 2 * vectors)),
            bytes_accessed=int(work * 2 * width * shard * len(blocks)),
            transcendentals=int(work * 2 * elements),
        ),
    )(*args)
    return dict(zip(names, found))


def split_kernel(shard, vectors, longer_ref, whole_ref, *halves):
    whole_ref[...] = longer_ref[0 : shard + vectors, :]
    points, some = shard // 2, vectors // 2
    for place, half in enumerate(halves):
        half[0:points, :] = longer_ref[pl.ds(place * points, points), :]
        half[points:, :] = longer_ref[pl.ds(shard + place * some, some), :]


def split(longer, shard, vectors):
    whole = pl.BlockSpec(memory_space=pltpu.VMEM)
    rows = [shard + vectors, (shard + vectors) // 2, (shard + vectors) // 2]
    return pl.pallas_call(
        functools.partial(split_kernel, shard, vectors),
        out_shape=[jax.ShapeDtypeStruct((count, longer.shape[1]), longer.dtype) for count in rows],
        in_specs=[whole],
        out_specs=[whole] * 3,
        compiler_params=pltpu.CompilerParams(vmem_limit_bytes=32 * 1024 * 1024),
    )(longer)


def on_device(features, probes, noise_level):
    count = lax.axis_size("blk")
    inner = group_size(count)
    outer = count // inner
    shard = features.shape[0]
    vectors = probes.shape[1]
    spare = jnp.zeros((16, features.shape[1]), features.dtype)
    longer = jnp.concatenate([features, probes.T, spare], axis=0)
    packed, *halves = split(longer, shard, vectors)

    def along_outer(value, edges):
        return lax.ppermute(value, "blk", [(s * inner + b, t * inner + b) for s, t in edges for b in range(inner)])

    def in_plane(value, hops):
        return lax.ppermute(value, "blk", [(a * inner + s, a * inner + t) for a in range(outer) for s, t in hops])

    def near(step):
        return [(plane_target(b, step, inner), b) for b in range(inner)]

    one_way, exchanges = outer_maps(outer)
    cols = [along_outer(longer, edges) for edges in one_way]
    others = [along_outer(packed, edges) for edges in exchanges]
    blocks = plane_blocks(packed, halves, inner, in_plane)
    direct = [step for step in range(1, inner) if step & (step - 1) == 0]
    passed = [step for step in range(1, inner) if step & (step - 1)]

    order = [0] + passed + direct + [inner + place for place in range(len(cols))]
    pairs = [(row, col, ("rows", "back")) for col in range(len(cols)) for row in range(inner)]
    sums = tile(blocks, cols, order, pairs, {}, shard, vectors, work=0.0)
    backs = [sums.pop(("back", place)) for place in range(len(cols))]
    pairs = [(row, col, ("rows",)) for col in range(len(others)) for row in range(inner)]
    sums = tile(blocks, others, range(inner + len(others)), pairs, sums, shard, vectors)
    pairs = [(row, 0, ("back",)) for row in range(inner)]
    own = tile(blocks, [packed], range(inner + 1), pairs, {}, shard, vectors, noise=[noise_level[None, :]])

    total = [sums["rows", 0], own["back", 0]]
    total += [in_plane(sums["rows", step], [(t, s) for s, t in near(step)]) for step in range(1, inner)]
    total += [along_outer(back, [(t, s) for s, t in edges]) for back, edges in zip(backs, one_way)]
    return functools.reduce(lambda sofar, term: sofar + term, total).T


def solution(mesh):
    placed = (P(("parts", "blk"), None), P(("parts", "blk"), None), P(("parts", "blk")))
    return jax.shard_map(
        on_device, mesh=mesh, in_specs=placed, out_specs=P(("parts", "blk"), None), check_vma=False
    )
```

```python
import functools
import math

import jax
import jax.numpy as jnp
from jax import lax
from jax.experimental import pallas as pl
from jax.experimental.pallas import tpu as pltpu
from jax.sharding import PartitionSpec as P

ROOT5 = math.sqrt(5.0)
DECAY = -ROOT5 * math.log2(math.e)
ROWS_BY_ROWS = (((1,), (1,)), ((), ()))


def group_size(count):
    size = 1
    while size * size < count or count % size:
        size += 1
    return size


def plane_blocks(value, count, send):
    if count & (count - 1):
        maps = {step: [(b, (b - step) % count) for b in range(count)] for step in range(1, count)}
        return [value] + [send(value, maps[step]) for step in range(1, count)]
    blocks = {0: value}
    bit = count // 2
    while bit:
        for known in list(blocks):
            blocks[known | bit] = send(blocks[known], [(b, b ^ bit) for b in range(count)])
        bit //= 2
    return [blocks[distance] for distance in range(count)]


def plane_target(index, step, count):
    return (index + step) % count if count & (count - 1) else index ^ step


def outer_maps(count):
    bits = count.bit_length() - 1
    order = list(range(count))
    if count == 1 << bits:
        order = [int(f"{a:0{bits}b}"[::-1], 2) if bits else a for a in reversed(order)]
    shifts = [[(order[p], order[(p + step) % count]) for p in range(count)] for step in range(1, count // 2 + 1)]
    if count % 2:
        return shifts, []
    return shifts[:-1], shifts[-1:]


def matern(dist2):
    dist2 = jnp.maximum(dist2, 1e-30)
    dist = dist2 * lax.rsqrt(dist2)
    poly = (1.0 + ROOT5 * dist) + (5.0 / 3.0) * dist2
    return (poly * jnp.exp2(DECAY * dist)).astype(jnp.bfloat16)


def lane_squares(block):
    wide = block.astype(jnp.float32)
    square = wide * wide
    high = square.astype(jnp.bfloat16)
    low = (square - high.astype(jnp.float32)).astype(jnp.bfloat16)
    ones = jnp.ones((8, block.shape[1]), jnp.bfloat16)
    total = lax.dot_general(ones, high, ROWS_BY_ROWS, preferred_element_type=jnp.float32)
    total += lax.dot_general(ones, low, ROWS_BY_ROWS, preferred_element_type=jnp.float32)
    return total[0:1, :]


def tile_kernel(order, pairs, known, counts, shard, vectors, *refs):
    rows_in, cols_in, noise_in = counts
    blocks = [refs[order.index(place)] for place in range(rows_in + cols_in)]
    rows, cols = blocks[:rows_in], blocks[rows_in:]
    rest = list(refs[rows_in + cols_in :])
    noise = [rest.pop(0) for _ in range(noise_in)]
    sums = {name: rest.pop(0)[...] for name in known}
    squares = {}
    for col in sorted({col for _, col, _ in pairs}):
        kind = next(kind for _, place, kind in pairs if place == col)
        members = [row for row, place, _ in pairs if place == col]
        for row in members:
            if row not in squares:
                wide = rows[row][0:shard, :].astype(jnp.float32)
                squares[row] = jnp.sum(wide * wide, axis=1, keepdims=True)
        block = cols[col][0:shard, :]
        scaled, col_squares = block * jnp.asarray(-2.0, block.dtype), lane_squares(block)
        joined = jnp.concatenate([rows[row][0:shard, :] for row in members])
        cross = lax.dot_general(joined, scaled, ROWS_BY_ROWS, preferred_element_type=jnp.float32)
        kernel = matern((jnp.concatenate([squares[row] for row in members]) + col_squares) + cross)
        found = {}
        if "back" in kind:
            probes = jnp.concatenate([rows[row][pl.ds(shard, vectors), :] for row in members], axis=1)
            found["back", col] = jnp.dot(probes, kernel, preferred_element_type=jnp.float32)
        if "rows" in kind:
            col_probes = cols[col][pl.ds(shard, vectors), :]
            terms = lax.dot_general(col_probes, kernel, ROWS_BY_ROWS, preferred_element_type=jnp.float32)
            for place, row in enumerate(members):
                found["rows", row] = terms[:, place * shard : (place + 1) * shard]
        for name, value in found.items():
            sums[name] = sums[name] + value if name in sums else value
    for place in range(noise_in):
        probes = cols[place][pl.ds(shard, vectors), :].astype(jnp.float32)
        sums["back", place] = sums["back", place] + noise[place][...] * probes
    for ref, name in zip(rest, sorted(sums)):
        ref[...] = sums[name]


def tile(rows, cols, order, pairs, sums, shard, vectors, noise=(), work=1.0):
    blocks = [*rows, *cols]
    args = [*[blocks[place] for place in order], *noise, *sums.values()]
    elements = len(pairs) * shard * shard
    width = rows[0].shape[1]
    names = sorted({(part, col if part == "back" else row) for row, col, kind in pairs for part in kind} | set(sums))
    whole = pl.BlockSpec(memory_space=pltpu.VMEM)
    found = pl.pallas_call(
        functools.partial(
            tile_kernel, list(order), tuple(pairs), tuple(sums), (len(rows), len(cols), len(noise)), shard, vectors
        ),
        out_shape=[jax.ShapeDtypeStruct((vectors, shard), jnp.float32)] * len(names),
        in_specs=[whole] * len(args),
        out_specs=[whole] * len(names),
        compiler_params=pltpu.CompilerParams(vmem_limit_bytes=32 * 1024 * 1024),
        cost_estimate=pl.CostEstimate(
            flops=int(work * 2 * elements * (width + 2 * vectors)),
            bytes_accessed=int(work * 2 * width * shard * len(blocks)),
            transcendentals=int(work * 2 * elements),
        ),
    )(*args)
    return dict(zip(names, found))


def copy_kernel(from_ref, to_ref):
    to_ref[0 : from_ref.shape[0], :] = from_ref[...]
    to_ref[from_ref.shape[0] :, :] = jnp.zeros((to_ref.shape[0] - from_ref.shape[0], to_ref.shape[1]), to_ref.dtype)


def copy_rows(value, rows):
    whole = pl.BlockSpec(memory_space=pltpu.VMEM)
    return pl.pallas_call(
        copy_kernel,
        out_shape=jax.ShapeDtypeStruct((rows, value.shape[1]), value.dtype),
        in_specs=[whole],
        out_specs=whole,
        compiler_params=pltpu.CompilerParams(vmem_limit_bytes=32 * 1024 * 1024),
    )(value)


def on_device(features, probes, noise_level):
    count = lax.axis_size("blk")
    inner = group_size(count)
    outer = count // inner
    shard = features.shape[0]
    vectors = probes.shape[1]
    packed = jnp.concatenate([features, probes.T], axis=0)

    def along_outer(value, edges):
        return lax.ppermute(value, "blk", [(s * inner + b, t * inner + b) for s, t in edges for b in range(inner)])

    def in_plane(value, hops):
        return lax.ppermute(value, "blk", [(a * inner + s, a * inner + t) for a in range(outer) for s, t in hops])

    def near(step):
        return [(plane_target(b, step, inner), b) for b in range(inner)]

    one_way, exchanges = outer_maps(outer)
    longer = copy_rows(packed, shard + vectors + 16)
    cols = [along_outer(longer, edges) for edges in one_way]
    others = [along_outer(longer, edges) for edges in exchanges]
    blocks = plane_blocks(packed, inner, in_plane)
    direct = [step for step in range(1, inner) if step & (step - 1) == 0]
    passed = [step for step in range(1, inner) if step & (step - 1)]

    order = [0] + passed + [inner + place for place in range(len(cols))] + direct
    pairs = [(row, col, ("rows", "back")) for col in range(len(cols)) for row in range(inner)]
    sums = tile(blocks, cols, order, pairs, {}, shard, vectors, work=0.0)
    backs = [sums.pop(("back", place)) for place in range(len(cols))]
    pairs = [(row, col, ("rows",)) for col in range(len(others)) for row in range(inner)]
    sums = tile(blocks, others, range(inner + len(others)), pairs, sums, shard, vectors)
    pairs = [(row, 0, ("back",)) for row in range(inner)]
    own = tile(blocks, [packed], range(inner + 1), pairs, {}, shard, vectors, noise=[noise_level[None, :]])

    total = [own["back", 0]]
    total += [in_plane(sums["rows", step], [(t, s) for s, t in near(step)]) for step in range(1, inner)]
    total += [along_outer(back, [(t, s) for s, t in edges]) for back, edges in zip(backs, one_way)]
    return functools.reduce(lambda sofar, term: sofar + term, total + [sums["rows", 0]]).T


def solution(mesh):
    placed = (P(("parts", "blk"), None), P(("parts", "blk"), None), P(("parts", "blk")))
    return jax.shard_map(
        on_device, mesh=mesh, in_specs=placed, out_specs=P(("parts", "blk"), None), check_vma=False
    )
```

```python
import functools
import math

import jax
import jax.numpy as jnp
from jax import lax
from jax.experimental import pallas as pl
from jax.experimental.pallas import tpu as pltpu
from jax.sharding import PartitionSpec as P

ROOT5 = math.sqrt(5.0)
DECAY = -ROOT5 * math.log2(math.e)
ROWS_BY_ROWS = (((1,), (1,)), ((), ()))


def group_size(count):
    size = 1
    while size * size < count or count % size:
        size += 1
    return size


def plane_blocks(value, count, send, cut):
    if count & (count - 1):
        maps = {step: [(b, (b - step) % count) for b in range(count)] for step in range(1, count)}
        return [(value,)] + [(send(value, maps[step]),) for step in range(1, count)]
    blocks = {0: (value,)}
    bit = count // 2
    while bit:
        hops = [(b, b ^ bit) for b in range(count)]
        for known in list(blocks):
            parts = blocks[known] if known == 0 or len(blocks[known]) > 1 else cut(*blocks[known])
            blocks[known | bit] = tuple(send(part, hops) for part in parts)
        bit //= 2
    return [blocks[distance] for distance in range(count)]


def plane_target(index, step, count):
    return (index + step) % count if count & (count - 1) else index ^ step


def outer_maps(count):
    bits = count.bit_length() - 1
    order = list(range(count))
    if count == 1 << bits:
        order = [int(f"{a:0{bits}b}"[::-1], 2) if bits else a for a in reversed(order)]
    shifts = [[(order[p], order[(p + step) % count]) for p in range(count)] for step in range(1, count // 2 + 1)]
    if count % 2:
        return shifts, []
    return shifts[:-1], shifts[-1:]


def matern(dist2):
    dist2 = jnp.maximum(dist2, 1e-30)
    dist = dist2 * lax.rsqrt(dist2)
    poly = (1.0 + ROOT5 * dist) + (5.0 / 3.0) * dist2
    return (poly * jnp.exp2(DECAY * dist)).astype(jnp.bfloat16)


def lane_squares(block):
    wide = block.astype(jnp.float32)
    square = wide * wide
    high = square.astype(jnp.bfloat16)
    low = (square - high.astype(jnp.float32)).astype(jnp.bfloat16)
    ones = jnp.ones((8, block.shape[1]), jnp.bfloat16)
    total = lax.dot_general(ones, high, ROWS_BY_ROWS, preferred_element_type=jnp.float32)
    total += lax.dot_general(ones, low, ROWS_BY_ROWS, preferred_element_type=jnp.float32)
    return total[0:1, :]


def joined(refs, shard, vectors):
    points, some = shard // len(refs), vectors // len(refs)
    features = [ref[0:points, :] for ref in refs]
    probes = [ref[pl.ds(points, some), :] for ref in refs]
    return (jnp.concatenate(features), jnp.concatenate(probes)) if len(refs) > 1 else (features[0], probes[0])


def tile_kernel(order, pairs, known, counts, shard, vectors, *refs):
    parts, cols_in, noise_in = counts
    rest = list(refs)
    blocks = {place: [rest.pop(0) for _ in range((*parts, *[1] * cols_in)[place])] for place in order}
    rows = [joined(blocks[place], shard, vectors) for place in range(len(parts))]
    cols = [blocks[len(parts) + place][0] for place in range(cols_in)]
    noise = [rest.pop(0) for _ in range(noise_in)]
    sums = {name: rest.pop(0)[...] for name in known}
    squares = {}
    for col in sorted({col for _, col, _ in pairs}):
        kind = next(kind for _, place, kind in pairs if place == col)
        members = [row for row, place, _ in pairs if place == col]
        for row in members:
            if row not in squares:
                wide = rows[row][0].astype(jnp.float32)
                squares[row] = jnp.sum(wide * wide, axis=1, keepdims=True)
        block = cols[col][0:shard, :]
        scaled, col_squares = block * jnp.asarray(-2.0, block.dtype), lane_squares(block)
        left = jnp.concatenate([rows[row][0] for row in members])
        cross = lax.dot_general(left, scaled, ROWS_BY_ROWS, preferred_element_type=jnp.float32)
        kernel = matern((jnp.concatenate([squares[row] for row in members]) + col_squares) + cross)
        found = {}
        if "back" in kind:
            probes = jnp.concatenate([rows[row][1] for row in members], axis=1)
            found["back", col] = jnp.dot(probes, kernel, preferred_element_type=jnp.float32)
        if "rows" in kind:
            col_probes = cols[col][pl.ds(shard, vectors), :]
            terms = lax.dot_general(col_probes, kernel, ROWS_BY_ROWS, preferred_element_type=jnp.float32)
            for place, row in enumerate(members):
                found["rows", row] = terms[:, place * shard : (place + 1) * shard]
        for name, value in found.items():
            sums[name] = sums[name] + value if name in sums else value
    for place in range(noise_in):
        probes = cols[place][pl.ds(shard, vectors), :].astype(jnp.float32)
        sums["back", place] = sums["back", place] + noise[place][...] * probes
    for ref, name in zip(rest, sorted(sums)):
        ref[...] = sums[name]


def tile(rows, cols, order, pairs, sums, shard, vectors, noise=(), work=1.0):
    blocks = [*rows, *[(col,) for col in cols]]
    args = [*[part for place in order for part in blocks[place]], *noise, *sums.values()]
    elements = len(pairs) * shard * shard
    width = cols[0].shape[1]
    names = sorted({(part, col if part == "back" else row) for row, col, kind in pairs for part in kind} | set(sums))
    whole = pl.BlockSpec(memory_space=pltpu.VMEM)
    found = pl.pallas_call(
        functools.partial(
            tile_kernel, list(order), tuple(pairs), tuple(sums), (tuple(map(len, rows)), len(cols), len(noise)), shard, vectors
        ),
        out_shape=[jax.ShapeDtypeStruct((vectors, shard), jnp.float32)] * len(names),
        in_specs=[whole] * len(args),
        out_specs=[whole] * len(names),
        compiler_params=pltpu.CompilerParams(vmem_limit_bytes=32 * 1024 * 1024),
        cost_estimate=pl.CostEstimate(
            flops=int(work * 2 * elements * (width + 2 * vectors)),
            bytes_accessed=int(work * 2 * width * shard * len(blocks)),
            transcendentals=int(work * 2 * elements),
        ),
    )(*args)
    return dict(zip(names, found))


def halve_kernel(shard, vectors, from_ref, *halves):
    points, some = shard // 2, vectors // 2
    for place, half in enumerate(halves):
        half[0:points, :] = from_ref[pl.ds(place * points, points), :]
        half[points:, :] = from_ref[pl.ds(shard + place * some, some), :]


def halve(value, shard, vectors):
    whole = pl.BlockSpec(memory_space=pltpu.VMEM)
    half = jax.ShapeDtypeStruct(((shard + vectors) // 2, value.shape[1]), value.dtype)
    return pl.pallas_call(
        functools.partial(halve_kernel, shard, vectors),
        out_shape=[half, half],
        in_specs=[whole],
        out_specs=[whole, whole],
        compiler_params=pltpu.CompilerParams(vmem_limit_bytes=32 * 1024 * 1024),
        cost_estimate=pl.CostEstimate(flops=0, bytes_accessed=0, transcendentals=0),
    )(value)


def on_device(features, probes, noise_level):
    count = lax.axis_size("blk")
    inner = group_size(count)
    outer = count // inner
    shard = features.shape[0]
    vectors = probes.shape[1]
    packed = jnp.concatenate([features, probes.T], axis=0)

    def along_outer(value, edges):
        return lax.ppermute(value, "blk", [(s * inner + b, t * inner + b) for s, t in edges for b in range(inner)])

    def in_plane(value, hops):
        return lax.ppermute(value, "blk", [(a * inner + s, a * inner + t) for a in range(outer) for s, t in hops])

    def near(step):
        return [(plane_target(b, step, inner), b) for b in range(inner)]

    one_way, exchanges = outer_maps(outer)
    cols = [along_outer(packed, edges) for edges in one_way]
    others = [along_outer(packed, edges) for edges in exchanges]
    blocks = plane_blocks(packed, inner, in_plane, lambda block: halve(block, shard, vectors))
    direct = [step for step in range(1, inner) if step & (step - 1) == 0]
    passed = [step for step in range(1, inner) if step & (step - 1)]

    order = [0] + passed + [inner + place for place in range(len(cols))] + direct
    pairs = [(row, col, ("rows", "back")) for col in range(len(cols)) for row in range(inner)]
    sums = tile(blocks, cols, order, pairs, {}, shard, vectors, work=0.0)
    backs = [sums.pop(("back", place)) for place in range(len(cols))]
    pairs = [(row, col, ("rows",)) for col in range(len(others)) for row in range(inner)]
    sums = tile(blocks, others, range(inner + len(others)), pairs, sums, shard, vectors)
    pairs = [(row, 0, ("back",)) for row in range(inner)]
    own = tile(blocks, [packed], range(inner + 1), pairs, {}, shard, vectors, noise=[noise_level[None, :]])

    total = [sums["rows", 0], own["back", 0]]
    total += [in_plane(sums["rows", step], [(t, s) for s, t in near(step)]) for step in range(1, inner)]
    total += [along_outer(back, [(t, s) for s, t in edges]) for back, edges in zip(backs, one_way)]
    return functools.reduce(lambda sofar, term: sofar + term, total).T


def solution(mesh):
    placed = (P(("parts", "blk"), None), P(("parts", "blk"), None), P(("parts", "blk")))
    return jax.shard_map(
        on_device, mesh=mesh, in_specs=placed, out_specs=P(("parts", "blk"), None), check_vma=False
    )
```

```python
import functools
import math

import jax
import jax.numpy as jnp
from jax import lax
from jax.experimental import pallas as pl
from jax.experimental.pallas import tpu as pltpu
from jax.sharding import PartitionSpec as P

ROOT5 = math.sqrt(5.0)
DECAY = -ROOT5 * math.log2(math.e)
ROWS_BY_ROWS = (((1,), (1,)), ((), ()))


def group_size(count):
    size = 1
    while size * size < count or count % size:
        size += 1
    return size


def plane_blocks(value, count, send, cut):
    if count & (count - 1):
        maps = {step: [(b, (b - step) % count) for b in range(count)] for step in range(1, count)}
        return [(value,)] + [(send(value, maps[step]),) for step in range(1, count)]
    blocks = {0: (value,)}
    bit = count // 2
    while bit:
        hops = [(b, b ^ bit) for b in range(count)]
        for known in list(blocks):
            whole = len(blocks[known]) == 1 and (known or bit < count // 2)
            parts = cut(*blocks[known]) if whole else blocks[known]
            blocks[known | bit] = tuple(send(part, hops) for part in parts)
        bit //= 2
    return [blocks[distance] for distance in range(count)]


def plane_target(index, step, count):
    return (index + step) % count if count & (count - 1) else index ^ step


def outer_maps(count):
    bits = count.bit_length() - 1
    order = list(range(count))
    if count == 1 << bits:
        order = [int(f"{a:0{bits}b}"[::-1], 2) if bits else a for a in reversed(order)]
    shifts = [[(order[p], order[(p + step) % count]) for p in range(count)] for step in range(1, count // 2 + 1)]
    if count % 2:
        return shifts, []
    return shifts[:-1], shifts[-1:]


def matern(dist2):
    dist2 = jnp.maximum(dist2, 1e-30)
    dist = dist2 * lax.rsqrt(dist2)
    poly = (1.0 + ROOT5 * dist) + (5.0 / 3.0) * dist2
    return (poly * jnp.exp2(DECAY * dist)).astype(jnp.bfloat16)


def lane_squares(block):
    wide = block.astype(jnp.float32)
    square = wide * wide
    high = square.astype(jnp.bfloat16)
    low = (square - high.astype(jnp.float32)).astype(jnp.bfloat16)
    ones = jnp.ones((8, block.shape[1]), jnp.bfloat16)
    total = lax.dot_general(ones, high, ROWS_BY_ROWS, preferred_element_type=jnp.float32)
    total += lax.dot_general(ones, low, ROWS_BY_ROWS, preferred_element_type=jnp.float32)
    return total[0:1, :]


def joined(refs, shard, vectors):
    points, some = shard // len(refs), vectors // len(refs)
    features = [ref[0:points, :] for ref in refs]
    probes = [ref[pl.ds(points, some), :] for ref in refs]
    return (jnp.concatenate(features), jnp.concatenate(probes)) if len(refs) > 1 else (features[0], probes[0])


def tile_kernel(order, pairs, known, counts, shard, vectors, *refs):
    parts, cols_in, noise_in = counts
    rest = list(refs)
    blocks = {place: [rest.pop(0) for _ in range((*parts, *[1] * cols_in)[place])] for place in order}
    rows = [joined(blocks[place], shard, vectors) for place in range(len(parts))]
    cols = [blocks[len(parts) + place][0] for place in range(cols_in)]
    noise = [rest.pop(0) for _ in range(noise_in)]
    sums = {name: rest.pop(0)[...] for name in known}
    squares = {}
    for col in sorted({col for _, col, _ in pairs}):
        kind = next(kind for _, place, kind in pairs if place == col)
        members = [row for row, place, _ in pairs if place == col]
        for row in members:
            if row not in squares:
                wide = rows[row][0].astype(jnp.float32)
                squares[row] = jnp.sum(wide * wide, axis=1, keepdims=True)
        block = cols[col][0:shard, :]
        scaled, col_squares = block * jnp.asarray(-2.0, block.dtype), lane_squares(block)
        left = jnp.concatenate([rows[row][0] for row in members])
        cross = lax.dot_general(left, scaled, ROWS_BY_ROWS, preferred_element_type=jnp.float32)
        kernel = matern((jnp.concatenate([squares[row] for row in members]) + col_squares) + cross)
        found = {}
        if "back" in kind:
            probes = jnp.concatenate([rows[row][1] for row in members], axis=1)
            found["back", col] = jnp.dot(probes, kernel, preferred_element_type=jnp.float32)
        if "rows" in kind:
            col_probes = cols[col][pl.ds(shard, vectors), :]
            terms = lax.dot_general(col_probes, kernel, ROWS_BY_ROWS, preferred_element_type=jnp.float32)
            for place, row in enumerate(members):
                found["rows", row] = terms[:, place * shard : (place + 1) * shard]
        for name, value in found.items():
            sums[name] = sums[name] + value if name in sums else value
    for place in range(noise_in):
        probes = cols[place][pl.ds(shard, vectors), :].astype(jnp.float32)
        sums["back", place] = sums["back", place] + noise[place][...] * probes
    for ref, name in zip(rest, sorted(sums)):
        ref[...] = sums[name]


def tile(rows, cols, order, pairs, sums, shard, vectors, noise=(), work=1.0):
    blocks = [*rows, *[(col,) for col in cols]]
    args = [*[part for place in order for part in blocks[place]], *noise, *sums.values()]
    elements = len(pairs) * shard * shard
    width = cols[0].shape[1]
    names = sorted({(part, col if part == "back" else row) for row, col, kind in pairs for part in kind} | set(sums))
    whole = pl.BlockSpec(memory_space=pltpu.VMEM)
    found = pl.pallas_call(
        functools.partial(
            tile_kernel, list(order), tuple(pairs), tuple(sums), (tuple(map(len, rows)), len(cols), len(noise)), shard, vectors
        ),
        out_shape=[jax.ShapeDtypeStruct((vectors, shard), jnp.float32)] * len(names),
        in_specs=[whole] * len(args),
        out_specs=[whole] * len(names),
        compiler_params=pltpu.CompilerParams(vmem_limit_bytes=32 * 1024 * 1024),
        cost_estimate=pl.CostEstimate(
            flops=int(work * 2 * elements * (width + 2 * vectors)),
            bytes_accessed=int(work * 2 * width * shard * len(blocks)),
            transcendentals=int(work * 2 * elements),
        ),
    )(*args)
    return dict(zip(names, found))


def halve_kernel(shard, vectors, from_ref, *halves):
    points, some = shard // 2, vectors // 2
    for place, half in enumerate(halves):
        half[0:points, :] = from_ref[pl.ds(place * points, points), :]
        half[points:, :] = from_ref[pl.ds(shard + place * some, some), :]


def halve(value, shard, vectors):
    whole = pl.BlockSpec(memory_space=pltpu.VMEM)
    half = jax.ShapeDtypeStruct(((shard + vectors) // 2, value.shape[1]), value.dtype)
    return pl.pallas_call(
        functools.partial(halve_kernel, shard, vectors),
        out_shape=[half, half],
        in_specs=[whole],
        out_specs=[whole, whole],
        compiler_params=pltpu.CompilerParams(vmem_limit_bytes=32 * 1024 * 1024),
        cost_estimate=pl.CostEstimate(flops=0, bytes_accessed=0, transcendentals=0),
    )(value)


def on_device(features, probes, noise_level):
    count = lax.axis_size("blk")
    inner = group_size(count)
    outer = count // inner
    shard = features.shape[0]
    vectors = probes.shape[1]
    packed = jnp.concatenate([features, probes.T], axis=0)

    def along_outer(value, edges):
        return lax.ppermute(value, "blk", [(s * inner + b, t * inner + b) for s, t in edges for b in range(inner)])

    def in_plane(value, hops):
        return lax.ppermute(value, "blk", [(a * inner + s, a * inner + t) for a in range(outer) for s, t in hops])

    def near(step):
        return [(plane_target(b, step, inner), b) for b in range(inner)]

    one_way, exchanges = outer_maps(outer)
    cols = [along_outer(packed, edges) for edges in one_way]
    others = [along_outer(packed, edges) for edges in exchanges]
    blocks = plane_blocks(packed, inner, in_plane, lambda block: halve(block, shard, vectors))
    direct = [step for step in range(1, inner) if step & (step - 1) == 0]
    passed = [step for step in range(1, inner) if step & (step - 1)]

    pairs = [(row, col, ("rows",)) for col in range(len(others)) for row in range(inner)]
    sums = tile(blocks, others, [0] + passed + direct + [inner + place for place in range(len(others))], pairs, {}, shard, vectors, work=0.0)
    pairs = [(row, col, ("rows", "back")) for col in range(len(cols)) for row in range(inner)]
    sums = tile(blocks, cols, [0] + passed + direct + [inner + place for place in range(len(cols))], pairs, sums, shard, vectors)
    backs = [sums["back", place] for place in range(len(cols))]
    pairs = [(row, 0, ("back",)) for row in range(inner)]
    own = tile(blocks, [packed], range(inner + 1), pairs, {}, shard, vectors, noise=[noise_level[None, :]])

    total = [along_outer(back, [(t, s) for s, t in edges]) for back, edges in zip(backs, one_way)]
    total += [in_plane(sums["rows", step], [(t, s) for s, t in near(step)]) for step in range(inner - 1, 0, -1)]
    return functools.reduce(lambda sofar, term: sofar + term, total + [own["back", 0], sums["rows", 0]]).T


def solution(mesh):
    placed = (P(("parts", "blk"), None), P(("parts", "blk"), None), P(("parts", "blk")))
    return jax.shard_map(
        on_device, mesh=mesh, in_specs=placed, out_specs=P(("parts", "blk"), None), check_vma=False
    )
```

```python
import functools
import math

import jax
import jax.numpy as jnp
from jax import lax
from jax.experimental import pallas as pl
from jax.experimental.pallas import tpu as pltpu
from jax.sharding import PartitionSpec as P

ROOT5 = math.sqrt(5.0)
DECAY = -ROOT5 * math.log2(math.e)
ROWS_BY_ROWS = (((1,), (1,)), ((), ()))


def group_size(count):
    size = 1
    while size * size < count or count % size:
        size += 1
    return size


def plane_blocks(value, count, send, cut):
    if count & (count - 1):
        maps = {step: [(b, (b - step) % count) for b in range(count)] for step in range(1, count)}
        return [(value,)] + [(send(value, maps[step]),) for step in range(1, count)]
    blocks = {0: (value,)}
    bit = count // 2
    while bit:
        hops = [(b, b ^ bit) for b in range(count)]
        for known in list(blocks):
            parts = blocks[known] if known == 0 or len(blocks[known]) > 1 else cut(*blocks[known])
            blocks[known | bit] = tuple(send(part, hops) for part in parts)
        bit //= 2
    return [blocks[distance] for distance in range(count)]


def plane_target(index, step, count):
    return (index + step) % count if count & (count - 1) else index ^ step


def outer_maps(count):
    bits = count.bit_length() - 1
    order = list(range(count))
    if count == 1 << bits:
        order = [int(f"{a:0{bits}b}"[::-1], 2) if bits else a for a in reversed(order)]
    shifts = [[(order[p], order[(p + step) % count]) for p in range(count)] for step in range(1, count // 2 + 1)]
    if count % 2:
        return shifts, []
    return shifts[:-1], shifts[-1:]


def matern(dist2):
    dist2 = jnp.maximum(dist2, 1e-30)
    dist = dist2 * lax.rsqrt(dist2)
    poly = (1.0 + ROOT5 * dist) + (5.0 / 3.0) * dist2
    return (poly * jnp.exp2(DECAY * dist)).astype(jnp.bfloat16)


def lane_squares(block):
    wide = block.astype(jnp.float32)
    square = wide * wide
    high = square.astype(jnp.bfloat16)
    low = (square - high.astype(jnp.float32)).astype(jnp.bfloat16)
    ones = jnp.ones((8, block.shape[1]), jnp.bfloat16)
    total = lax.dot_general(ones, high, ROWS_BY_ROWS, preferred_element_type=jnp.float32)
    total += lax.dot_general(ones, low, ROWS_BY_ROWS, preferred_element_type=jnp.float32)
    return total[0:1, :]


def joined(refs, shard, vectors):
    points, some = shard // len(refs), vectors // len(refs)
    features = [ref[0:points, :] for ref in refs]
    probes = [ref[pl.ds(points, some), :] for ref in refs]
    return (jnp.concatenate(features), jnp.concatenate(probes)) if len(refs) > 1 else (features[0], probes[0])


def tile_kernel(order, pairs, known, counts, shard, vectors, *refs):
    parts, cols_in, noise_in = counts
    rest = list(refs)
    blocks = {place: [rest.pop(0) for _ in range((*parts, *[1] * cols_in)[place])] for place in order}
    rows = [joined(blocks[place], shard, vectors) for place in range(len(parts))]
    cols = [blocks[len(parts) + place][0] for place in range(cols_in)]
    noise = [rest.pop(0) for _ in range(noise_in)]
    sums = {name: rest.pop(0)[...] for name in known}
    squares = {}
    for col in sorted({col for _, col, _ in pairs}):
        kind = next(kind for _, place, kind in pairs if place == col)
        members = [row for row, place, _ in pairs if place == col]
        for row in members:
            if row not in squares:
                wide = rows[row][0].astype(jnp.float32)
                squares[row] = jnp.sum(wide * wide, axis=1, keepdims=True)
        block = cols[col][0:shard, :]
        scaled, col_squares = block * jnp.asarray(-2.0, block.dtype), lane_squares(block)
        left = jnp.concatenate([rows[row][0] for row in members])
        cross = lax.dot_general(left, scaled, ROWS_BY_ROWS, preferred_element_type=jnp.float32)
        kernel = matern((jnp.concatenate([squares[row] for row in members]) + col_squares) + cross)
        found = {}
        if "back" in kind:
            probes = jnp.concatenate([rows[row][1] for row in members], axis=1)
            found["back", col] = jnp.dot(probes, kernel, preferred_element_type=jnp.float32)
        if "rows" in kind:
            col_probes = cols[col][pl.ds(shard, vectors), :]
            terms = lax.dot_general(col_probes, kernel, ROWS_BY_ROWS, preferred_element_type=jnp.float32)
            for place, row in enumerate(members):
                found["rows", row] = terms[:, place * shard : (place + 1) * shard]
        for name, value in found.items():
            sums[name] = sums[name] + value if name in sums else value
    for place in range(noise_in):
        probes = cols[place][pl.ds(shard, vectors), :].astype(jnp.float32)
        sums["back", place] = sums["back", place] + noise[place][...] * probes
    for ref, name in zip(rest, sorted(sums)):
        ref[...] = sums[name]


def tile(rows, cols, order, pairs, sums, shard, vectors, noise=(), work=1.0):
    blocks = [*rows, *[(col,) for col in cols]]
    args = [*[part for place in order for part in blocks[place]], *noise, *sums.values()]
    elements = len(pairs) * shard * shard
    width = cols[0].shape[1]
    names = sorted({(part, col if part == "back" else row) for row, col, kind in pairs for part in kind} | set(sums))
    whole = pl.BlockSpec(memory_space=pltpu.VMEM)
    found = pl.pallas_call(
        functools.partial(
            tile_kernel, list(order), tuple(pairs), tuple(sums), (tuple(map(len, rows)), len(cols), len(noise)), shard, vectors
        ),
        out_shape=[jax.ShapeDtypeStruct((vectors, shard), jnp.float32)] * len(names),
        in_specs=[whole] * len(args),
        out_specs=[whole] * len(names),
        compiler_params=pltpu.CompilerParams(vmem_limit_bytes=32 * 1024 * 1024),
        cost_estimate=pl.CostEstimate(
            flops=int(work * 2 * elements * (width + 2 * vectors)),
            bytes_accessed=int(work * 2 * width * shard * len(blocks)),
            transcendentals=int(work * 2 * elements),
        ),
    )(*args)
    return dict(zip(names, found))


def halve_kernel(shard, vectors, from_ref, *halves):
    points, some = shard // 2, vectors // 2
    for place, half in enumerate(halves):
        half[0:points, :] = from_ref[pl.ds(place * points, points), :]
        half[points:, :] = from_ref[pl.ds(shard + place * some, some), :]


def halve(value, shard, vectors):
    whole = pl.BlockSpec(memory_space=pltpu.VMEM)
    half = jax.ShapeDtypeStruct(((shard + vectors) // 2, value.shape[1]), value.dtype)
    return pl.pallas_call(
        functools.partial(halve_kernel, shard, vectors),
        out_shape=[half, half],
        in_specs=[whole],
        out_specs=[whole, whole],
        compiler_params=pltpu.CompilerParams(vmem_limit_bytes=32 * 1024 * 1024),
        cost_estimate=pl.CostEstimate(flops=0, bytes_accessed=0, transcendentals=0),
    )(value)


def on_device(features, probes, noise_level):
    count = lax.axis_size("blk")
    inner = group_size(count)
    outer = count // inner
    shard = features.shape[0]
    vectors = probes.shape[1]
    packed = jnp.concatenate([features, probes.T], axis=0)

    def along_outer(value, edges):
        return lax.ppermute(value, "blk", [(s * inner + b, t * inner + b) for s, t in edges for b in range(inner)])

    def in_plane(value, hops):
        return lax.ppermute(value, "blk", [(a * inner + s, a * inner + t) for a in range(outer) for s, t in hops])

    def near(step):
        return [(plane_target(b, step, inner), b) for b in range(inner)]

    one_way, exchanges = outer_maps(outer)
    cols = [along_outer(packed, edges) for edges in one_way]
    others = [along_outer(packed, edges) for edges in exchanges]
    blocks = plane_blocks(packed, inner, in_plane, lambda block: halve(block, shard, vectors))
    direct = [step for step in range(1, inner) if step & (step - 1) == 0]
    passed = [step for step in range(1, inner) if step & (step - 1)]

    order = [0] + passed + [inner + place for place in range(len(cols))] + direct
    pairs = [(row, col, ("rows", "back")) for col in range(len(cols)) for row in range(inner)]
    sums = tile(blocks, cols, order, pairs, {}, shard, vectors, work=0.0)
    backs = [sums.pop(("back", place)) for place in range(len(cols))]
    half = inner // 2
    far, near_by = list(range(half, inner)), list(range(half))
    for rows in (far, near_by):
        pairs = [(place, col, ("rows",)) for col in range(len(others)) for place in range(len(rows))]
        known = {("rows", place): sums[("rows", row)] for place, row in enumerate(rows)}
        found = tile([blocks[row] for row in rows], others, range(len(rows) + len(others)), pairs, known, shard, vectors)
        sums.update({("rows", row): found[("rows", place)] for place, row in enumerate(rows)})
    pairs = [(row, 0, ("back",)) for row in range(inner)]
    own = tile(blocks, [packed], range(inner + 1), pairs, {}, shard, vectors, noise=[noise_level[None, :]])

    total = [sums["rows", 0], own["back", 0]]
    total += [in_plane(sums["rows", step], [(t, s) for s, t in near(step)]) for step in range(1, inner)]
    total += [along_outer(back, [(t, s) for s, t in edges]) for back, edges in zip(backs, one_way)]
    return functools.reduce(lambda sofar, term: sofar + term, total).T


def solution(mesh):
    placed = (P(("parts", "blk"), None), P(("parts", "blk"), None), P(("parts", "blk")))
    return jax.shard_map(
        on_device, mesh=mesh, in_specs=placed, out_specs=P(("parts", "blk"), None), check_vma=False
    )
```

```python
import functools
import math

import jax
import jax.numpy as jnp
from jax import lax
from jax.experimental import pallas as pl
from jax.experimental.pallas import tpu as pltpu
from jax.sharding import PartitionSpec as P

ROOT5 = math.sqrt(5.0)
DECAY = -ROOT5 * math.log2(math.e)
ROWS_BY_ROWS = (((1,), (1,)), ((), ()))


def group_size(count):
    size = 1
    while size * size < count or count % size:
        size += 1
    return size


def plane_blocks(value, count, send, cut):
    if count & (count - 1):
        maps = {step: [(b, (b - step) % count) for b in range(count)] for step in range(1, count)}
        return [(value,)] + [(send(value, maps[step]),) for step in range(1, count)]
    blocks = {0: (value,)}
    bit = count // 2
    while bit:
        hops = [(b, b ^ bit) for b in range(count)]
        for known in list(blocks):
            parts = blocks[known] if known == 0 or len(blocks[known]) > 1 else cut(*blocks[known])
            blocks[known | bit] = tuple(send(part, hops) for part in parts)
        bit //= 2
    return [blocks[distance] for distance in range(count)]


def plane_target(index, step, count):
    return (index + step) % count if count & (count - 1) else index ^ step


def outer_maps(count):
    bits = count.bit_length() - 1
    order = list(range(count))
    if count == 1 << bits:
        order = [int(f"{a:0{bits}b}"[::-1], 2) if bits else a for a in reversed(order)]
    shifts = [[(order[p], order[(p + step) % count]) for p in range(count)] for step in range(1, count // 2 + 1)]
    if count % 2:
        return shifts, []
    return shifts[:-1], shifts[-1:]


def matern(dist2):
    dist2 = jnp.maximum(dist2, 1e-30)
    dist = dist2 * lax.rsqrt(dist2)
    poly = (1.0 + ROOT5 * dist) + (5.0 / 3.0) * dist2
    return (poly * jnp.exp2(DECAY * dist)).astype(jnp.bfloat16)


def lane_squares(block):
    wide = block.astype(jnp.float32)
    sums = jnp.sum(wide * wide, axis=1, keepdims=True)
    return jnp.transpose(jnp.broadcast_to(sums, (block.shape[0], 128)))[0:1, :]


def joined(refs, shard, vectors):
    points, some = shard // len(refs), vectors // len(refs)
    features = [ref[0:points, :] for ref in refs]
    probes = [ref[pl.ds(points, some), :] for ref in refs]
    return (jnp.concatenate(features), jnp.concatenate(probes)) if len(refs) > 1 else (features[0], probes[0])


def tile_kernel(order, pairs, known, counts, shard, vectors, *refs):
    parts, cols_in, noise_in = counts
    rest = list(refs)
    blocks = {place: [rest.pop(0) for _ in range((*parts, *[1] * cols_in)[place])] for place in order}
    rows = [joined(blocks[place], shard, vectors) for place in range(len(parts))]
    cols = [blocks[len(parts) + place][0] for place in range(cols_in)]
    noise = [rest.pop(0) for _ in range(noise_in)]
    sums = {name: rest.pop(0)[...] for name in known}
    squares = {}
    for col in sorted({col for _, col, _ in pairs}):
        kind = next(kind for _, place, kind in pairs if place == col)
        members = [row for row, place, _ in pairs if place == col]
        for row in members:
            if row not in squares:
                wide = rows[row][0].astype(jnp.float32)
                squares[row] = jnp.sum(wide * wide, axis=1, keepdims=True)
        block = cols[col][0:shard, :]
        scaled, col_squares = block * jnp.asarray(-2.0, block.dtype), lane_squares(block)
        left = jnp.concatenate([rows[row][0] for row in members])
        cross = lax.dot_general(left, scaled, ROWS_BY_ROWS, preferred_element_type=jnp.float32)
        kernel = matern((jnp.concatenate([squares[row] for row in members]) + col_squares) + cross)
        found = {}
        if "back" in kind:
            probes = jnp.concatenate([rows[row][1] for row in members], axis=1)
            found["back", col] = jnp.dot(probes, kernel, preferred_element_type=jnp.float32)
        if "rows" in kind:
            col_probes = cols[col][pl.ds(shard, vectors), :]
            terms = lax.dot_general(col_probes, kernel, ROWS_BY_ROWS, preferred_element_type=jnp.float32)
            for place, row in enumerate(members):
                found["rows", row] = terms[:, place * shard : (place + 1) * shard]
        for name, value in found.items():
            sums[name] = sums[name] + value if name in sums else value
    for place in range(noise_in):
        probes = cols[place][pl.ds(shard, vectors), :].astype(jnp.float32)
        sums["back", place] = sums["back", place] + noise[place][...] * probes
    for ref, name in zip(rest, sorted(sums)):
        ref[...] = sums[name]


def tile(rows, cols, order, pairs, sums, shard, vectors, noise=(), work=1.0):
    blocks = [*rows, *[(col,) for col in cols]]
    args = [*[part for place in order for part in blocks[place]], *noise, *sums.values()]
    elements = len(pairs) * shard * shard
    width = cols[0].shape[1]
    names = sorted({(part, col if part == "back" else row) for row, col, kind in pairs for part in kind} | set(sums))
    whole = pl.BlockSpec(memory_space=pltpu.VMEM)
    found = pl.pallas_call(
        functools.partial(
            tile_kernel, list(order), tuple(pairs), tuple(sums), (tuple(map(len, rows)), len(cols), len(noise)), shard, vectors
        ),
        out_shape=[jax.ShapeDtypeStruct((vectors, shard), jnp.float32)] * len(names),
        in_specs=[whole] * len(args),
        out_specs=[whole] * len(names),
        compiler_params=pltpu.CompilerParams(vmem_limit_bytes=32 * 1024 * 1024),
        cost_estimate=pl.CostEstimate(
            flops=int(work * 2 * elements * (width + 2 * vectors)),
            bytes_accessed=int(work * 2 * width * shard * len(blocks)),
            transcendentals=int(work * 2 * elements),
        ),
    )(*args)
    return dict(zip(names, found))


def halve_kernel(shard, vectors, from_ref, *halves):
    points, some = shard // 2, vectors // 2
    for place, half in enumerate(halves):
        half[0:points, :] = from_ref[pl.ds(place * points, points), :]
        half[points:, :] = from_ref[pl.ds(shard + place * some, some), :]


def halve(value, shard, vectors):
    whole = pl.BlockSpec(memory_space=pltpu.VMEM)
    half = jax.ShapeDtypeStruct(((shard + vectors) // 2, value.shape[1]), value.dtype)
    return pl.pallas_call(
        functools.partial(halve_kernel, shard, vectors),
        out_shape=[half, half],
        in_specs=[whole],
        out_specs=[whole, whole],
        compiler_params=pltpu.CompilerParams(vmem_limit_bytes=32 * 1024 * 1024),
        cost_estimate=pl.CostEstimate(flops=0, bytes_accessed=0, transcendentals=0),
    )(value)


def on_device(features, probes, noise_level):
    count = lax.axis_size("blk")
    inner = group_size(count)
    outer = count // inner
    shard = features.shape[0]
    vectors = probes.shape[1]
    packed = jnp.concatenate([features, probes.T], axis=0)

    def along_outer(value, edges):
        return lax.ppermute(value, "blk", [(s * inner + b, t * inner + b) for s, t in edges for b in range(inner)])

    def in_plane(value, hops):
        return lax.ppermute(value, "blk", [(a * inner + s, a * inner + t) for a in range(outer) for s, t in hops])

    def near(step):
        return [(plane_target(b, step, inner), b) for b in range(inner)]

    one_way, exchanges = outer_maps(outer)
    cols = [along_outer(packed, edges) for edges in one_way]
    others = [along_outer(packed, edges) for edges in exchanges]
    blocks = plane_blocks(packed, inner, in_plane, lambda block: halve(block, shard, vectors))
    direct = [step for step in range(1, inner) if step & (step - 1) == 0]
    passed = [step for step in range(1, inner) if step & (step - 1)]

    order = [0] + passed + [inner + place for place in range(len(cols))] + direct
    pairs = [(row, col, ("rows", "back")) for col in range(len(cols)) for row in range(inner)]
    sums = tile(blocks, cols, order, pairs, {}, shard, vectors, work=0.0)
    backs = [sums.pop(("back", place)) for place in range(len(cols))]
    half = inner // 2
    far, near_by = list(range(half, inner)), list(range(half))
    for rows in (far, near_by):
        pairs = [(place, col, ("rows",)) for col in range(len(others)) for place in range(len(rows))]
        known = {("rows", place): sums[("rows", row)] for place, row in enumerate(rows)}
        found = tile([blocks[row] for row in rows], others, range(len(rows) + len(others)), pairs, known, shard, vectors)
        sums.update({("rows", row): found[("rows", place)] for place, row in enumerate(rows)})
    pairs = [(row, 0, ("back",)) for row in range(inner)]
    own = tile(blocks, [packed], range(inner + 1), pairs, {}, shard, vectors, noise=[noise_level[None, :]])

    total = [sums["rows", 0], own["back", 0]]
    total += [in_plane(sums["rows", step], [(t, s) for s, t in near(step)]) for step in range(1, inner)]
    total += [along_outer(back, [(t, s) for s, t in edges]) for back, edges in zip(backs, one_way)]
    return functools.reduce(lambda sofar, term: sofar + term, total).T


def solution(mesh):
    placed = (P(("parts", "blk"), None), P(("parts", "blk"), None), P(("parts", "blk")))
    return jax.shard_map(
        on_device, mesh=mesh, in_specs=placed, out_specs=P(("parts", "blk"), None), check_vma=False
    )
```

```python
import functools
import math

import jax
import jax.numpy as jnp
from jax import lax
from jax.experimental import pallas as pl
from jax.experimental.pallas import tpu as pltpu
from jax.sharding import PartitionSpec as P

ROOT5 = math.sqrt(5.0)
DECAY = -ROOT5 * math.log2(math.e)
ROWS_BY_ROWS = (((1,), (1,)), ((), ()))


def group_size(count):
    size = 1
    while size * size < count or count % size:
        size += 1
    return size


def plane_blocks(value, count, send, cut):
    if count & (count - 1):
        maps = {step: [(b, (b - step) % count) for b in range(count)] for step in range(1, count)}
        return [(value,)] + [(send(value, maps[step]),) for step in range(1, count)]
    blocks = {0: (value,)}
    bit = count // 2
    while bit:
        hops = [(b, b ^ bit) for b in range(count)]
        for known in list(blocks):
            parts = blocks[known] if known == 0 or len(blocks[known]) > 1 else cut(*blocks[known])
            blocks[known | bit] = tuple(send(part, hops) for part in parts)
        bit //= 2
    return [blocks[distance] for distance in range(count)]


def plane_target(index, step, count):
    return (index + step) % count if count & (count - 1) else index ^ step


def outer_maps(count):
    bits = count.bit_length() - 1
    order = list(range(count))
    if count == 1 << bits:
        order = [int(f"{a:0{bits}b}"[::-1], 2) if bits else a for a in reversed(order)]
    shifts = [[(order[p], order[(p + step) % count]) for p in range(count)] for step in range(1, count // 2 + 1)]
    if count % 2:
        return shifts, []
    return shifts[:-1], shifts[-1:]


def matern(dist2):
    dist2 = jnp.maximum(dist2, 1e-30)
    dist = dist2 * lax.rsqrt(dist2)
    poly = (1.0 + ROOT5 * dist) + (5.0 / 3.0) * dist2
    return (poly * jnp.exp2(DECAY * dist)).astype(jnp.bfloat16)


def lane_squares(block):
    wide = block.astype(jnp.float32)
    sums = jnp.sum(wide * wide, axis=1, keepdims=True)
    return jnp.transpose(jnp.broadcast_to(sums, (block.shape[0], 128)))[0:1, :]


def joined(refs, shard, vectors):
    points, some = shard // len(refs), vectors // len(refs)
    features = [ref[0:points, :] for ref in refs]
    probes = [ref[pl.ds(points, some), :] for ref in refs]
    return (jnp.concatenate(features), jnp.concatenate(probes)) if len(refs) > 1 else (features[0], probes[0])


def tile_kernel(order, pairs, known, counts, shard, vectors, *refs):
    parts, cols_in, noise_in = counts
    rest = list(refs)
    blocks = {place: [rest.pop(0) for _ in range((*parts, *[1] * cols_in)[place])] for place in order}
    rows = [joined(blocks[place], shard, vectors) for place in range(len(parts))]
    cols = [blocks[len(parts) + place][0] for place in range(cols_in)]
    noise = [rest.pop(0) for _ in range(noise_in)]
    sums = {name: rest.pop(0)[...] for name in known}
    squares = {}
    for col in sorted({col for _, col, _ in pairs}):
        kind = next(kind for _, place, kind in pairs if place == col)
        members = [row for row, place, _ in pairs if place == col]
        for row in members:
            if row not in squares:
                wide = rows[row][0].astype(jnp.float32)
                squares[row] = jnp.sum(wide * wide, axis=1, keepdims=True)
        block = cols[col][0:shard, :]
        scaled, col_squares = block * jnp.asarray(-2.0, block.dtype), lane_squares(block)
        left = jnp.concatenate([rows[row][0] for row in members])
        cross = lax.dot_general(left, scaled, ROWS_BY_ROWS, preferred_element_type=jnp.float32)
        kernel = matern((jnp.concatenate([squares[row] for row in members]) + col_squares) + cross)
        found = {}
        if "back" in kind:
            probes = jnp.concatenate([rows[row][1] for row in members], axis=1)
            found["back", col] = jnp.dot(probes, kernel, preferred_element_type=jnp.float32)
        if "rows" in kind:
            col_probes = cols[col][pl.ds(shard, vectors), :]
            terms = lax.dot_general(col_probes, kernel, ROWS_BY_ROWS, preferred_element_type=jnp.float32)
            for place, row in enumerate(members):
                found["rows", row] = terms[:, place * shard : (place + 1) * shard]
        for name, value in found.items():
            sums[name] = sums[name] + value if name in sums else value
    for place in range(noise_in):
        probes = cols[place][pl.ds(shard, vectors), :].astype(jnp.float32)
        sums["back", place] = sums["back", place] + noise[place][...] * probes
    for ref, name in zip(rest, sorted(sums)):
        ref[...] = sums[name].astype(ref.dtype)


def tile(rows, cols, order, pairs, sums, shard, vectors, noise=(), work=1.0, sent=()):
    blocks = [*rows, *[(col,) for col in cols]]
    args = [*[part for place in order for part in blocks[place]], *noise, *sums.values()]
    elements = len(pairs) * shard * shard
    width = cols[0].shape[1]
    names = sorted({(part, col if part == "back" else row) for row, col, kind in pairs for part in kind} | set(sums))
    whole = pl.BlockSpec(memory_space=pltpu.VMEM)
    found = pl.pallas_call(
        functools.partial(
            tile_kernel, list(order), tuple(pairs), tuple(sums), (tuple(map(len, rows)), len(cols), len(noise)), shard, vectors
        ),
        out_shape=[
            jax.ShapeDtypeStruct((vectors, shard), jnp.bfloat16 if name in sent else jnp.float32) for name in names
        ],
        in_specs=[whole] * len(args),
        out_specs=[whole] * len(names),
        compiler_params=pltpu.CompilerParams(vmem_limit_bytes=32 * 1024 * 1024),
        cost_estimate=pl.CostEstimate(
            flops=int(work * 2 * elements * (width + 2 * vectors)),
            bytes_accessed=int(work * 2 * width * shard * len(blocks)),
            transcendentals=int(work * 2 * elements),
        ),
    )(*args)
    return dict(zip(names, found))


def halve_kernel(shard, vectors, from_ref, *halves):
    points, some = shard // 2, vectors // 2
    for place, half in enumerate(halves):
        half[0:points, :] = from_ref[pl.ds(place * points, points), :]
        half[points:, :] = from_ref[pl.ds(shard + place * some, some), :]


def halve(value, shard, vectors):
    whole = pl.BlockSpec(memory_space=pltpu.VMEM)
    half = jax.ShapeDtypeStruct(((shard + vectors) // 2, value.shape[1]), value.dtype)
    return pl.pallas_call(
        functools.partial(halve_kernel, shard, vectors),
        out_shape=[half, half],
        in_specs=[whole],
        out_specs=[whole, whole],
        compiler_params=pltpu.CompilerParams(vmem_limit_bytes=32 * 1024 * 1024),
        cost_estimate=pl.CostEstimate(flops=0, bytes_accessed=0, transcendentals=0),
    )(value)


def on_device(features, probes, noise_level):
    count = lax.axis_size("blk")
    inner = group_size(count)
    outer = count // inner
    shard = features.shape[0]
    vectors = probes.shape[1]
    packed = jnp.concatenate([features, probes.T], axis=0)

    def along_outer(value, edges):
        return lax.ppermute(value, "blk", [(s * inner + b, t * inner + b) for s, t in edges for b in range(inner)])

    def in_plane(value, hops):
        return lax.ppermute(value, "blk", [(a * inner + s, a * inner + t) for a in range(outer) for s, t in hops])

    def near(step):
        return [(plane_target(b, step, inner), b) for b in range(inner)]

    one_way, exchanges = outer_maps(outer)
    cols = [along_outer(packed, edges) for edges in one_way]
    others = [along_outer(packed, edges) for edges in exchanges]
    blocks = plane_blocks(packed, inner, in_plane, lambda block: halve(block, shard, vectors))
    direct = [step for step in range(1, inner) if step & (step - 1) == 0]
    passed = [step for step in range(1, inner) if step & (step - 1)]

    order = [0] + passed + [inner + place for place in range(len(cols))] + direct
    pairs = [(row, col, ("rows", "back")) for col in range(len(cols)) for row in range(inner)]
    sums = tile(blocks, cols, order, pairs, {}, shard, vectors, work=0.0)
    backs = [sums.pop(("back", place)) for place in range(len(cols))]
    half = inner // 2
    far, near_by = list(range(half, inner)), list(range(half))
    for rows in (far, near_by):
        pairs = [(place, col, ("rows",)) for col in range(len(others)) for place in range(len(rows))]
        known = {("rows", place): sums[("rows", row)] for place, row in enumerate(rows)}
        sent = [("rows", place) for place, row in enumerate(rows) if row]
        order = range(len(rows) + len(others))
        found = tile([blocks[row] for row in rows], others, order, pairs, known, shard, vectors, sent=sent)
        sums.update({("rows", row): found[("rows", place)] for place, row in enumerate(rows)})
    pairs = [(row, 0, ("back",)) for row in range(inner)]
    own = tile(blocks, [packed], range(inner + 1), pairs, {}, shard, vectors, noise=[noise_level[None, :]])

    total = [sums["rows", 0], own["back", 0]]
    total += [in_plane(sums["rows", step], [(t, s) for s, t in near(step)]) for step in range(1, inner)]
    total += [along_outer(back, [(t, s) for s, t in edges]) for back, edges in zip(backs, one_way)]
    return functools.reduce(lambda sofar, term: sofar + term, total).T


def solution(mesh):
    placed = (P(("parts", "blk"), None), P(("parts", "blk"), None), P(("parts", "blk")))
    return jax.shard_map(
        on_device, mesh=mesh, in_specs=placed, out_specs=P(("parts", "blk"), None), check_vma=False
    )
```

```python
import functools
import math

import jax
import jax.numpy as jnp
from jax import lax
from jax.experimental import pallas as pl
from jax.experimental.pallas import tpu as pltpu
from jax.sharding import PartitionSpec as P

ROOT5 = math.sqrt(5.0)
DECAY = -ROOT5 * math.log2(math.e)
ROWS_BY_ROWS = (((1,), (1,)), ((), ()))


def group_size(count):
    size = 1
    while size * size < count or count % size:
        size += 1
    return size


def plane_blocks(value, count, send, cut):
    if count & (count - 1):
        maps = {step: [(b, (b - step) % count) for b in range(count)] for step in range(1, count)}
        return [(value,)] + [(send(value, maps[step]),) for step in range(1, count)]
    blocks = {0: (value,)}
    bit = count // 2
    while bit:
        hops = [(b, b ^ bit) for b in range(count)]
        for known in list(blocks):
            parts = blocks[known] if known == 0 or len(blocks[known]) > 1 else cut(*blocks[known])
            blocks[known | bit] = tuple(send(part, hops) for part in parts)
        bit //= 2
    return [blocks[distance] for distance in range(count)]


def plane_target(index, step, count):
    return (index + step) % count if count & (count - 1) else index ^ step


def outer_maps(count):
    bits = count.bit_length() - 1
    order = list(range(count))
    if count == 1 << bits:
        order = [int(f"{a:0{bits}b}"[::-1], 2) if bits else a for a in reversed(order)]
    shifts = [[(order[p], order[(p + step) % count]) for p in range(count)] for step in range(1, count // 2 + 1)]
    if count % 2:
        return shifts, []
    return shifts[:-1], shifts[-1:]


def matern(dist2):
    dist2 = jnp.maximum(dist2, 1e-30)
    dist = dist2 * lax.rsqrt(dist2)
    poly = (1.0 + ROOT5 * dist) + (5.0 / 3.0) * dist2
    return (poly * jnp.exp2(DECAY * dist)).astype(jnp.bfloat16)


def lane_squares(block):
    wide = block.astype(jnp.float32)
    sums = jnp.sum(wide * wide, axis=1, keepdims=True)
    return jnp.transpose(jnp.broadcast_to(sums, (block.shape[0], 128)))[0:1, :]


def joined(refs, shard, vectors):
    points, some = shard // len(refs), vectors // len(refs)
    features = [ref[0:points, :] for ref in refs]
    probes = [ref[pl.ds(points, some), :] for ref in refs]
    return (jnp.concatenate(features), jnp.concatenate(probes)) if len(refs) > 1 else (features[0], probes[0])


def tile_kernel(order, pairs, known, counts, shard, vectors, *refs):
    parts, cols_in, noise_in = counts
    rest = list(refs)
    blocks = {place: [rest.pop(0) for _ in range((*parts, *[1] * cols_in)[place])] for place in order}
    rows = [joined(blocks[place], shard, vectors) for place in range(len(parts))]
    cols = [blocks[len(parts) + place][0] for place in range(cols_in)]
    noise = [rest.pop(0) for _ in range(noise_in)]
    sums = {name: rest.pop(0)[...] for name in known}
    squares = {}
    for col in sorted({col for _, col, _ in pairs}):
        kind = next(kind for _, place, kind in pairs if place == col)
        members = [row for row, place, _ in pairs if place == col]
        for row in members:
            if row not in squares:
                wide = rows[row][0].astype(jnp.float32)
                squares[row] = jnp.sum(wide * wide, axis=1, keepdims=True)
        block = cols[col][0:shard, :]
        scaled, col_squares = block * jnp.asarray(-2.0, block.dtype), lane_squares(block)
        left = jnp.concatenate([rows[row][0] for row in members])
        cross = lax.dot_general(left, scaled, ROWS_BY_ROWS, preferred_element_type=jnp.float32)
        kernel = matern((jnp.concatenate([squares[row] for row in members]) + col_squares) + cross)
        found = {}
        if "back" in kind:
            probes = jnp.concatenate([rows[row][1] for row in members], axis=1)
            found["back", col] = jnp.dot(probes, kernel, preferred_element_type=jnp.float32)
        if "rows" in kind:
            col_probes = cols[col][pl.ds(shard, vectors), :]
            terms = lax.dot_general(col_probes, kernel, ROWS_BY_ROWS, preferred_element_type=jnp.float32)
            for place, row in enumerate(members):
                found["rows", row] = terms[:, place * shard : (place + 1) * shard]
        for name, value in found.items():
            sums[name] = sums[name] + value if name in sums else value
    for place in range(noise_in):
        probes = cols[place][pl.ds(shard, vectors), :].astype(jnp.float32)
        sums["back", place] = sums["back", place] + noise[place][...] * probes
    for ref, name in zip(rest, sorted(sums)):
        ref[...] = sums[name].astype(ref.dtype)


def tile(rows, cols, order, pairs, sums, shard, vectors, noise=(), work=1.0, sent=()):
    blocks = [*rows, *[(col,) for col in cols]]
    args = [*[part for place in order for part in blocks[place]], *noise, *sums.values()]
    elements = len(pairs) * shard * shard
    width = cols[0].shape[1]
    names = sorted({(part, col if part == "back" else row) for row, col, kind in pairs for part in kind} | set(sums))
    whole = pl.BlockSpec(memory_space=pltpu.VMEM)
    found = pl.pallas_call(
        functools.partial(
            tile_kernel, list(order), tuple(pairs), tuple(sums), (tuple(map(len, rows)), len(cols), len(noise)), shard, vectors
        ),
        out_shape=[
            jax.ShapeDtypeStruct((vectors, shard), jnp.bfloat16 if name in sent else jnp.float32) for name in names
        ],
        in_specs=[whole] * len(args),
        out_specs=[whole] * len(names),
        compiler_params=pltpu.CompilerParams(vmem_limit_bytes=32 * 1024 * 1024),
        cost_estimate=pl.CostEstimate(
            flops=int(work * 2 * elements * (width + 2 * vectors)),
            bytes_accessed=int(work * 2 * width * shard * len(blocks)),
            transcendentals=int(work * 2 * elements),
        ),
    )(*args)
    return dict(zip(names, found))


def features_of(rows):
    left = jnp.concatenate([row[0] for row in rows])
    wide = left.astype(jnp.float32)
    return left, jnp.sum(wide * wide, axis=1, keepdims=True)


def kernel_of(left, squares, col):
    scaled = col * jnp.asarray(-2.0, col.dtype)
    cross = lax.dot_general(left, scaled, ROWS_BY_ROWS, preferred_element_type=jnp.float32)
    return matern((squares + lane_squares(col)) + cross)


def cycle_kernel(order, parts, cols_in, shard, vectors, *refs):
    rest = list(refs)
    blocks = {place: [rest.pop(0) for _ in range((*parts, *[1] * cols_in)[place])] for place in order}
    rows = [joined(blocks[place], shard, vectors) for place in range(len(parts))]
    left, squares = features_of(rows)
    probes = jnp.concatenate([row[1] for row in rows], axis=1)
    for col in range(cols_in):
        kernel = kernel_of(left, squares, blocks[len(parts) + col][0][0:shard, :])
        rest[col][...] = jnp.dot(probes, kernel, preferred_element_type=jnp.float32)
        rest[cols_in + col][...] = kernel


def rows_kernel(parts, start, known, fresh, shard, vectors, *refs):
    rest = list(refs)
    rows = [joined([rest.pop(0) for _ in range(count)], shard, vectors) for count in parts]
    cols, kernels, known_cols = ([rest.pop(0) for _ in range(n)] for n in (fresh, known, known))
    left, squares = features_of(rows)
    total = jnp.zeros((vectors, len(parts) * shard), jnp.float32)
    for kernel, col in zip(kernels, known_cols):
        some = kernel[start * shard : (start + len(parts)) * shard, :]
        probes = col[pl.ds(shard, vectors), :]
        total += lax.dot_general(probes, some, ROWS_BY_ROWS, preferred_element_type=jnp.float32)
    for col in cols:
        kernel = kernel_of(left, squares, col[0:shard, :])
        probes = col[pl.ds(shard, vectors), :]
        total += lax.dot_general(probes, kernel, ROWS_BY_ROWS, preferred_element_type=jnp.float32)
    for place, ref in enumerate(rest):
        ref[...] = total[:, place * shard : (place + 1) * shard].astype(ref.dtype)


def call(body, args, outs, work):
    whole = pl.BlockSpec(memory_space=pltpu.VMEM)
    return pl.pallas_call(
        body,
        out_shape=outs,
        in_specs=[whole] * len(args),
        out_specs=[whole] * len(outs),
        compiler_params=pltpu.CompilerParams(vmem_limit_bytes=32 * 1024 * 1024),
        cost_estimate=pl.CostEstimate(flops=2 * work, bytes_accessed=0, transcendentals=0),
    )(*args)


def halve_kernel(shard, vectors, from_ref, *halves):
    points, some = shard // 2, vectors // 2
    for place, half in enumerate(halves):
        half[0:points, :] = from_ref[pl.ds(place * points, points), :]
        half[points:, :] = from_ref[pl.ds(shard + place * some, some), :]


def halve(value, shard, vectors):
    whole = pl.BlockSpec(memory_space=pltpu.VMEM)
    half = jax.ShapeDtypeStruct(((shard + vectors) // 2, value.shape[1]), value.dtype)
    return pl.pallas_call(
        functools.partial(halve_kernel, shard, vectors),
        out_shape=[half, half],
        in_specs=[whole],
        out_specs=[whole, whole],
        compiler_params=pltpu.CompilerParams(vmem_limit_bytes=32 * 1024 * 1024),
        cost_estimate=pl.CostEstimate(flops=0, bytes_accessed=0, transcendentals=0),
    )(value)


def on_device(features, probes, noise_level):
    count = lax.axis_size("blk")
    inner = group_size(count)
    outer = count // inner
    shard = features.shape[0]
    vectors = probes.shape[1]
    packed = jnp.concatenate([features, probes.T], axis=0)

    def along_outer(value, edges):
        return lax.ppermute(value, "blk", [(s * inner + b, t * inner + b) for s, t in edges for b in range(inner)])

    def in_plane(value, hops):
        return lax.ppermute(value, "blk", [(a * inner + s, a * inner + t) for a in range(outer) for s, t in hops])

    def near(step):
        return [(plane_target(b, step, inner), b) for b in range(inner)]

    one_way, exchanges = outer_maps(outer)
    cols = [along_outer(packed, edges) for edges in one_way]
    others = [along_outer(packed, edges) for edges in exchanges]
    blocks = plane_blocks(packed, inner, in_plane, lambda block: halve(block, shard, vectors))
    direct = [step for step in range(1, inner) if step & (step - 1) == 0]
    passed = [step for step in range(1, inner) if step & (step - 1)]

    order = [0] + passed + [inner + place for place in range(len(cols))] + direct
    parts = tuple(map(len, blocks))
    operands = [*blocks, *[(col,) for col in cols]]
    flat = jax.ShapeDtypeStruct((vectors, shard), jnp.float32)
    sent = jax.ShapeDtypeStruct((vectors, shard), jnp.bfloat16)
    matrix = jax.ShapeDtypeStruct((inner * shard, shard), jnp.bfloat16)
    found = call(
        functools.partial(cycle_kernel, order, parts, len(cols), shard, vectors),
        [part for place in order for part in operands[place]],
        [flat] * len(cols) + [matrix] * len(cols),
        0,
    )
    backs, kernels = found[: len(cols)], found[len(cols) :]
    half = inner // 2
    sums = {}
    for start, stop in ((half, inner), (0, half)):
        some = blocks[start:stop]
        found = call(
            functools.partial(rows_kernel, parts[start:stop], start, len(cols), len(others), shard, vectors),
            [*[part for block in some for part in block], *others, *kernels, *cols],
            [sent if row else flat for row in range(start, stop)],
            len(some) * len(others) * shard * shard * features.shape[1],
        )
        sums.update({("rows", start + place): value for place, value in enumerate(found)})
    pairs = [(row, 0, ("back",)) for row in range(inner)]
    own = tile(blocks, [packed], range(inner + 1), pairs, {}, shard, vectors, noise=[noise_level[None, :]])

    total = [sums["rows", 0], own["back", 0]]
    total += [in_plane(sums["rows", step], [(t, s) for s, t in near(step)]) for step in range(1, inner)]
    total += [along_outer(back, [(t, s) for s, t in edges]) for back, edges in zip(backs, one_way)]
    return functools.reduce(lambda sofar, term: sofar + term, total).T


def solution(mesh):
    placed = (P(("parts", "blk"), None), P(("parts", "blk"), None), P(("parts", "blk")))
    return jax.shard_map(
        on_device, mesh=mesh, in_specs=placed, out_specs=P(("parts", "blk"), None), check_vma=False
    )
```

```python
import functools
import math

import jax
import jax.numpy as jnp
from jax import lax
from jax.experimental import pallas as pl
from jax.experimental.pallas import tpu as pltpu
from jax.sharding import PartitionSpec as P

ROOT5 = math.sqrt(5.0)
DECAY = -ROOT5 * math.log2(math.e)
ROWS_BY_ROWS = (((1,), (1,)), ((), ()))


def group_size(count):
    size = 1
    while size * size < count or count % size:
        size += 1
    return size


def plane_blocks(value, count, send, cut):
    if count & (count - 1):
        maps = {step: [(b, (b - step) % count) for b in range(count)] for step in range(1, count)}
        return [(value,)] + [(send(value, maps[step]),) for step in range(1, count)]
    blocks = {0: (value,)}
    bit = count // 2
    while bit:
        hops = [(b, b ^ bit) for b in range(count)]
        for known in list(blocks):
            parts = blocks[known] if known == 0 or len(blocks[known]) > 1 else cut(*blocks[known])
            blocks[known | bit] = tuple(send(part, hops) for part in parts)
        bit //= 2
    return [blocks[distance] for distance in range(count)]


def plane_target(index, step, count):
    return (index + step) % count if count & (count - 1) else index ^ step


def outer_maps(count):
    bits = count.bit_length() - 1
    order = list(range(count))
    if count == 1 << bits:
        order = [int(f"{a:0{bits}b}"[::-1], 2) if bits else a for a in reversed(order)]
    shifts = [[(order[p], order[(p + step) % count]) for p in range(count)] for step in range(1, count // 2 + 1)]
    if count % 2:
        return shifts, []
    return shifts[:-1], shifts[-1:]


def matern(dist2):
    dist2 = jnp.maximum(dist2, 1e-30)
    dist = dist2 * lax.rsqrt(dist2)
    poly = (1.0 + ROOT5 * dist) + (5.0 / 3.0) * dist2
    return (poly * jnp.exp2(DECAY * dist)).astype(jnp.bfloat16)


def lane_squares(block):
    wide = block.astype(jnp.float32)
    sums = jnp.sum(wide * wide, axis=1, keepdims=True)
    return jnp.transpose(jnp.broadcast_to(sums, (block.shape[0], 128)))[0:1, :]


def joined(refs, shard, vectors):
    points, some = shard // len(refs), vectors // len(refs)
    features = [ref[0:points, :] for ref in refs]
    probes = [ref[pl.ds(points, some), :] for ref in refs]
    return (jnp.concatenate(features), jnp.concatenate(probes)) if len(refs) > 1 else (features[0], probes[0])


def tile_kernel(order, pairs, known, counts, shard, vectors, *refs):
    parts, cols_in, noise_in = counts
    rest = list(refs)
    blocks = {place: [rest.pop(0) for _ in range((*parts, *[1] * cols_in)[place])] for place in order}
    rows = [joined(blocks[place], shard, vectors) for place in range(len(parts))]
    cols = [blocks[len(parts) + place][0] for place in range(cols_in)]
    noise = [rest.pop(0) for _ in range(noise_in)]
    sums = {name: rest.pop(0)[...] for name in known}
    squares = {}
    for col in sorted({col for _, col, _ in pairs}):
        kind = next(kind for _, place, kind in pairs if place == col)
        members = [row for row, place, _ in pairs if place == col]
        for row in members:
            if row not in squares:
                wide = rows[row][0].astype(jnp.float32)
                squares[row] = jnp.sum(wide * wide, axis=1, keepdims=True)
        block = cols[col][0:shard, :]
        scaled, col_squares = block * jnp.asarray(-2.0, block.dtype), lane_squares(block)
        left = jnp.concatenate([rows[row][0] for row in members])
        cross = lax.dot_general(left, scaled, ROWS_BY_ROWS, preferred_element_type=jnp.float32)
        kernel = matern((jnp.concatenate([squares[row] for row in members]) + col_squares) + cross)
        found = {}
        if "back" in kind:
            probes = jnp.concatenate([rows[row][1] for row in members], axis=1)
            found["back", col] = jnp.dot(probes, kernel, preferred_element_type=jnp.float32)
        if "rows" in kind:
            col_probes = cols[col][pl.ds(shard, vectors), :]
            terms = lax.dot_general(col_probes, kernel, ROWS_BY_ROWS, preferred_element_type=jnp.float32)
            for place, row in enumerate(members):
                found["rows", row] = terms[:, place * shard : (place + 1) * shard]
        for name, value in found.items():
            sums[name] = sums[name] + value if name in sums else value
    for place in range(noise_in):
        probes = cols[place][pl.ds(shard, vectors), :].astype(jnp.float32)
        sums["back", place] = sums["back", place] + noise[place][...] * probes
    for ref, name in zip(rest, sorted(sums)):
        ref[...] = sums[name].astype(ref.dtype)


def tile(rows, cols, order, pairs, sums, shard, vectors, noise=(), work=1.0, sent=()):
    blocks = [*rows, *[(col,) for col in cols]]
    args = [*[part for place in order for part in blocks[place]], *noise, *sums.values()]
    elements = len(pairs) * shard * shard
    width = cols[0].shape[1]
    names = sorted({(part, col if part == "back" else row) for row, col, kind in pairs for part in kind} | set(sums))
    whole = pl.BlockSpec(memory_space=pltpu.VMEM)
    found = pl.pallas_call(
        functools.partial(
            tile_kernel, list(order), tuple(pairs), tuple(sums), (tuple(map(len, rows)), len(cols), len(noise)), shard, vectors
        ),
        out_shape=[
            jax.ShapeDtypeStruct((vectors, shard), jnp.bfloat16 if name in sent else jnp.float32) for name in names
        ],
        in_specs=[whole] * len(args),
        out_specs=[whole] * len(names),
        compiler_params=pltpu.CompilerParams(vmem_limit_bytes=32 * 1024 * 1024),
        cost_estimate=pl.CostEstimate(
            flops=int(work * 2 * elements * (width + 2 * vectors)),
            bytes_accessed=int(work * 2 * width * shard * len(blocks)),
            transcendentals=int(work * 2 * elements),
        ),
    )(*args)
    return dict(zip(names, found))


def features_of(rows):
    left = jnp.concatenate([row[0] for row in rows])
    wide = left.astype(jnp.float32)
    return left, jnp.sum(wide * wide, axis=1, keepdims=True)


def kernel_of(left, squares, col):
    scaled = col * jnp.asarray(-2.0, col.dtype)
    cross = lax.dot_general(left, scaled, ROWS_BY_ROWS, preferred_element_type=jnp.float32)
    return matern((squares + lane_squares(col)) + cross)


def cycle_kernel(order, parts, cols_in, shard, vectors, own_ref, *refs):
    rest = list(refs)
    blocks = {place: [rest.pop(0) for _ in range((*parts, *[1] * cols_in)[place])] for place in order}
    rows = [joined(blocks[place], shard, vectors) for place in range(len(parts))]
    left, squares = features_of(rows)
    probes = jnp.concatenate([row[1] for row in rows], axis=1)
    for col in range(cols_in):
        kernel = kernel_of(left, squares, blocks[len(parts) + col][0][0:shard, :])
        rest[col][...] = jnp.dot(probes, kernel, preferred_element_type=jnp.float32)
        rest[cols_in + col][...] = kernel
    rest[2 * cols_in][...] = own_ref[...]


def rows_kernel(parts, start, known, fresh, shard, vectors, *refs):
    rest = list(refs)
    rows = [joined([rest.pop(0) for _ in range(count)], shard, vectors) for count in parts]
    cols, kernels, known_cols = ([rest.pop(0) for _ in range(n)] for n in (fresh, known, known))
    left, squares = features_of(rows)
    total = jnp.zeros((vectors, len(parts) * shard), jnp.float32)
    for kernel, col in zip(kernels, known_cols):
        some = kernel[start * shard : (start + len(parts)) * shard, :]
        probes = col[pl.ds(shard, vectors), :]
        total += lax.dot_general(probes, some, ROWS_BY_ROWS, preferred_element_type=jnp.float32)
    for col in cols:
        kernel = kernel_of(left, squares, col[0:shard, :])
        probes = col[pl.ds(shard, vectors), :]
        total += lax.dot_general(probes, kernel, ROWS_BY_ROWS, preferred_element_type=jnp.float32)
    for place, ref in enumerate(rest):
        ref[...] = total[:, place * shard : (place + 1) * shard].astype(ref.dtype)


def call(body, args, outs, work):
    whole = pl.BlockSpec(memory_space=pltpu.VMEM)
    return pl.pallas_call(
        body,
        out_shape=outs,
        in_specs=[whole] * len(args),
        out_specs=[whole] * len(outs),
        compiler_params=pltpu.CompilerParams(vmem_limit_bytes=32 * 1024 * 1024),
        cost_estimate=pl.CostEstimate(flops=2 * work, bytes_accessed=0, transcendentals=0),
    )(*args)


def halve_kernel(shard, vectors, from_ref, *halves):
    points, some = shard // 2, vectors // 2
    for place, half in enumerate(halves):
        half[0:points, :] = from_ref[pl.ds(place * points, points), :]
        half[points:, :] = from_ref[pl.ds(shard + place * some, some), :]


def halve(value, shard, vectors):
    whole = pl.BlockSpec(memory_space=pltpu.VMEM)
    half = jax.ShapeDtypeStruct(((shard + vectors) // 2, value.shape[1]), value.dtype)
    return pl.pallas_call(
        functools.partial(halve_kernel, shard, vectors),
        out_shape=[half, half],
        in_specs=[whole],
        out_specs=[whole, whole],
        compiler_params=pltpu.CompilerParams(vmem_limit_bytes=32 * 1024 * 1024),
        cost_estimate=pl.CostEstimate(flops=0, bytes_accessed=0, transcendentals=0),
    )(value)


def on_device(features, probes, noise_level):
    count = lax.axis_size("blk")
    inner = group_size(count)
    outer = count // inner
    shard = features.shape[0]
    vectors = probes.shape[1]
    packed = jnp.concatenate([features, probes.T], axis=0)

    def along_outer(value, edges):
        return lax.ppermute(value, "blk", [(s * inner + b, t * inner + b) for s, t in edges for b in range(inner)])

    def in_plane(value, hops):
        return lax.ppermute(value, "blk", [(a * inner + s, a * inner + t) for a in range(outer) for s, t in hops])

    def near(step):
        return [(plane_target(b, step, inner), b) for b in range(inner)]

    one_way, exchanges = outer_maps(outer)
    cols = [along_outer(packed, edges) for edges in one_way]
    others = [along_outer(packed, edges) for edges in exchanges]
    blocks = plane_blocks(packed, inner, in_plane, lambda block: halve(block, shard, vectors))
    direct = [step for step in range(1, inner) if step & (step - 1) == 0]
    passed = [step for step in range(1, inner) if step & (step - 1)]

    order = [0] + passed + [inner + place for place in range(len(cols))] + direct
    parts = tuple(map(len, blocks))
    operands = [*blocks, *[(col,) for col in cols]]
    flat = jax.ShapeDtypeStruct((vectors, shard), jnp.float32)
    sent = jax.ShapeDtypeStruct((vectors, shard), jnp.bfloat16)
    matrix = jax.ShapeDtypeStruct((inner * shard, shard), jnp.bfloat16)
    early = sorted({0, inner // 2})
    pairs = [(row, 0, ("back",)) for row in range(len(early))]
    started = tile(
        [blocks[row] for row in early],
        [packed],
        range(len(early) + 1),
        pairs,
        {},
        shard,
        vectors,
        noise=[noise_level[None, :]],
        work=0.0,
    )
    found = call(
        functools.partial(cycle_kernel, order, parts, len(cols), shard, vectors),
        [started["back", 0], *[part for place in order for part in operands[place]]],
        [flat] * len(cols) + [matrix] * len(cols) + [flat],
        0,
    )
    backs, kernels, started = found[: len(cols)], found[len(cols) : -1], found[-1]
    half = inner // 2
    sums = {}
    for start, stop in ((half, inner), (0, half)):
        some = blocks[start:stop]
        found = call(
            functools.partial(rows_kernel, parts[start:stop], start, len(cols), len(others), shard, vectors),
            [*[part for block in some for part in block], *others, *kernels, *cols],
            [sent if row else flat for row in range(start, stop)],
            len(some) * len(others) * shard * shard * features.shape[1],
        )
        sums.update({("rows", start + place): value for place, value in enumerate(found)})
    later = [row for row in range(inner) if row not in early]
    pairs = [(row, 0, ("back",)) for row in range(len(later))]
    known = {("back", 0): started}
    own = tile([blocks[row] for row in later], [packed], range(len(later) + 1), pairs, known, shard, vectors)

    total = [sums["rows", 0], own["back", 0]]
    total += [in_plane(sums["rows", step], [(t, s) for s, t in near(step)]) for step in range(1, inner)]
    total += [along_outer(back, [(t, s) for s, t in edges]) for back, edges in zip(backs, one_way)]
    return functools.reduce(lambda sofar, term: sofar + term, total).T


def solution(mesh):
    placed = (P(("parts", "blk"), None), P(("parts", "blk"), None), P(("parts", "blk")))
    return jax.shard_map(
        on_device, mesh=mesh, in_specs=placed, out_specs=P(("parts", "blk"), None), check_vma=False
    )
```

```python
import functools
import math

import jax
import jax.numpy as jnp
from jax import lax
from jax.experimental import pallas as pl
from jax.experimental.pallas import tpu as pltpu
from jax.sharding import PartitionSpec as P

ROOT5 = math.sqrt(5.0)
DECAY = -ROOT5 * math.log2(math.e)
ROWS_BY_ROWS = (((1,), (1,)), ((), ()))


def group_size(count):
    size = 1
    while size * size < count or count % size:
        size += 1
    return size


def plane_blocks(value, count, send, cut):
    if count & (count - 1):
        maps = {step: [(b, (b - step) % count) for b in range(count)] for step in range(1, count)}
        return [(value,)] + [(send(value, maps[step]),) for step in range(1, count)]
    blocks = {0: (value,)}
    bit = count // 2
    while bit:
        hops = [(b, b ^ bit) for b in range(count)]
        for known in list(blocks):
            parts = blocks[known] if known == 0 or len(blocks[known]) > 1 else cut(*blocks[known])
            blocks[known | bit] = tuple(send(part, hops) for part in parts)
        bit //= 2
    return [blocks[distance] for distance in range(count)]


def plane_target(index, step, count):
    return (index + step) % count if count & (count - 1) else index ^ step


def outer_maps(count):
    bits = count.bit_length() - 1
    order = list(range(count))
    if count == 1 << bits:
        order = [int(f"{a:0{bits}b}"[::-1], 2) if bits else a for a in reversed(order)]
    shifts = [[(order[p], order[(p + step) % count]) for p in range(count)] for step in range(1, count // 2 + 1)]
    if count % 2:
        return shifts, []
    return shifts[:-1], shifts[-1:]


def matern(dist2):
    dist2 = jnp.maximum(dist2, 1e-30)
    dist = dist2 * lax.rsqrt(dist2)
    poly = (1.0 + ROOT5 * dist) + (5.0 / 3.0) * dist2
    return (poly * jnp.exp2(DECAY * dist)).astype(jnp.bfloat16)


def lane_squares(block):
    wide = block.astype(jnp.float32)
    sums = jnp.sum(wide * wide, axis=1, keepdims=True)
    return jnp.transpose(jnp.broadcast_to(sums, (block.shape[0], 128)))[0:1, :]


def joined(refs, shard, vectors):
    points, some = shard // len(refs), vectors // len(refs)
    features = [ref[0:points, :] for ref in refs]
    probes = [ref[pl.ds(points, some), :] for ref in refs]
    return (jnp.concatenate(features), jnp.concatenate(probes)) if len(refs) > 1 else (features[0], probes[0])


def tile_kernel(order, pairs, known, counts, shard, vectors, *refs):
    parts, cols_in, noise_in = counts
    rest = list(refs)
    blocks = {place: [rest.pop(0) for _ in range((*parts, *[1] * cols_in)[place])] for place in order}
    rows = [joined(blocks[place], shard, vectors) for place in range(len(parts))]
    cols = [blocks[len(parts) + place][0] for place in range(cols_in)]
    noise = [rest.pop(0) for _ in range(noise_in)]
    sums = {name: rest.pop(0)[...] for name in known}
    squares = {}
    for col in sorted({col for _, col, _ in pairs}):
        kind = next(kind for _, place, kind in pairs if place == col)
        members = [row for row, place, _ in pairs if place == col]
        for row in members:
            if row not in squares:
                wide = rows[row][0].astype(jnp.float32)
                squares[row] = jnp.sum(wide * wide, axis=1, keepdims=True)
        block = cols[col][0:shard, :]
        scaled, col_squares = block * jnp.asarray(-2.0, block.dtype), lane_squares(block)
        left = jnp.concatenate([rows[row][0] for row in members])
        cross = lax.dot_general(left, scaled, ROWS_BY_ROWS, preferred_element_type=jnp.float32)
        kernel = matern((jnp.concatenate([squares[row] for row in members]) + col_squares) + cross)
        found = {}
        if "back" in kind:
            probes = jnp.concatenate([rows[row][1] for row in members], axis=1)
            found["back", col] = jnp.dot(probes, kernel, preferred_element_type=jnp.float32)
        if "rows" in kind:
            col_probes = cols[col][pl.ds(shard, vectors), :]
            terms = lax.dot_general(col_probes, kernel, ROWS_BY_ROWS, preferred_element_type=jnp.float32)
            for place, row in enumerate(members):
                found["rows", row] = terms[:, place * shard : (place + 1) * shard]
        for name, value in found.items():
            sums[name] = sums[name] + value if name in sums else value
    for place in range(noise_in):
        probes = cols[place][pl.ds(shard, vectors), :].astype(jnp.float32)
        sums["back", place] = sums["back", place] + noise[place][...] * probes
    for ref, name in zip(rest, sorted(sums)):
        ref[...] = sums[name].astype(ref.dtype)


def tile(rows, cols, order, pairs, sums, shard, vectors, noise=(), work=1.0, sent=()):
    blocks = [*rows, *[(col,) for col in cols]]
    args = [*[part for place in order for part in blocks[place]], *noise, *sums.values()]
    elements = len(pairs) * shard * shard
    width = cols[0].shape[1]
    names = sorted({(part, col if part == "back" else row) for row, col, kind in pairs for part in kind} | set(sums))
    whole = pl.BlockSpec(memory_space=pltpu.VMEM)
    found = pl.pallas_call(
        functools.partial(
            tile_kernel, list(order), tuple(pairs), tuple(sums), (tuple(map(len, rows)), len(cols), len(noise)), shard, vectors
        ),
        out_shape=[
            jax.ShapeDtypeStruct((vectors, shard), jnp.bfloat16 if name in sent else jnp.float32) for name in names
        ],
        in_specs=[whole] * len(args),
        out_specs=[whole] * len(names),
        compiler_params=pltpu.CompilerParams(vmem_limit_bytes=32 * 1024 * 1024),
        cost_estimate=pl.CostEstimate(
            flops=int(work * 2 * elements * (width + 2 * vectors)),
            bytes_accessed=int(work * 2 * width * shard * len(blocks)),
            transcendentals=int(work * 2 * elements),
        ),
    )(*args)
    return dict(zip(names, found))


def features_of(rows):
    left = jnp.concatenate([row[0] for row in rows])
    wide = left.astype(jnp.float32)
    return left, jnp.sum(wide * wide, axis=1, keepdims=True)


def lane_squares_by_products(block):
    wide = block.astype(jnp.float32)
    square = wide * wide
    high = square.astype(jnp.bfloat16)
    low = (square - high.astype(jnp.float32)).astype(jnp.bfloat16)
    ones = jnp.ones((8, block.shape[1]), jnp.bfloat16)
    total = lax.dot_general(ones, high, ROWS_BY_ROWS, preferred_element_type=jnp.float32)
    total += lax.dot_general(ones, low, ROWS_BY_ROWS, preferred_element_type=jnp.float32)
    return total[0:1, :]


def kernel_of(left, squares, col, lanes=lane_squares):
    scaled = col * jnp.asarray(-2.0, col.dtype)
    cross = lax.dot_general(left, scaled, ROWS_BY_ROWS, preferred_element_type=jnp.float32)
    return matern((squares + lanes(col)) + cross)


def cycle_kernel(order, parts, cols_in, shard, vectors, *refs):
    rest = list(refs)
    blocks = {place: [rest.pop(0) for _ in range((*parts, *[1] * cols_in)[place])] for place in order}
    rows = [joined(blocks[place], shard, vectors) for place in range(len(parts))]
    left, squares = features_of(rows)
    probes = jnp.concatenate([row[1] for row in rows], axis=1)
    for col in range(cols_in):
        kernel = kernel_of(left, squares, blocks[len(parts) + col][0][0:shard, :], lane_squares_by_products)
        rest[col][...] = jnp.dot(probes, kernel, preferred_element_type=jnp.float32)
        rest[cols_in + col][...] = kernel


def rows_kernel(parts, start, known, fresh, shard, vectors, *refs):
    rest = list(refs)
    rows = [joined([rest.pop(0) for _ in range(count)], shard, vectors) for count in parts]
    cols, kernels, known_cols = ([rest.pop(0) for _ in range(n)] for n in (fresh, known, known))
    left, squares = features_of(rows)
    total = jnp.zeros((vectors, len(parts) * shard), jnp.float32)
    for kernel, col in zip(kernels, known_cols):
        some = kernel[start * shard : (start + len(parts)) * shard, :]
        probes = col[pl.ds(shard, vectors), :]
        total += lax.dot_general(probes, some, ROWS_BY_ROWS, preferred_element_type=jnp.float32)
    for col in cols:
        kernel = kernel_of(left, squares, col[0:shard, :])
        probes = col[pl.ds(shard, vectors), :]
        total += lax.dot_general(probes, kernel, ROWS_BY_ROWS, preferred_element_type=jnp.float32)
    for place, ref in enumerate(rest):
        ref[...] = total[:, place * shard : (place + 1) * shard].astype(ref.dtype)


def call(body, args, outs, work):
    whole = pl.BlockSpec(memory_space=pltpu.VMEM)
    return pl.pallas_call(
        body,
        out_shape=outs,
        in_specs=[whole] * len(args),
        out_specs=[whole] * len(outs),
        compiler_params=pltpu.CompilerParams(vmem_limit_bytes=32 * 1024 * 1024),
        cost_estimate=pl.CostEstimate(flops=2 * work, bytes_accessed=0, transcendentals=0),
    )(*args)


def halve_kernel(shard, vectors, from_ref, *halves):
    points, some = shard // 2, vectors // 2
    for place, half in enumerate(halves):
        half[0:points, :] = from_ref[pl.ds(place * points, points), :]
        half[points:, :] = from_ref[pl.ds(shard + place * some, some), :]


def halve(value, shard, vectors):
    whole = pl.BlockSpec(memory_space=pltpu.VMEM)
    half = jax.ShapeDtypeStruct(((shard + vectors) // 2, value.shape[1]), value.dtype)
    return pl.pallas_call(
        functools.partial(halve_kernel, shard, vectors),
        out_shape=[half, half],
        in_specs=[whole],
        out_specs=[whole, whole],
        compiler_params=pltpu.CompilerParams(vmem_limit_bytes=32 * 1024 * 1024),
        cost_estimate=pl.CostEstimate(flops=0, bytes_accessed=0, transcendentals=0),
    )(value)


def on_device(features, probes, noise_level):
    count = lax.axis_size("blk")
    inner = group_size(count)
    outer = count // inner
    shard = features.shape[0]
    vectors = probes.shape[1]
    packed = jnp.concatenate([features, probes.T], axis=0)

    def along_outer(value, edges):
        return lax.ppermute(value, "blk", [(s * inner + b, t * inner + b) for s, t in edges for b in range(inner)])

    def in_plane(value, hops):
        return lax.ppermute(value, "blk", [(a * inner + s, a * inner + t) for a in range(outer) for s, t in hops])

    def near(step):
        return [(plane_target(b, step, inner), b) for b in range(inner)]

    one_way, exchanges = outer_maps(outer)
    cols = [along_outer(packed, edges) for edges in one_way]
    others = [along_outer(packed, edges) for edges in exchanges]
    blocks = plane_blocks(packed, inner, in_plane, lambda block: halve(block, shard, vectors))
    direct = [step for step in range(1, inner) if step & (step - 1) == 0]
    passed = [step for step in range(1, inner) if step & (step - 1)]

    order = [0] + passed + [inner + place for place in range(len(cols))] + direct
    parts = tuple(map(len, blocks))
    operands = [*blocks, *[(col,) for col in cols]]
    flat = jax.ShapeDtypeStruct((vectors, shard), jnp.float32)
    sent = jax.ShapeDtypeStruct((vectors, shard), jnp.bfloat16)
    matrix = jax.ShapeDtypeStruct((inner * shard, shard), jnp.bfloat16)
    found = call(
        functools.partial(cycle_kernel, order, parts, len(cols), shard, vectors),
        [part for place in order for part in operands[place]],
        [flat] * len(cols) + [matrix] * len(cols),
        0,
    )
    backs, kernels = found[: len(cols)], found[len(cols) :]
    half = inner // 2
    sums = {}
    for start, stop in ((half, inner), (0, half)):
        some = blocks[start:stop]
        found = call(
            functools.partial(rows_kernel, parts[start:stop], start, len(cols), len(others), shard, vectors),
            [*[part for block in some for part in block], *others, *kernels, *cols],
            [sent if row else flat for row in range(start, stop)],
            len(some) * len(others) * shard * shard * features.shape[1],
        )
        sums.update({("rows", start + place): value for place, value in enumerate(found)})
    pairs = [(row, 0, ("back",)) for row in range(inner)]
    own = tile(blocks, [packed], range(inner + 1), pairs, {}, shard, vectors, noise=[noise_level[None, :]])

    total = [sums["rows", 0], own["back", 0]]
    total += [in_plane(sums["rows", step], [(t, s) for s, t in near(step)]) for step in range(1, inner)]
    total += [along_outer(back, [(t, s) for s, t in edges]) for back, edges in zip(backs, one_way)]
    return functools.reduce(lambda sofar, term: sofar + term, total).T


def solution(mesh):
    placed = (P(("parts", "blk"), None), P(("parts", "blk"), None), P(("parts", "blk")))
    return jax.shard_map(
        on_device, mesh=mesh, in_specs=placed, out_specs=P(("parts", "blk"), None), check_vma=False
    )
```

```python
import functools
import math

import jax
import jax.numpy as jnp
from jax import lax
from jax.experimental import pallas as pl
from jax.experimental.pallas import tpu as pltpu
from jax.sharding import PartitionSpec as P

ROOT5 = math.sqrt(5.0)
DECAY = -ROOT5 * math.log2(math.e)
ROWS_BY_ROWS = (((1,), (1,)), ((), ()))


def group_size(count):
    size = 1
    while size * size < count or count % size:
        size += 1
    return size


def plane_blocks(value, count, send, cut):
    if count & (count - 1):
        maps = {step: [(b, (b - step) % count) for b in range(count)] for step in range(1, count)}
        return [(value,)] + [(send(value, maps[step]),) for step in range(1, count)]
    blocks = {0: (value,)}
    bit = count // 2
    while bit:
        hops = [(b, b ^ bit) for b in range(count)]
        for known in list(blocks):
            parts = blocks[known] if known == 0 or len(blocks[known]) > 1 else cut(*blocks[known])
            blocks[known | bit] = tuple(send(part, hops) for part in parts)
        bit //= 2
    return [blocks[distance] for distance in range(count)]


def plane_target(index, step, count):
    return (index + step) % count if count & (count - 1) else index ^ step


def outer_maps(count):
    bits = count.bit_length() - 1
    order = list(range(count))
    if count == 1 << bits:
        order = [int(f"{a:0{bits}b}"[::-1], 2) if bits else a for a in reversed(order)]
    shifts = [[(order[p], order[(p + step) % count]) for p in range(count)] for step in range(1, count // 2 + 1)]
    if count % 2:
        return shifts, []
    return shifts[:-1], shifts[-1:]


def matern(dist2):
    dist2 = jnp.maximum(dist2, 1e-30)
    dist = dist2 * lax.rsqrt(dist2)
    poly = (1.0 + ROOT5 * dist) + (5.0 / 3.0) * dist2
    return (poly * jnp.exp2(DECAY * dist)).astype(jnp.bfloat16)


def lane_squares(block):
    wide = block.astype(jnp.float32)
    sums = jnp.sum(wide * wide, axis=1, keepdims=True)
    return jnp.transpose(jnp.broadcast_to(sums, (block.shape[0], 128)))[0:1, :]


def joined(refs, shard, vectors):
    points, some = shard // len(refs), vectors // len(refs)
    features = [ref[0:points, :] for ref in refs]
    probes = [ref[pl.ds(points, some), :] for ref in refs]
    return (jnp.concatenate(features), jnp.concatenate(probes)) if len(refs) > 1 else (features[0], probes[0])


def tile_kernel(order, pairs, known, counts, shard, vectors, *refs):
    parts, cols_in, noise_in = counts
    rest = list(refs)
    blocks = {place: [rest.pop(0) for _ in range((*parts, *[1] * cols_in)[place])] for place in order}
    rows = [joined(blocks[place], shard, vectors) for place in range(len(parts))]
    cols = [blocks[len(parts) + place][0] for place in range(cols_in)]
    noise = [rest.pop(0) for _ in range(noise_in)]
    sums = {name: rest.pop(0)[...] for name in known}
    squares = {}
    for col in sorted({col for _, col, _ in pairs}):
        kind = next(kind for _, place, kind in pairs if place == col)
        members = [row for row, place, _ in pairs if place == col]
        for row in members:
            if row not in squares:
                wide = rows[row][0].astype(jnp.float32)
                squares[row] = jnp.sum(wide * wide, axis=1, keepdims=True)
        block = cols[col][0:shard, :]
        scaled, col_squares = block * jnp.asarray(-2.0, block.dtype), lane_squares(block)
        left = jnp.concatenate([rows[row][0] for row in members])
        cross = lax.dot_general(left, scaled, ROWS_BY_ROWS, preferred_element_type=jnp.float32)
        kernel = matern((jnp.concatenate([squares[row] for row in members]) + col_squares) + cross)
        found = {}
        if "back" in kind:
            probes = jnp.concatenate([rows[row][1] for row in members], axis=1)
            found["back", col] = jnp.dot(probes, kernel, preferred_element_type=jnp.float32)
        if "rows" in kind:
            col_probes = cols[col][pl.ds(shard, vectors), :]
            terms = lax.dot_general(col_probes, kernel, ROWS_BY_ROWS, preferred_element_type=jnp.float32)
            for place, row in enumerate(members):
                found["rows", row] = terms[:, place * shard : (place + 1) * shard]
        for name, value in found.items():
            sums[name] = sums[name] + value if name in sums else value
    for place in range(noise_in):
        probes = cols[place][pl.ds(shard, vectors), :].astype(jnp.float32)
        sums["back", place] = sums["back", place] + noise[place][...] * probes
    for ref, name in zip(rest, sorted(sums)):
        ref[...] = sums[name].astype(ref.dtype)


def tile(rows, cols, order, pairs, sums, shard, vectors, noise=(), work=1.0, sent=()):
    blocks = [*rows, *[(col,) for col in cols]]
    args = [*[part for place in order for part in blocks[place]], *noise, *sums.values()]
    elements = len(pairs) * shard * shard
    width = cols[0].shape[1]
    names = sorted({(part, col if part == "back" else row) for row, col, kind in pairs for part in kind} | set(sums))
    whole = pl.BlockSpec(memory_space=pltpu.VMEM)
    found = pl.pallas_call(
        functools.partial(
            tile_kernel, list(order), tuple(pairs), tuple(sums), (tuple(map(len, rows)), len(cols), len(noise)), shard, vectors
        ),
        out_shape=[
            jax.ShapeDtypeStruct((vectors, shard), jnp.bfloat16 if name in sent else jnp.float32) for name in names
        ],
        in_specs=[whole] * len(args),
        out_specs=[whole] * len(names),
        compiler_params=pltpu.CompilerParams(vmem_limit_bytes=32 * 1024 * 1024),
        cost_estimate=pl.CostEstimate(
            flops=int(work * 2 * elements * (width + 2 * vectors)),
            bytes_accessed=int(work * 2 * width * shard * len(blocks)),
            transcendentals=int(work * 2 * elements),
        ),
    )(*args)
    return dict(zip(names, found))


def features_of(rows):
    left = jnp.concatenate([row[0] for row in rows])
    wide = left.astype(jnp.float32)
    return left, jnp.sum(wide * wide, axis=1, keepdims=True)


def kernel_of(left, squares, col):
    scaled = col * jnp.asarray(-2.0, col.dtype)
    cross = lax.dot_general(left, scaled, ROWS_BY_ROWS, preferred_element_type=jnp.float32)
    return matern((squares + lane_squares(col)) + cross)


def cycle_kernel(order, parts, cols_in, shard, vectors, noise_ref, *refs):
    rest = list(refs)
    blocks = {place: [rest.pop(0) for _ in range((*parts, *[1] * cols_in)[place])] for place in order}
    rows = [joined(blocks[place], shard, vectors) for place in range(len(parts))]
    left, squares = features_of(rows)
    probes = jnp.concatenate([row[1] for row in rows], axis=1)
    for col in range(cols_in):
        kernel = kernel_of(left, squares, blocks[len(parts) + col][0][0:shard, :])
        rest[col][...] = jnp.dot(probes, kernel, preferred_element_type=jnp.float32)
        rest[cols_in + col][...] = kernel
    rest[2 * cols_in][...] = noise_ref[...] * rows[0][1].astype(jnp.float32)


def rows_kernel(parts, start, known, fresh, shard, vectors, *refs):
    rest = list(refs)
    rows = [joined([rest.pop(0) for _ in range(count)], shard, vectors) for count in parts]
    cols, kernels, known_cols = ([rest.pop(0) for _ in range(n)] for n in (fresh, known, known))
    left, squares = features_of(rows)
    total = jnp.zeros((vectors, len(parts) * shard), jnp.float32)
    for kernel, col in zip(kernels, known_cols):
        some = kernel[start * shard : (start + len(parts)) * shard, :]
        probes = col[pl.ds(shard, vectors), :]
        total += lax.dot_general(probes, some, ROWS_BY_ROWS, preferred_element_type=jnp.float32)
    for col in cols:
        kernel = kernel_of(left, squares, col[0:shard, :])
        probes = col[pl.ds(shard, vectors), :]
        total += lax.dot_general(probes, kernel, ROWS_BY_ROWS, preferred_element_type=jnp.float32)
    for place, ref in enumerate(rest):
        ref[...] = total[:, place * shard : (place + 1) * shard].astype(ref.dtype)


def call(body, args, outs, work):
    whole = pl.BlockSpec(memory_space=pltpu.VMEM)
    return pl.pallas_call(
        body,
        out_shape=outs,
        in_specs=[whole] * len(args),
        out_specs=[whole] * len(outs),
        compiler_params=pltpu.CompilerParams(vmem_limit_bytes=32 * 1024 * 1024),
        cost_estimate=pl.CostEstimate(flops=2 * work, bytes_accessed=0, transcendentals=0),
    )(*args)


def halve_kernel(shard, vectors, from_ref, *halves):
    points, some = shard // 2, vectors // 2
    for place, half in enumerate(halves):
        half[0:points, :] = from_ref[pl.ds(place * points, points), :]
        half[points:, :] = from_ref[pl.ds(shard + place * some, some), :]


def halve(value, shard, vectors):
    whole = pl.BlockSpec(memory_space=pltpu.VMEM)
    half = jax.ShapeDtypeStruct(((shard + vectors) // 2, value.shape[1]), value.dtype)
    return pl.pallas_call(
        functools.partial(halve_kernel, shard, vectors),
        out_shape=[half, half],
        in_specs=[whole],
        out_specs=[whole, whole],
        compiler_params=pltpu.CompilerParams(vmem_limit_bytes=32 * 1024 * 1024),
        cost_estimate=pl.CostEstimate(flops=0, bytes_accessed=0, transcendentals=0),
    )(value)


def on_device(features, probes, noise_level):
    count = lax.axis_size("blk")
    inner = group_size(count)
    outer = count // inner
    shard = features.shape[0]
    vectors = probes.shape[1]
    packed = jnp.concatenate([features, probes.T], axis=0)

    def along_outer(value, edges):
        return lax.ppermute(value, "blk", [(s * inner + b, t * inner + b) for s, t in edges for b in range(inner)])

    def in_plane(value, hops):
        return lax.ppermute(value, "blk", [(a * inner + s, a * inner + t) for a in range(outer) for s, t in hops])

    def near(step):
        return [(plane_target(b, step, inner), b) for b in range(inner)]

    one_way, exchanges = outer_maps(outer)
    cols = [along_outer(packed, edges) for edges in one_way]
    others = [along_outer(packed, edges) for edges in exchanges]
    blocks = plane_blocks(packed, inner, in_plane, lambda block: halve(block, shard, vectors))
    direct = [step for step in range(1, inner) if step & (step - 1) == 0]
    passed = [step for step in range(1, inner) if step & (step - 1)]

    order = [0] + passed + [inner + place for place in range(len(cols))] + direct
    parts = tuple(map(len, blocks))
    operands = [*blocks, *[(col,) for col in cols]]
    flat = jax.ShapeDtypeStruct((vectors, shard), jnp.float32)
    sent = jax.ShapeDtypeStruct((vectors, shard), jnp.bfloat16)
    matrix = jax.ShapeDtypeStruct((inner * shard, shard), jnp.bfloat16)
    found = call(
        functools.partial(cycle_kernel, order, parts, len(cols), shard, vectors),
        [noise_level[None, :], *[part for place in order for part in operands[place]]],
        [flat] * len(cols) + [matrix] * len(cols) + [flat],
        0,
    )
    backs, kernels, noise = found[: len(cols)], found[len(cols) : -1], found[-1]
    half = inner // 2
    sums = {}
    for start, stop in ((half, inner), (0, half)):
        some = blocks[start:stop]
        found = call(
            functools.partial(rows_kernel, parts[start:stop], start, len(cols), len(others), shard, vectors),
            [*[part for block in some for part in block], *others, *kernels, *cols],
            [sent if row else flat for row in range(start, stop)],
            len(some) * len(others) * shard * shard * features.shape[1],
        )
        sums.update({("rows", start + place): value for place, value in enumerate(found)})
    pairs = [(row, 0, ("back",)) for row in range(inner)]
    own = tile(blocks, [packed], range(inner + 1), pairs, {("back", 0): noise}, shard, vectors)

    total = [sums["rows", 0], own["back", 0]]
    total += [in_plane(sums["rows", step], [(t, s) for s, t in near(step)]) for step in range(1, inner)]
    total += [along_outer(back, [(t, s) for s, t in edges]) for back, edges in zip(backs, one_way)]
    return functools.reduce(lambda sofar, term: sofar + term, total).T


def solution(mesh):
    placed = (P(("parts", "blk"), None), P(("parts", "blk"), None), P(("parts", "blk")))
    return jax.shard_map(
        on_device, mesh=mesh, in_specs=placed, out_specs=P(("parts", "blk"), None), check_vma=False
    )
```
